32 devices in a mesh: ep: 8 (over z, y), dp: 4 (over x, core).
Axes of the slice: x: 2, y: 2, z: 4, core: 2. Of those that a mesh axis runs over, the one named last changes fastest.
Arguments:
- layer_input: bfloat16 [4096, 2048], P(('ep', 'dp')), may hold values from -6 to 6
- grad_out: bfloat16 [4096, 2048], P(('ep', 'dp')), may hold values from -6 to 6
- attn_gain: bfloat16 [2048], P(('ep', 'dp')), may hold values from 0.5 to 1.5
- w_q: bfloat16 [2048, 2048], P(('ep', 'dp')), may hold values from -0.125 to 0.125
- w_k: bfloat16 [2048, 2048], P(('ep', 'dp')), may hold values from -0.125 to 0.125
- w_v: bfloat16 [2048, 2048], P(('ep', 'dp')), may hold values from -0.125 to 0.125
- q_gain: bfloat16 [2048], P(('ep', 'dp')), may hold values from 0.5 to 1.5
- k_gain: bfloat16 [2048], P(('ep', 'dp')), may hold values from 0.5 to 1.5
- w_o: bfloat16 [2048, 2048], P(('ep', 'dp')), may hold values from -0.5 to 0.5
- ffn_gain: bfloat16 [2048], P(('ep', 'dp')), may hold values from 0.5 to 1.5
- router: bfloat16 [2048, 64], P(('ep', 'dp')), may hold values from -0.0625 to 0.0625
- w_gate: bfloat16 [64, 2048, 1024], P('ep', None, 'dp'), may hold values from -0.125 to 0.125
- w_up: bfloat16 [64, 2048, 1024], P('ep', None, 'dp'), may hold values from -0.125 to 0.125
- w_down: bfloat16 [64, 1024, 2048], P('ep', 'dp'), may hold values from -0.75 to 0.75
- routes: int32 [4096, 8], P(('ep', 'dp')), may hold values from 0 to 63, all different within a row; in each aligned block of 128 rows (0 to 127, 128 to 255, ...) at most 32 rows name the same one
Outputs:
- output: bfloat16 [4096, 2048], P(('ep', 'dp'))
- grad_input: float32 [4096, 2048], P(('ep', 'dp'))
- grad_attn_gain: float32 [2048], P(('ep', 'dp'))
- grad_w_q: float32 [2048, 2048], P(('ep', 'dp'))
- grad_w_k: float32 [2048, 2048], P(('ep', 'dp'))
- grad_w_v: float32 [2048, 2048], P(('ep', 'dp'))
- grad_q_gain: float32 [2048], P(('ep', 'dp'))
- grad_k_gain: float32 [2048], P(('ep', 'dp'))
- grad_w_o: float32 [2048, 2048], P(('ep', 'dp'))
- grad_ffn_gain: float32 [2048], P(('ep', 'dp'))
- grad_router: float32 [2048, 64], P(('ep', 'dp'))
- grad_w_gate: float32 [64, 2048, 1024], P('ep', None, 'dp')
- grad_w_up: float32 [64, 2048, 1024], P('ep', None, 'dp')
- grad_w_down: float32 [64, 1024, 2048], P('ep', 'dp')
The draws below stay inside these ranges and needn't reach their ends.
Inputs may be any that keep to these rules, and one draw needn't show every extreme that they name: `routes`: each row names 8 different experts; in each aligned block of 128 rows (the rows of one device) no expert is named by more than 32 rows.
All inputs are finite; a program needn't handle non-finite values.
Results may differ from the reference program's by a relative error of at most 0.02.
Values may be sent and summed in bfloat16 or wider, within the bound.
A program may use at most 448 MiB of HBM per device.

```python
import math
import jax
import jax.numpy as jnp
import numpy as np
from jax import lax

D = 2048
HEADS = 16
HEAD_DIM = 128
FF = 1024
EXPERTS = 64
TOP = 8
TOK_DEV = 128
CAP = 32
TOKENS = 4096
N_DP = 4


def level_of(own_key, dims, cuts, smallest, high):
    factor_of, own = 1.0, jax.random.fold_in(own_key, 6)
    for position, shards_of in cuts:
        steps = jnp.exp(jax.random.uniform(jax.random.fold_in(own, position), (shards_of,), jnp.float32, smallest / len(cuts), high / len(cuts)))
        factor_of = factor_of * jnp.repeat(steps, dims[position] // shards_of).reshape([-1 if axis == position else 1 for axis in range(len(dims))])
    return factor_of


def assign_block(key, own, number, rows, number_of, top, limit, slope):
    ranking = jax.random.permutation(key, number_of)
    crowded, ordinary = load_shares(number_of, rows * top, limit, slope, True), load_shares(number_of, rows * top, limit, slope, False)
    places = jnp.arange(number_of)

    def named(lengths, rotation):
        used = int((lengths > 0).sum())
        fixed = max(1, used // 4)
        shifted = fixed + (places - fixed + rotation * (used - fixed)) % max(1, number_of - fixed)
        return jnp.zeros((number_of,), jnp.int32).at[ranking[jnp.where(places < fixed, places, shifted)]].set(jnp.asarray(lengths, jnp.int32))

    lengths = jnp.where(number % 4 == 0, named(crowded, number // 4), named(ordinary, number - number // 4 - 1))
    mixed = jax.random.permutation(jax.random.fold_in(own, 3), number_of)
    donor, taker = mixed[0:number_of // 2 * 2:2], mixed[1:number_of // 2 * 2:2]
    slack = jnp.minimum(lengths[donor] - 1, limit - lengths[taker]) // 2
    slack = jnp.where((donor == ranking[0]) | (taker == ranking[0]) | (lengths[taker] == 0), 0, jnp.maximum(slack, 0))
    shifted = jax.random.randint(jax.random.fold_in(own, 4), (number_of // 2,), 0, 1 << 20) % (slack + 1)
    lengths = lengths.at[donor].add(-shifted).at[taker].add(shifted)
    members = jnp.searchsorted(jnp.cumsum(lengths), jnp.arange(rows * top), side="right").astype(jnp.int32)
    grid = members.reshape(top, rows).T
    grid = grid[jax.random.permutation(jax.random.fold_in(own, 1), rows)]
    rotation = jax.random.randint(jax.random.fold_in(own, 2), (rows, 1), 0, top)
    return jnp.take_along_axis(grid, (jnp.arange(top)[None, :] + rotation) % top, axis=1)


def load_shares(amount, total, reach, skew, full):
    loads = [(1 << 20) // math.isqrt(rank ** skew) + 1 for rank in range(1, amount + 1)]
    largest = reach if full else min(reach, max(-(-total // amount), total * loads[0] // sum(loads)))
    least = 1 if total - largest >= amount - 1 else 0
    holding, rest = [largest] + [least] * (amount - 1), total - largest - least * (amount - 1)
    while rest > 0:
        candidates = [i for i in range(1, amount) if holding[i] < largest] or [i for i in range(1, amount) if holding[i] < reach]
        whole, remaining = sum([loads[i] for i in candidates]), rest
        for i in candidates:
            more = min(reach - holding[i], max(1, remaining * loads[i] // whole), rest)
            holding[i] = holding[i] + more
            rest = rest - more
    return np.array(holding)


def noise(stream_key, shape, width, reach, shards=(), kind=jnp.bfloat16):
    values = width * jax.random.normal(stream_key, shape, jnp.float32)
    if shards:
        values = values * level_of(stream_key, shape, shards, -0.22, 0.18)
    return jnp.clip(values, -reach, reach).astype(kind)


def setup_inputs(seed: int = 0) -> dict:
    key_list = jax.random.split(jax.random.key(seed), 16)
    layer_input = noise(key_list[0], (TOKENS, D), 1.0, 6.0, ((0, 32),))
    grad_out = noise(key_list[1], (TOKENS, D), 1.0, 6.0, ((0, 32),))
    attn_gain = jnp.clip(1.0 + 0.1 * jax.random.normal(key_list[2], (D,), jnp.float32), 0.5, 1.5).astype(jnp.bfloat16)
    w_q = noise(key_list[3], (D, D), D ** -0.5, 0.125, ((0, 32),))
    w_k = noise(key_list[4], (D, D), D ** -0.5, 0.125, ((0, 32),))
    w_v = noise(key_list[5], (D, D), D ** -0.5, 0.125, ((0, 32),))
    q_gain = jnp.clip(1.0 + 0.1 * jax.random.normal(key_list[6], (D,), jnp.float32), 0.5, 1.5).astype(jnp.bfloat16)
    k_gain = jnp.clip(1.0 + 0.1 * jax.random.normal(key_list[7], (D,), jnp.float32), 0.5, 1.5).astype(jnp.bfloat16)
    w_o = noise(key_list[8], (D, D), (D // 16) ** -0.5, 0.5, ((0, 32),))
    ffn_gain = jnp.clip(1.0 + 0.1 * jax.random.normal(key_list[9], (D,), jnp.float32), 0.5, 1.5).astype(jnp.bfloat16)
    router = noise(key_list[10], (D, EXPERTS), (4 * D) ** -0.5, 0.0625, ((0, 32),))
    w_gate = noise(key_list[11], (EXPERTS, D, FF), D ** -0.5, 0.125, ((0, 8), (2, 4)))
    w_up = noise(key_list[12], (EXPERTS, D, FF), D ** -0.5, 0.125, ((0, 8), (2, 4)))
    w_down = noise(key_list[13], (EXPERTS, FF, D), (FF // 16) ** -0.5, 0.75, ((0, 8), (1, 4)))
    routes_keys = jax.random.split(jax.random.fold_in(key_list[14], 1), TOKENS // TOK_DEV)
    routes_turns = jax.random.permutation(jax.random.fold_in(key_list[14], 3), TOKENS // TOK_DEV)
    routes = jax.vmap(lambda own, number: assign_block(jax.random.fold_in(key_list[14], 2), own, number, TOK_DEV, EXPERTS, TOP, CAP, 1))(routes_keys, routes_turns).reshape((TOKENS, TOP))
    return dict(layer_input=layer_input, grad_out=grad_out, attn_gain=attn_gain, w_q=w_q, w_k=w_k, w_v=w_v, q_gain=q_gain, k_gain=k_gain, w_o=w_o, ffn_gain=ffn_gain, router=router, w_gate=w_gate, w_up=w_up, w_down=w_down, routes=routes)


EPSILON = 1e-05
HIGHEST = lax.Precision.HIGHEST

@jax.custom_vjp
def low(v):
    return lax.optimization_barrier(v.astype(jnp.bfloat16)).astype(jnp.float32)

@jax.custom_vjp
def low_back(v):
    return v

def low_keep(v):
    return (low(v), None)

def low_pass(kept, grad):
    return (grad,)

def back_keep(v):
    return (v, None)

def back_low(kept, grad):
    return (low(grad),)
low.defvjp(low_keep, low_pass)
low_back.defvjp(back_keep, back_low)

def matmul_high(left, right):
    return jnp.dot(left, right, precision=HIGHEST, preferred_element_type=jnp.float32)

def rms_scale(value, gain):
    return value * lax.rsqrt(lax.optimization_barrier(jnp.mean(value * value, axis=-1, keepdims=True)) + EPSILON) * gain

def rotate(value, positions):
    half_dim = value.shape[-1] // 2
    frequency = 10000.0 ** (-jnp.arange(half_dim, dtype=jnp.float32) * 2.0 / value.shape[-1])
    angle_table = positions.astype(jnp.float32)[:, None] * frequency[None, :]
    cosine = jnp.concatenate([jnp.cos(angle_table), jnp.cos(angle_table)], axis=-1)[:, None, :]
    sine_part = jnp.concatenate([jnp.sin(angle_table), jnp.sin(angle_table)], axis=-1)[:, None, :]
    first_half = value[..., :half_dim]
    second_half = value[..., half_dim:]
    turned = jnp.concatenate([-second_half, first_half], axis=-1)
    return value * cosine + turned * sine_part

def attend(seq_block):
    queries, key_rot, values = seq_block
    length = queries.shape[0]
    scores = jnp.einsum('qhd,khd->hqk', queries, key_rot, precision=HIGHEST) * queries.shape[-1] ** (-0.5)
    scores = low_back(scores)
    causal = jnp.arange(length)[:, None] >= jnp.arange(length)[None, :]
    scores = jnp.where(causal[None], scores, -1e+30)
    weights = low(jax.nn.softmax(scores, axis=-1))
    return jnp.einsum('hqk,khd->qhd', weights, values, precision=HIGHEST)

def forward(layer_input, attn_gain, w_q, w_k, w_v, q_gain, k_gain, w_o, ffn_gain, router, w_gate, w_up, w_down, routes):
    tokens = layer_input.shape[0]
    seq_len = TOK_DEV * N_DP
    seq_count = tokens // seq_len
    normed = low(rms_scale(layer_input, attn_gain))
    q_raw = low_back(matmul_high(normed, w_q))
    k_raw = low_back(matmul_high(normed, w_k))
    v_raw = low(low_back(matmul_high(normed, w_v)))
    positions = jnp.arange(seq_len, dtype=jnp.int32)
    seq_shape = (seq_count, seq_len, HEADS, HEAD_DIM)
    q_rot = low(rotate(rms_scale(q_raw, q_gain).reshape(seq_shape), positions))
    k_rot = low(rotate(rms_scale(k_raw, k_gain).reshape(seq_shape), positions))
    attended = lax.map(jax.checkpoint(attend), (q_rot, k_rot, v_raw.reshape(seq_shape)))
    mixed_low = low(low_back(attended.reshape(tokens, D)))
    residual = layer_input + low_back(matmul_high(mixed_low, w_o))
    normed2 = low(rms_scale(residual, ffn_gain))
    logits = low_back(matmul_high(normed2, router))
    picked_mask = routes[:, :, None] == jnp.arange(EXPERTS, dtype=jnp.int32)[None, None, :]
    chosen = lax.optimization_barrier(jnp.sum(jnp.where(picked_mask, logits[:, None, :], 0.0), axis=-1))
    gate_values = jax.nn.softmax(chosen, axis=-1)
    expert_hits = lax.optimization_barrier(jnp.sum(picked_mask.astype(jnp.int32), axis=1))
    blocks = expert_hits.reshape(tokens // TOK_DEV, TOK_DEV, EXPERTS)
    hits_before = (jnp.cumsum(blocks, axis=1) - blocks).reshape(tokens, EXPERTS)
    slot_index = lax.optimization_barrier(jnp.sum(jnp.where(picked_mask, hits_before[:, None, :], 0), axis=-1)).astype(jnp.int32)
    slot_place = ((jnp.arange(tokens, dtype=jnp.int32) // TOK_DEV)[:, None] * CAP + slot_index).astype(jnp.int32)
    slot_count = tokens // TOK_DEV * CAP
    token_ids = jnp.broadcast_to(jnp.arange(tokens, dtype=jnp.int32)[:, None], routes.shape).reshape(-1)
    flat_place = slot_place.reshape(-1)
    flat_routes = routes.reshape(-1)

    def expert_step(moe_total, expert_item):
        gate_weight, up_weight, down_weight, number = expert_item
        hit_mask = flat_routes == number
        slot_target = jnp.where(hit_mask, flat_place, slot_count).astype(jnp.int32)
        source = jnp.zeros((slot_count + 1,), jnp.int32).at[slot_target].set(token_ids)[:slot_count]
        filled = jnp.zeros((slot_count + 1,), normed2.dtype).at[slot_target].set(1.0)[:slot_count]
        expert_rows = low_back(jnp.take(normed2, source, axis=0) * filled[:, None])
        gate_part = low_back(matmul_high(expert_rows, gate_weight))
        up_part = low_back(matmul_high(expert_rows, up_weight))
        hidden = low(jax.nn.silu(gate_part) * up_part)
        output = low(low_back(matmul_high(hidden, down_weight)))
        weight = lax.optimization_barrier(jnp.sum(jnp.where(routes == number, gate_values, 0.0), axis=1))
        where_row = lax.optimization_barrier(jnp.sum(jnp.where(routes == number, slot_place, 0), axis=1)).astype(jnp.int32)
        return (moe_total + weight[:, None] * jnp.take(output, where_row, axis=0), None)
    expert_sum, _ = lax.scan(jax.checkpoint(expert_step), jnp.zeros_like(layer_input), (w_gate, w_up, w_down, jnp.arange(EXPERTS, dtype=jnp.int32)))
    return residual + expert_sum

def reference(layer_input, grad_out, attn_gain, w_q, w_k, w_v, q_gain, k_gain, w_o, ffn_gain, router, w_gate, w_up, w_down, routes):
    float_args = [value.astype(jnp.float32) for value in (layer_input, attn_gain, w_q, w_k, w_v, q_gain, k_gain, w_o, ffn_gain, router, w_gate, w_up, w_down)]

    def wrapped(*values):
        return forward(*values, routes)
    result, pullback = jax.vjp(wrapped, *float_args)
    gradients = pullback(grad_out.astype(jnp.float32))
    return (result.astype(jnp.bfloat16), gradients[0], gradients[1], gradients[2], gradients[3], gradients[4], gradients[5], gradients[6], gradients[7], gradients[8], gradients[9], gradients[10], gradients[11], gradients[12])
```

```python
import jax
import jax.numpy as jnp
from jax import lax
from jax.sharding import PartitionSpec as P

HEAD_DIM = 128
EPSILON = 1e-05
BF = jnp.bfloat16
F32 = jnp.float32
AXES = ("ep", "dp")


def dot(left, right):
    return jnp.dot(left, right, preferred_element_type=F32)


def ein(spec, left, right):
    return jnp.einsum(spec, left, right, preferred_element_type=F32)


def inv_rms(value):
    return lax.rsqrt(jnp.mean(value * value, axis=-1, keepdims=True) + EPSILON)


def half_turn(value):
    half = value.shape[-1] // 2
    return jnp.concatenate([-value[..., half:], value[..., :half]], axis=-1)


def half_turn_back(value):
    half = value.shape[-1] // 2
    return jnp.concatenate([value[..., half:], -value[..., :half]], axis=-1)


def build(n_ep, n_dp):
    n_dev = n_ep * n_dp
    group = 2 * n_dp
    n_group = n_dev // group
    rows_of = [[g * group + r for r in range(group)] for g in range(n_group)]
    cols_of = [[g * group + r for g in range(n_group)] for r in range(group)]

    def group_gather(value, axis=0):
        return lax.all_gather(value, AXES, axis=axis, tiled=True, axis_index_groups=rows_of)

    def group_scatter(value):
        return lax.psum_scatter(
            value, AXES, scatter_dimension=0, tiled=True, axis_index_groups=rows_of
        )

    def group_swap(value):
        return lax.all_to_all(value, AXES, 0, 0, tiled=True, axis_index_groups=rows_of)

    def column_gather(value):
        return lax.all_gather(value, AXES, axis=0, tiled=False, axis_index_groups=cols_of)

    def column_scatter(value):
        return lax.psum_scatter(
            value, AXES, scatter_dimension=0, tiled=False, axis_index_groups=cols_of
        )

    def shards(
        layer_input, grad_out, attn_gain, w_q, w_k, w_v, q_gain, k_gain, w_o, ffn_gain,
        router, w_gate, w_up, w_down, routes,
    ):
        rows, width = layer_input.shape
        cols = width // group
        heads = cols // HEAD_DIM
        seqs = 2
        seq_len = rows * n_dp
        scale = HEAD_DIM ** (-0.5)
        own = width // n_dev
        rank = (lax.axis_index("ep") % 2) * n_dp + lax.axis_index("dp")
        local_experts = w_gate.shape[0]
        experts = router.shape[1]
        top = routes.shape[1]
        cap = 2 * rows * top // experts

        qkv = jnp.stack([w_q, w_k, w_v]).reshape(3, own, group, cols).transpose(2, 0, 1, 3)
        qkv = group_swap(qkv)
        qkv = column_gather(qkv)
        qkv = qkv.transpose(2, 0, 1, 3, 4).reshape(3, width, cols)
        wq, wk, wv = qkv[0], qkv[1], qkv[2]
        wo = column_gather(w_o)
        halves = group // n_dp
        return_rank = [(halves * g) % group for g in range(n_group)]
        del return_rank
        full_o = lax.all_gather(w_o, AXES, axis=0, tiled=True)
        wo = lax.dynamic_slice_in_dim(full_o, rank * cols, cols, 0)

        small = jnp.concatenate(
            [jnp.stack([attn_gain, q_gain, k_gain, ffn_gain], axis=1), router], axis=1
        )
        small = lax.all_gather(small, AXES, axis=0, tiled=True)
        full_attn_gain = small[:, 0].astype(F32)
        full_ffn_gain = small[:, 3].astype(F32)
        full_router = small[:, 4:]
        q_gain_own = lax.dynamic_slice_in_dim(small[:, 1], rank * cols, cols, 0).astype(F32)
        k_gain_own = lax.dynamic_slice_in_dim(small[:, 2], rank * cols, cols, 0).astype(F32)

        group_input = group_gather(layer_input).astype(F32)
        normed = (group_input * inv_rms(group_input) * full_attn_gain).astype(BF)
        q_raw, k_raw = dot(normed, wq), dot(normed, wk)
        v_low = dot(normed, wv).astype(BF)
        squares = jnp.stack([jnp.sum(q_raw * q_raw, -1), jnp.sum(k_raw * k_raw, -1)])
        squares = lax.psum(squares, AXES, axis_index_groups=rows_of)
        roots = lax.rsqrt(squares / width + EPSILON)
        q_root, k_root = roots[0][:, None], roots[1][:, None]
        half_dim = HEAD_DIM // 2
        frequency = 10000.0 ** (-jnp.arange(half_dim, dtype=F32) * 2.0 / HEAD_DIM)
        angle = jnp.arange(seq_len, dtype=F32)[:, None] * frequency[None, :]
        cosine = jnp.concatenate([jnp.cos(angle)] * 2, axis=-1)[None, :, None, :]
        sine = jnp.concatenate([jnp.sin(angle)] * 2, axis=-1)[None, :, None, :]
        by_head = (seqs, seq_len, heads, HEAD_DIM)

        def rope(value):
            value = value.reshape(by_head)
            return (value * cosine + half_turn(value) * sine).astype(BF)

        def rope_back(value):
            return (value * cosine + half_turn_back(value * sine)).reshape(seqs * seq_len, cols)

        q_n, k_n = q_raw * q_root, k_raw * k_root
        q_rot, k_rot = rope(q_n * q_gain_own), rope(k_n * k_gain_own)
        values = v_low.reshape(by_head)
        causal = jnp.arange(seq_len)[:, None] >= jnp.arange(seq_len)[None, :]
        scores = jnp.where(causal, ein("bqhd,bkhd->bhqk", q_rot, k_rot) * scale, -1e30)
        probs = jax.nn.softmax(scores, axis=-1)
        probs_low = probs.astype(BF)
        mixed = ein("bhqk,bkhd->bqhd", probs_low, values).astype(BF).reshape(-1, cols)
        attn_out = group_scatter(dot(mixed, wo).astype(BF)).astype(F32)
        residual = layer_input.astype(F32) + attn_out
        res_root = inv_rms(residual)
        res_n = residual * res_root
        normed2 = (res_n * full_ffn_gain).astype(BF)

        logits = dot(normed2, full_router)
        expert_ids = jnp.arange(experts, dtype=jnp.int32)
        picked = routes[:, :, None] == expert_ids
        chosen = jnp.sum(jnp.where(picked, logits[:, None, :], 0.0), axis=-1)
        gates = jax.nn.softmax(chosen, axis=-1)
        gates_dense = jnp.sum(jnp.where(picked, gates[:, :, None], 0.0), axis=1)
        hits = jnp.any(picked, axis=1)

        all_x = lax.all_gather(normed2, AXES, axis=0, tiled=True).reshape(n_dev, rows, width)
        all_g = lax.all_gather(grad_out, AXES, axis=0, tiled=True).reshape(n_dev, rows, width)
        first = lax.axis_index("ep") * local_experts
        all_gates = lax.all_gather(gates_dense, AXES, axis=0, tiled=False)
        all_routes = lax.all_gather(routes, AXES, axis=0, tiled=False)
        local_ids = first + jnp.arange(local_experts, dtype=jnp.int32)
        local_hits = jnp.any(all_routes[..., None] == local_ids, axis=2).astype(jnp.int32)
        before = jnp.cumsum(local_hits, axis=1) - local_hits
        place = jnp.where(local_hits > 0, before, -1)
        table = (
            place.transpose(0, 2, 1)[:, :, None, :]
            == jnp.arange(cap, dtype=jnp.int32)[None, None, :, None]
        )
        table_low = table.astype(BF)
        local_gates = lax.dynamic_slice_in_dim(all_gates, first, local_experts, 2)
        slot_gates = jnp.sum(
            jnp.where(table, local_gates.transpose(0, 2, 1)[:, :, None, :], 0.0), axis=-1
        )
        slot_gates = slot_gates.transpose(1, 0, 2).reshape(local_experts, n_dev * cap, 1)
        slots = (local_experts, n_dev * cap)
        x_rows = ein("best,btd->ebsd", table_low, all_x).astype(BF).reshape(*slots, width)
        g_rows = ein("best,btd->ebsd", table_low, all_g).astype(BF).reshape(*slots, width)
        gate_part = ein("erd,edf->erf", x_rows, w_gate)
        up_part = ein("erd,edf->erf", x_rows, w_up)
        sig = jax.nn.sigmoid(gate_part)
        silu = gate_part * sig
        hidden = silu * up_part
        raw_grad = ein("erd,efd->erf", g_rows, w_down)
        hidden_gated = (slot_gates * hidden).astype(BF)
        slot_gate_grads = jnp.sum(hidden * raw_grad, axis=-1).reshape(local_experts, n_dev, cap)
        grad_hidden = raw_grad * slot_gates
        gpart_low = (grad_hidden * up_part * sig * (1.0 + gate_part * (1.0 - sig))).astype(BF)
        upart_low = (grad_hidden * silu).astype(BF)
        out_rows = ein("erf,efd->erd", hidden_gated, w_down).astype(BF)
        grad_rows = (
            ein("erf,edf->erd", gpart_low, w_gate) + ein("erf,edf->erd", upart_low, w_up)
        ).astype(BF)
        back = (local_experts, n_dev, cap, width)
        out_part = ein("best,ebsd->btd", table_low, out_rows.reshape(back)).astype(BF)
        grad_part = ein("best,ebsd->btd", table_low, grad_rows.reshape(back)).astype(BF)
        grad_w_down = ein("erf,erd->efd", hidden_gated, g_rows)
        grad_w_gate = ein("erd,erf->edf", x_rows, gpart_low)
        grad_w_up = ein("erd,erf->edf", x_rows, upart_low)

        expert_sum = lax.psum_scatter(out_part, AXES, scatter_dimension=0, tiled=True)
        output = (residual + expert_sum[0].astype(F32)).astype(BF)
        grad_n2 = lax.psum_scatter(grad_part, AXES, scatter_dimension=0, tiled=True)[0]

        gate_grads = jnp.sum(
            jnp.where(table, slot_gate_grads.transpose(1, 0, 2)[..., None], 0.0), axis=2
        )
        gate_grads = gate_grads.reshape(n_ep, n_dp, local_experts, rows)
        gate_grads = lax.psum_scatter(gate_grads, "dp", scatter_dimension=1, tiled=False)
        gate_grads = lax.all_to_all(gate_grads, "ep", 0, 0, tiled=True)
        gate_grads = gate_grads.reshape(experts, rows).T
        gate_grads = jnp.where(hits, gate_grads, 0.0)
        weighted = jnp.sum(gates_dense * gate_grads, axis=-1, keepdims=True)
        grad_logits = (gates_dense * (gate_grads - weighted)).astype(BF)

        grad_n2 = grad_n2.astype(F32) + ein("te,de->td", grad_logits, full_router)
        grad_router = ein("td,te->de", normed2, grad_logits)
        grad_y = grad_out.astype(F32)
        grad_ffn_gain = jnp.sum(grad_n2 * res_n, axis=0)
        dn = grad_n2 * full_ffn_gain
        grad_residual = grad_y + res_root * (dn - res_n * jnp.mean(dn * res_n, -1, keepdims=True))

        gao = group_gather(grad_residual.astype(BF))
        grad_wo = ein("td,te->de", mixed, gao)
        grad_mixed = ein("te,de->td", gao, wo).astype(BF).reshape(by_head)
        grad_values = ein("bhqk,bqhd->bkhd", probs_low, grad_mixed)
        grad_probs = ein("bqhd,bkhd->bhqk", grad_mixed, values)
        delta = jnp.sum(probs * grad_probs, axis=-1, keepdims=True)
        grad_scores = (probs * (grad_probs - delta)).astype(BF)
        grad_q_rot = ein("bhqk,bkhd->bqhd", grad_scores, k_rot) * scale
        grad_k_rot = ein("bhqk,bqhd->bkhd", grad_scores, q_rot) * scale
        gq, gk = rope_back(grad_q_rot), rope_back(grad_k_rot)
        grad_q_gain, grad_k_gain = jnp.sum(gq * q_n, axis=0), jnp.sum(gk * k_n, axis=0)
        gq, gk = gq * q_gain_own, gk * k_gain_own
        inner = jnp.stack([jnp.sum(gq * q_n, -1), jnp.sum(gk * k_n, -1)])
        inner = lax.psum(inner, AXES, axis_index_groups=rows_of) / width
        gq = (q_root * (gq - q_n * inner[0][:, None])).astype(BF)
        gk = (k_root * (gk - k_n * inner[1][:, None])).astype(BF)
        gv = grad_values.reshape(-1, cols).astype(BF)
        grad_normed = ein("te,de->td", gq, wq) + ein("te,de->td", gk, wk)
        grad_normed = grad_normed + ein("te,de->td", gv, wv)
        grad_normed = group_scatter(grad_normed.astype(BF)).astype(F32)
        own_input = layer_input.astype(F32)
        in_root = inv_rms(own_input)
        in_n = own_input * in_root
        grad_attn_gain = jnp.sum(grad_normed * in_n, axis=0)
        dn = grad_normed * full_attn_gain
        grad_input = grad_residual + in_root * (
            dn - in_n * jnp.mean(dn * in_n, -1, keepdims=True)
        )
        grad_qkv = jnp.stack(
            [ein("td,te->de", normed, part) for part in (gq, gk, gv)]
        ).astype(BF)
        grad_qkv = grad_qkv.reshape(3, n_group, group, own, cols).transpose(1, 2, 0, 3, 4)
        grad_qkv = column_scatter(grad_qkv)
        grad_qkv = group_swap(grad_qkv).transpose(1, 2, 0, 3).reshape(3, own, width).astype(F32)
        grad_o = jnp.zeros((width, width), BF)
        grad_o = lax.dynamic_update_slice_in_dim(grad_o, grad_wo.astype(BF), rank * cols, 0)
        grad_o = lax.psum_scatter(grad_o, AXES, scatter_dimension=0, tiled=True).astype(F32)

        def spread(part):
            return lax.dynamic_update_slice_in_dim(jnp.zeros((width,), F32), part, rank * cols, 0)

        small_grads = jnp.concatenate(
            [
                jnp.stack(
                    [grad_attn_gain, spread(grad_q_gain), spread(grad_k_gain), grad_ffn_gain],
                    axis=1,
                ),
                grad_router,
            ],
            axis=1,
        )
        small_grads = lax.psum_scatter(small_grads, AXES, scatter_dimension=0, tiled=True)
        return (
            output, grad_input, small_grads[:, 0], grad_qkv[0], grad_qkv[1], grad_qkv[2],
            small_grads[:, 1], small_grads[:, 2], grad_o, small_grads[:, 3], small_grads[:, 4:],
            grad_w_gate, grad_w_up, grad_w_down,
        )

    return shards


def solution(mesh):
    row, vec = P(("ep", "dp"), None), P(("ep", "dp"))
    wide, deep = P("ep", None, "dp"), P("ep", "dp", None)
    in_specs = (
        row, row, vec, row, row, row, vec, vec, row, vec, row, wide, wide, deep, row,
    )
    out_specs = (
        row, row, vec, row, row, row, vec, vec, row, vec, row, wide, wide, deep,
    )
    shards = build(mesh.shape["ep"], mesh.shape["dp"])
    return jax.shard_map(shards, mesh=mesh, in_specs=in_specs, out_specs=out_specs, check_vma=False)
```

```python
import functools

import jax
import jax.numpy as jnp
from jax import lax
from jax.experimental import pallas as pl
from jax.experimental.pallas import tpu as pltpu
from jax.sharding import PartitionSpec as P

HEAD_DIM = 128
EPSILON = 1e-05
AXES = ("ep", "dp")
BF = jnp.bfloat16
F32 = jnp.float32
ANY = pl.BlockSpec(memory_space=pl.ANY)
VMEM = pl.BlockSpec(memory_space=pltpu.VMEM)
MESH = pl.DeviceIdType.MESH
STEP = 512
HOOKS = 8


def dot(left, right):
    return jnp.dot(left, right, preferred_element_type=F32)


def dot_t(left, right):
    return lax.dot_general(left, right, (((1,), (1,)), ((), ())), preferred_element_type=F32)


def tdot(left, right):
    return lax.dot_general(left, right, (((0,), (0,)), ((), ())), preferred_element_type=F32)


def flip(value, other, count):
    result, bit = 0, 1
    while bit < count:
        result = result + ((value // bit) % 2 + (other // bit) % 2) % 2 * bit
        bit *= 2
    return result


class Place:
    def __init__(self, n_dp):
        ep, dp = lax.axis_index("ep"), lax.axis_index("dp")
        half = n_dp // 2
        self.n_dp, self.half = n_dp, half
        self.layer, self.y = ep // 2, ep % 2
        self.x, self.core = dp // 2, dp % 2
        self.rank = self.y * n_dp + dp
        self.ep, self.dp = ep, dp
        self.sibling = (ep, self.x * 2 + 1 - self.core)
        self.over_x = (ep, (1 - self.x) * 2 + self.core)
        self.over_y = (self.layer * 2 + 1 - self.y, dp)

    def at_layer(self, layer):
        return (layer * 2 + self.y, self.dp)


def greet(partners):
    barrier = pltpu.get_barrier_semaphore()
    for partner in partners:
        pl.semaphore_signal(barrier, inc=1, device_id=partner, device_id_type=MESH)
    pl.semaphore_wait(barrier, len(partners))


def experts_kernel(
    n_dp, experts,
    x_own, all_g, table, wg_hbm, wu_hbm, wd_hbm,
    out_sum, grad_sum, x_out, g_out, acts_out, all_x,
    sib_o, sib_g, one_o, one_g, two_o, two_g, z_o, z_g,
    wg, wu, wd, xs, gs, gate_rows, acts, xin, gin, stage_o, stage_g, acc_o, acc_g, tmp_o, tmp_g,
    mine_o, mine_g,
    w_sem, in_sem, keep_sem, act_sem, own_sem, zx_send, zx_recv, ag_send, ag_recv,
    sib_send, sib_recv, one_send, one_recv, two_send, two_recv, z_send, z_recv, tmp_sem,
):
    n_dev, rows, wide = all_x.shape
    local, width, hid = wg.shape
    cap = xs.shape[2]
    group = 2 * n_dp
    layers = n_dev // group
    m = group * cap
    slots = xin.shape[0]
    half = width // 2
    here = Place(n_dp)
    rank, core, x, y = here.rank, here.core, here.x, here.y
    first = here.ep * local

    def remote(src, dst, send, recv, device):
        return pltpu.make_async_remote_copy(
            src_ref=src, dst_ref=dst, send_sem=send, recv_sem=recv,
            device_id=device, device_id_type=MESH,
        )

    def layer_of(i):
        return flip(here.layer, i, layers)

    def weights():
        return [
            pltpu.make_async_copy(s, d, w_sem.at[i])
            for i, (s, d) in enumerate(((wg_hbm, wg), (wu_hbm, wu), (wd_hbm, wd)))
        ]

    def z_copy(i):
        me = here.layer * group + rank
        return remote(
            x_own, all_x.at[me], zx_send.at[i], zx_recv.at[i], here.at_layer(layer_of(i))
        )

    def own_copy():
        return pltpu.make_async_copy(x_own, all_x.at[here.layer * group + rank], own_sem.at[0])

    over_x_rank = y * n_dp + (1 - x) * 2 + core
    over_y_rank = (1 - y) * n_dp + x * 2 + core
    across_rank = (1 - y) * n_dp + (1 - x) * 2 + core
    first_half, second_half = pl.ds(0, half), pl.ds(half, wide - half)

    def gather_copy(i, kind):
        base = layer_of(i) * group
        which, cols, device = {
            0: (rank, first_half, here.over_x),
            1: (rank, second_half, here.over_x),
            2: (rank, first_half, here.over_y),
            3: (rank, second_half, here.over_y),
            4: (over_x_rank, first_half, here.over_y),
            5: (over_y_rank, second_half, here.over_x),
            6: (rank, pl.ds(0, wide), here.sibling),
            7: (over_x_rank, pl.ds(0, wide), here.sibling),
            8: (over_y_rank, pl.ds(0, wide), here.sibling),
            9: (across_rank, pl.ds(0, wide), here.sibling),
        }[kind]
        ref = all_x.at[base + which, :, cols]
        return remote(ref, ref, ag_send.at[i, kind], ag_recv.at[i, kind], device)

    def gather_a(i):
        if isinstance(i, int) and i == 0:
            own_copy().wait()
        else:
            z_copy(i).wait_recv()
        for kind in (0, 3, 1, 2, 6):
            gather_copy(i, kind).start()

    def gather_b(i):
        for got, then in ((0, 4), (3, 5), (1, 7), (2, 8)):
            gather_copy(i, got).wait_recv()
            gather_copy(i, then).start()

    def gather_c(i):
        gather_copy(i, 4).wait_recv()
        gather_copy(i, 5).wait_recv()
        gather_copy(i, 9).start()

    def gather_d(i):
        for kind in (6, 7, 8, 9):
            gather_copy(i, kind).wait_recv()

    def sib_copy(i, q, slot):
        return (
            remote(stage_o.at[slot], sib_o.at[i, q], sib_send.at[0, slot], sib_recv.at[0, i, q],
                   here.sibling),
            remote(stage_g.at[slot], sib_g.at[i, q], sib_send.at[1, slot], sib_recv.at[1, i, q],
                   here.sibling),
        )

    def one_copy(i, j):
        return (
            remote(acc_o.at[j * 2 + 1 - x], one_o.at[i, j], one_send.at[0, j],
                   one_recv.at[0, i, j], here.over_x),
            remote(acc_g.at[(1 - y) * 2 + j], one_g.at[i, j], one_send.at[1, j],
                   one_recv.at[1, i, j], here.over_y),
        )

    def two_copy(i):
        return (
            remote(acc_o.at[(1 - y) * 2 + x], two_o.at[i], two_send.at[0], two_recv.at[0, i],
                   here.over_y),
            remote(acc_g.at[y * 2 + 1 - x], two_g.at[i], two_send.at[1], two_recv.at[1, i],
                   here.over_x),
        )

    def out_copy(i):
        device = here.at_layer(layer_of(i))
        own = y * 2 + x
        return (
            remote(acc_o.at[own], z_o.at[i], z_send.at[0], z_recv.at[0, i], device),
            remote(acc_g.at[own], z_g.at[i], z_send.at[1], z_recv.at[1, i], device),
        )

    def fetch(src_o, src_g, slot):
        return (
            pltpu.make_async_copy(src_o, tmp_o.at[slot], tmp_sem.at[0, slot]),
            pltpu.make_async_copy(src_g, tmp_g.at[slot], tmp_sem.at[1, slot]),
        )

    def start(copies):
        for copy in copies:
            copy.start()

    def finish(copies):
        for copy in copies:
            copy.wait()

    def add(dst, q, tmp, slot):
        total = dst[q].astype(F32) + tmp[slot].astype(F32)
        dst[q] = total.astype(BF)

    def sum_sibling(i):
        def bring(q, slot):
            for copy in sib_copy(i, q, 0):
                copy.wait_recv()
            start(fetch(sib_o.at[i, q], sib_g.at[i, q], slot))

        bring(0, 0)
        for q in range(4):
            if q < 3:
                bring(q + 1, (q + 1) % 2)
            finish(fetch(sib_o.at[i, q], sib_g.at[i, q], q % 2))
            add(acc_o, q, tmp_o, q % 2)
            add(acc_g, q, tmp_g, q % 2)
        for j in range(2):
            start(one_copy(i, j))

    def sum_one(i):
        def bring(j):
            for copy in one_copy(i, j):
                copy.wait_recv()
            start(fetch(one_o.at[i, j], one_g.at[i, j], j))

        bring(0)
        bring(1)
        for j in range(2):
            finish(fetch(one_o.at[i, j], one_g.at[i, j], j))
            add(acc_o, j * 2 + x, tmp_o, j)
            add(acc_g, y * 2 + j, tmp_g, j)
        start(two_copy(i))

    def sum_two(i):
        for copy in two_copy(i):
            copy.wait_recv()
        start(fetch(two_o.at[i], two_g.at[i], 0))
        finish(fetch(two_o.at[i], two_g.at[i], 0))
        own = y * 2 + x
        add(acc_o, own, tmp_o, 0)
        add(acc_g, own, tmp_g, 0)
        for j in range(2):
            for copy in one_copy(i, j):
                copy.wait_send()
        for copy in two_copy(i):
            copy.wait_send()

        @pl.when(i == 0)
        def _():
            mine_o[...] = acc_o[own]
            mine_g[...] = acc_g[own]

        @pl.when(i > 0)
        def _():
            start(out_copy(i))

    start(weights())
    greet([here.over_x, here.over_y, here.sibling]
          + [here.at_layer(layer_of(i)) for i in range(1, layers)])
    own_copy().start()
    for i in range(1, layers):
        z_copy(i).start()
    gather_a(0)
    gather_b(0)
    gather_c(0)
    gather_a(1)

    def chunk(i, carry):
        base = layer_of(i) * group

        @pl.when(i > 0)
        def _():
            sum_sibling(i - 1)

        gather_d(i)

        def load(b, slot):
            return (
                pltpu.make_async_copy(all_x.at[base + b], xin.at[slot], in_sem.at[0, slot]),
                pltpu.make_async_copy(
                    all_g.at[base + b, :, pl.ds(0, width)], gin.at[slot], in_sem.at[1, slot]
                ),
            )

        for b in range(slots - 1):
            start(load(b, b))

        def bring(b, c):
            slot = lax.rem(b, slots)
            finish(load(b, slot))

            @pl.when(b + slots - 1 < group)
            def _():
                start(load(b + slots - 1, lax.rem(b + slots - 1, slots)))

            hot = table[base + b]
            for src, dst in ((xin, xs), (gin, gs)):
                for n in range(0, width, STEP):
                    got = dot(hot, src[slot, :, n : n + STEP]).astype(BF)
                    dst[:, b, :, n : n + STEP] = got.reshape(local, cap, STEP)
            gates = dot(hot, xin[slot, :, width:wide])
            lanes = lax.broadcasted_iota(jnp.int32, gates.shape, 1) % experts
            expert = lax.broadcasted_iota(jnp.int32, gates.shape, 0) // cap + first
            gates = jnp.sum(jnp.where(lanes == expert, gates, 0.0), axis=1, keepdims=True)
            gate_rows[:, b] = jnp.broadcast_to(gates, (local * cap, 128)).reshape(local, cap, 128)
            return c

        lax.fori_loop(0, group, bring, 0)

        def keep(e):
            return (
                pltpu.make_async_copy(xs.at[e], x_out.at[e, pl.ds(base, group)], keep_sem.at[0, e]),
                pltpu.make_async_copy(gs.at[e], g_out.at[e, pl.ds(base, group)], keep_sem.at[1, e]),
            )

        def keep_acts(e, slot):
            return pltpu.make_async_copy(
                acts.at[slot], acts_out.at[:, e, pl.ds(base * cap, m)], act_sem.at[slot]
            )

        lax.fori_loop(0, local, lambda e, c: (start(keep(e)), c)[1], 0)

        @pl.when(i == 0)
        def _():
            finish(weights())

        def expert(e, c):
            def hook(number, when, action):
                @pl.when(jnp.logical_and(e == number * local // HOOKS, when))
                def _():
                    action()

            hook(1, i + 2 < layers, lambda: gather_a(i + 2))
            hook(2, i + 1 < layers, lambda: gather_b(i + 1))
            hook(4, i + 1 < layers, lambda: gather_c(i + 1))
            hook(5, i > 0, lambda: sum_one(i - 1))
            hook(7, i > 0, lambda: sum_two(i - 1))
            slot = lax.rem(e, 2)

            @pl.when(jnp.logical_or(i > 0, e >= 2))
            def _():
                keep_acts(e, slot).wait()

            xe = xs[e].reshape(m, width)
            ge = gs[e].reshape(m, width)
            gate_part = dot(xe, wg[e])
            up_part = dot(xe, wu[e])
            raw = dot_t(ge, wd[e])
            gate = gate_rows[e].reshape(m, 128)[:, :1]
            sig = 1.0 / (1.0 + jnp.exp(-gate_part))
            silu = gate_part * sig
            hidden = silu * up_part
            own = jnp.sum(hidden * raw, axis=1, keepdims=True)
            lanes = lax.broadcasted_iota(jnp.int32, (m, 128), 1)
            grad_hidden = raw * gate
            hg = (hidden * gate).astype(BF)
            dg = (grad_hidden * up_part * sig * (1.0 + gate_part * (1.0 - sig))).astype(BF)
            du = (grad_hidden * silu).astype(BF)
            gate_rows[e] = jnp.where(lanes == first + e, own, 0.0).reshape(group, cap, 128)
            acts[slot, 0] = hg
            acts[slot, 1] = dg
            acts[slot, 2] = du
            keep_acts(e, slot).start()
            finish(keep(e))
            for n in range(0, width, STEP):
                out = dot(hg, wd[e, :, n : n + STEP]).astype(BF)
                gs[e, :, :, n : n + STEP] = out.reshape(group, cap, STEP)
                back = dot_t(dg, wg[e, n : n + STEP, :]) + dot_t(du, wu[e, n : n + STEP, :])
                xs[e, :, :, n : n + STEP] = back.astype(BF).reshape(group, cap, STEP)
            return c

        lax.fori_loop(0, local, expert, 0)

        def combine(b, put_o, put_g):
            hot = table[base + b]
            for n in range(0, width, STEP):
                got = gs[:, b, :, n : n + STEP].reshape(local * cap, STEP)
                put_o(n, STEP, tdot(hot, got).astype(BF))
                got = xs[:, b, :, n : n + STEP].reshape(local * cap, STEP)
                put_g(n, STEP, tdot(hot, got).astype(BF))
            got = gate_rows[:, b].reshape(local * cap, 128).astype(BF)
            put_g(width, 128, tdot(hot, got).astype(BF))

        def give(q, c):
            slot = lax.rem(q, 2)

            @pl.when(jnp.logical_or(i > 0, q >= 2))
            def _():
                for copy in sib_copy(i, q, slot):
                    copy.wait_send()

            def put_o(n, size, value):
                stage_o[slot, :, pl.ds(n, size)] = value

            def put_g(n, size, value):
                stage_g[slot, :, pl.ds(n, size)] = value

            combine(q * 2 + 1 - core, put_o, put_g)
            start(sib_copy(i, q, slot))
            return c

        lax.fori_loop(0, 4, give, 0)

        @pl.when(i > 1)
        def _():
            for copy in out_copy(i - 1):
                copy.wait_send()

        def hold(q, c):
            def put_o(n, size, value):
                acc_o[q, :, pl.ds(n, size)] = value

            def put_g(n, size, value):
                acc_g[q, :, pl.ds(n, size)] = value

            combine(q * 2 + core, put_o, put_g)
            return c

        lax.fori_loop(0, 4, hold, 0)
        return carry

    lax.fori_loop(0, layers, chunk, 0)
    last = layers - 1
    sum_sibling(last)
    sum_one(last)
    sum_two(last)
    out_sum[...] = mine_o[...].astype(F32)
    grad_sum[...] = mine_g[...].astype(F32)

    def last_sum(i, c):
        for copy in out_copy(i):
            copy.wait_recv()
        start(fetch(z_o.at[i], z_g.at[i], 0))
        finish(fetch(z_o.at[i], z_g.at[i], 0))
        out_sum[...] += tmp_o[0].astype(F32)
        grad_sum[...] += tmp_g[0].astype(F32)
        return c

    lax.fori_loop(1, layers, last_sum, 0)
    for copy in out_copy(last):
        copy.wait_send()
    for slot in range(2):
        for copy in sib_copy(last, slot, slot):
            copy.wait_send()
        pltpu.make_async_copy(
            acts.at[slot], acts_out.at[:, 0, pl.ds(0, m)], act_sem.at[slot]
        ).wait()

    def drain(i, c):
        for kind in range(10):
            gather_copy(i, kind).wait_send()
        return c

    lax.fori_loop(0, layers, drain, 0)
    lax.fori_loop(1, layers, lambda i, c: (z_copy(i).wait_send(), c)[1], 0)


def run_experts(x_own, all_g, table, wg, wu, wd, n_dp, experts, cap):
    rows, wide = x_own.shape
    n_dev = all_g.shape[0]
    local, width, hid = wg.shape
    group = 2 * n_dp
    layers = n_dev // group
    m = group * cap
    wide_g = width + 128
    slots = 3
    dma = pltpu.SemaphoreType.DMA
    shape = jax.ShapeDtypeStruct
    slot_rows = shape((local, n_dev, cap, width), BF)
    flops = 12 * n_dev * cap * local * width * hid
    result = pl.pallas_call(
        functools.partial(experts_kernel, n_dp, experts),
        out_shape=(
            shape((rows, width), F32), shape((rows, wide_g), F32),
            slot_rows, slot_rows,
            shape((3, local, n_dev * cap, hid), BF),
            shape((n_dev, rows, wide), BF),
            shape((layers, 4, rows, width), BF), shape((layers, 4, rows, wide_g), BF),
            shape((layers, 2, rows, width), BF), shape((layers, 2, rows, wide_g), BF),
            shape((layers, rows, width), BF), shape((layers, rows, wide_g), BF),
            shape((layers, rows, width), BF), shape((layers, rows, wide_g), BF),
        ),
        in_specs=[ANY, ANY, VMEM, ANY, ANY, ANY],
        out_specs=(VMEM, VMEM) + (ANY,) * 12,
        scratch_shapes=[
            pltpu.VMEM(wg.shape, BF), pltpu.VMEM(wu.shape, BF), pltpu.VMEM(wd.shape, BF),
            pltpu.VMEM((local, group, cap, width), BF),
            pltpu.VMEM((local, group, cap, width), BF),
            pltpu.VMEM((local, group, cap, 128), F32),
            pltpu.VMEM((2, 3, m, hid), BF),
            pltpu.VMEM((slots, rows, wide), BF),
            pltpu.VMEM((slots, rows, width), BF),
            pltpu.VMEM((2, rows, width), BF), pltpu.VMEM((2, rows, wide_g), BF),
            pltpu.VMEM((4, rows, width), BF), pltpu.VMEM((4, rows, wide_g), BF),
            pltpu.VMEM((2, rows, width), BF), pltpu.VMEM((2, rows, wide_g), BF),
            pltpu.VMEM((rows, width), BF), pltpu.VMEM((rows, wide_g), BF),
            dma((3,)), dma((2, slots)), dma((2, local)), dma((2,)), dma((1,)),
            dma((layers,)), dma((layers,)), dma((layers, 10)), dma((layers, 10)),
            dma((2, 2)), dma((2, layers, 4)), dma((2, 2)), dma((2, layers, 2)),
            dma((2,)), dma((2, layers)), dma((2,)), dma((2, layers)), dma((2, 2)),
        ],
        compiler_params=pltpu.CompilerParams(
            collective_id=1, has_side_effects=True, vmem_limit_bytes=64 * 2**20
        ),
        cost_estimate=pl.CostEstimate(flops=flops, bytes_accessed=200 * 2**20, transcendentals=0),
    )(x_own, all_g, table, wg, wu, wd)
    return result[:5]


def weights_kernel(x, g, acts, grad_g, grad_u, grad_d):
    first = pl.program_id(1) == 0
    xe, ge = x[0], g[0]

    def put(ref, n, size, value, axis):
        at = (0, pl.ds(n, size), slice(None)) if axis == 0 else (0, slice(None), pl.ds(n, size))

        @pl.when(first)
        def _():
            ref[at] = value

        @pl.when(jnp.logical_not(first))
        def _():
            ref[at] += value

    hg, dg, du = acts[0, 0], acts[1, 0], acts[2, 0]
    for n in range(0, xe.shape[1], STEP):
        part = xe[:, n : n + STEP]
        put(grad_g, n, STEP, tdot(part, dg), 0)
        put(grad_u, n, STEP, tdot(part, du), 0)
        put(grad_d, n, STEP, tdot(hg, ge[:, n : n + STEP]), 1)


def run_weights(x_slots, g_slots, acts):
    local, n_dev, cap, width = x_slots.shape
    hid = acts.shape[-1]
    total = n_dev * cap
    tile = min(1024, total)
    x_slots = x_slots.reshape(local, total, width)
    g_slots = g_slots.reshape(local, total, width)
    row = pl.BlockSpec((1, tile, width), lambda e, k: (e, k, 0))
    wide = pl.BlockSpec((1, width, hid), lambda e, k: (e, 0, 0))
    deep = pl.BlockSpec((1, hid, width), lambda e, k: (e, 0, 0))
    return pl.pallas_call(
        weights_kernel,
        grid=(local, total // tile),
        out_shape=(
            jax.ShapeDtypeStruct((local, width, hid), F32),
            jax.ShapeDtypeStruct((local, width, hid), F32),
            jax.ShapeDtypeStruct((local, hid, width), F32),
        ),
        in_specs=[row, row, pl.BlockSpec((3, 1, tile, hid), lambda e, k: (0, e, k, 0))],
        out_specs=(wide, wide, deep),
        compiler_params=pltpu.CompilerParams(vmem_limit_bytes=60 * 2**20),
        cost_estimate=pl.CostEstimate(
            flops=6 * local * total * width * hid, bytes_accessed=130 * 2**20, transcendentals=0
        ),
    )(x_slots, g_slots, acts)


def ein(spec, left, right):
    return jnp.einsum(spec, left, right, preferred_element_type=F32)


def inv_rms(value):
    return lax.rsqrt(jnp.mean(value * value, axis=-1, keepdims=True) + EPSILON)


def half_turn(value):
    half = value.shape[-1] // 2
    return jnp.concatenate([-value[..., half:], value[..., :half]], axis=-1)


def half_turn_back(value):
    half = value.shape[-1] // 2
    return jnp.concatenate([value[..., half:], -value[..., :half]], axis=-1)


def build(n_ep, n_dp):
    n_dev = n_ep * n_dp
    group = 2 * n_dp
    n_group = n_dev // group
    rows_of = [[g * group + r for r in range(group)] for g in range(n_group)]
    cols_of = [[g * group + r for g in range(n_group)] for r in range(group)]

    def group_gather(value, axis=0):
        return lax.all_gather(value, AXES, axis=axis, tiled=True, axis_index_groups=rows_of)

    def group_scatter(value):
        return lax.psum_scatter(
            value, AXES, scatter_dimension=0, tiled=True, axis_index_groups=rows_of
        )

    def group_swap(value):
        return lax.all_to_all(value, AXES, 0, 0, tiled=True, axis_index_groups=rows_of)

    def column_gather(value):
        return lax.all_gather(value, AXES, axis=0, tiled=False, axis_index_groups=cols_of)

    def column_scatter(value):
        return lax.psum_scatter(
            value, AXES, scatter_dimension=0, tiled=False, axis_index_groups=cols_of
        )

    def shards(
        layer_input, grad_out, attn_gain, w_q, w_k, w_v, q_gain, k_gain, w_o, ffn_gain,
        router, w_gate, w_up, w_down, routes,
    ):
        rows, width = layer_input.shape
        cols = width // group
        heads = cols // HEAD_DIM
        seqs = 2
        seq_len = rows * n_dp
        scale = HEAD_DIM ** (-0.5)
        own = width // n_dev
        rank = (lax.axis_index("ep") % 2) * n_dp + lax.axis_index("dp")
        local_experts = w_gate.shape[0]
        experts = router.shape[1]
        top = routes.shape[1]
        cap = 2 * rows * top // experts

        qkv = jnp.stack([w_q, w_k, w_v]).reshape(3, own, group, cols).transpose(2, 0, 1, 3)
        qkv = group_swap(qkv)
        qkv = column_gather(qkv)
        qkv = qkv.transpose(2, 0, 1, 3, 4).reshape(3, width, cols)
        wq, wk, wv = qkv[0], qkv[1], qkv[2]
        full_o = lax.all_gather(w_o, AXES, axis=0, tiled=True)
        wo = lax.dynamic_slice_in_dim(full_o, rank * cols, cols, 0)

        small = jnp.concatenate(
            [jnp.stack([attn_gain, q_gain, k_gain, ffn_gain], axis=1), router], axis=1
        )
        small = lax.all_gather(small, AXES, axis=0, tiled=True)
        full_attn_gain = small[:, 0].astype(F32)
        full_ffn_gain = small[:, 3].astype(F32)
        full_router = small[:, 4:]
        q_gain_own = lax.dynamic_slice_in_dim(small[:, 1], rank * cols, cols, 0).astype(F32)
        k_gain_own = lax.dynamic_slice_in_dim(small[:, 2], rank * cols, cols, 0).astype(F32)

        group_input = group_gather(layer_input).astype(F32)
        normed = (group_input * inv_rms(group_input) * full_attn_gain).astype(BF)
        q_raw, k_raw = dot(normed, wq), dot(normed, wk)
        v_low = dot(normed, wv).astype(BF)
        squares = jnp.stack([jnp.sum(q_raw * q_raw, -1), jnp.sum(k_raw * k_raw, -1)])
        squares = lax.psum(squares, AXES, axis_index_groups=rows_of)
        roots = lax.rsqrt(squares / width + EPSILON)
        q_root, k_root = roots[0][:, None], roots[1][:, None]
        half_dim = HEAD_DIM // 2
        frequency = 10000.0 ** (-jnp.arange(half_dim, dtype=F32) * 2.0 / HEAD_DIM)
        angle = jnp.arange(seq_len, dtype=F32)[:, None] * frequency[None, :]
        cosine = jnp.concatenate([jnp.cos(angle)] * 2, axis=-1)[None, :, None, :]
        sine = jnp.concatenate([jnp.sin(angle)] * 2, axis=-1)[None, :, None, :]
        by_head = (seqs, seq_len, heads, HEAD_DIM)

        def rope(value):
            value = value.reshape(by_head)
            return (value * cosine + half_turn(value) * sine).astype(BF)

        def rope_back(value):
            return (value * cosine + half_turn_back(value * sine)).reshape(seqs * seq_len, cols)

        q_n, k_n = q_raw * q_root, k_raw * k_root
        q_rot, k_rot = rope(q_n * q_gain_own), rope(k_n * k_gain_own)
        values = v_low.reshape(by_head)
        causal = jnp.arange(seq_len)[:, None] >= jnp.arange(seq_len)[None, :]
        scores = jnp.where(causal, ein("bqhd,bkhd->bhqk", q_rot, k_rot) * scale, -1e30)
        probs = jax.nn.softmax(scores, axis=-1)
        probs_low = probs.astype(BF)
        mixed = ein("bhqk,bkhd->bqhd", probs_low, values).astype(BF).reshape(-1, cols)
        attn_out = group_scatter(dot(mixed, wo).astype(BF)).astype(F32)
        residual = layer_input.astype(F32) + attn_out
        res_root = inv_rms(residual)
        res_n = residual * res_root
        normed2 = (res_n * full_ffn_gain).astype(BF)

        logits = dot(normed2, full_router)
        expert_ids = jnp.arange(experts, dtype=jnp.int32)
        picked = routes[:, :, None] == expert_ids
        chosen = jnp.sum(jnp.where(picked, logits[:, None, :], 0.0), axis=-1)
        gates = jax.nn.softmax(chosen, axis=-1)
        gates_dense = jnp.sum(jnp.where(picked, gates[:, :, None], 0.0), axis=1)
        hits = jnp.any(picked, axis=1)

        before = jnp.cumsum(hits.astype(jnp.int32), axis=0) - hits.astype(jnp.int32)
        place = jnp.where(hits, before, -1).astype(BF)
        sent = jnp.concatenate([grad_out, place, jnp.zeros((rows, 128 - experts), BF)], axis=1)
        all_g = lax.all_gather(sent, AXES, axis=0, tiled=True).reshape(n_dev, rows, -1)
        first = lax.axis_index("ep") * local_experts
        own_place = lax.dynamic_slice_in_dim(all_g, width + first, local_experts, 2)
        table = (
            own_place.transpose(0, 2, 1)[:, :, None, :]
            == jnp.arange(cap, dtype=jnp.int32).astype(BF)[None, None, :, None]
        )
        table = table.astype(BF).reshape(n_dev, local_experts * cap, rows)

        gates_high = gates_dense.astype(BF)
        gates_rest = (gates_dense - gates_high.astype(F32)).astype(BF)
        x_own = jnp.concatenate([normed2, gates_high, gates_rest], axis=1)
        expert_sum, grad_sum, x_slots, g_slots, acts = run_experts(
            x_own, all_g, table, w_gate, w_up, w_down, n_dp, experts, cap
        )
        grad_w_gate, grad_w_up, grad_w_down = run_weights(x_slots, g_slots, acts)
        output = (residual + expert_sum).astype(BF)
        gate_grads = jnp.where(hits, grad_sum[:, width : width + experts], 0.0)
        weighted = jnp.sum(gates_dense * gate_grads, axis=-1, keepdims=True)
        grad_logits = (gates_dense * (gate_grads - weighted)).astype(BF)

        grad_n2 = grad_sum[:, :width] + ein("te,de->td", grad_logits, full_router)
        grad_router = ein("td,te->de", normed2, grad_logits)
        grad_y = grad_out.astype(F32)
        grad_ffn_gain = jnp.sum(grad_n2 * res_n, axis=0)
        dn = grad_n2 * full_ffn_gain
        grad_residual = grad_y + res_root * (dn - res_n * jnp.mean(dn * res_n, -1, keepdims=True))

        gao = group_gather(grad_residual.astype(BF))
        grad_wo = ein("td,te->de", mixed, gao)
        grad_mixed = ein("te,de->td", gao, wo).astype(BF).reshape(by_head)
        grad_values = ein("bhqk,bqhd->bkhd", probs_low, grad_mixed)
        grad_probs = ein("bqhd,bkhd->bhqk", grad_mixed, values)
        delta = jnp.sum(probs * grad_probs, axis=-1, keepdims=True)
        grad_scores = (probs * (grad_probs - delta)).astype(BF)
        grad_q_rot = ein("bhqk,bkhd->bqhd", grad_scores, k_rot) * scale
        grad_k_rot = ein("bhqk,bqhd->bkhd", grad_scores, q_rot) * scale
        gq, gk = rope_back(grad_q_rot), rope_back(grad_k_rot)
        grad_q_gain, grad_k_gain = jnp.sum(gq * q_n, axis=0), jnp.sum(gk * k_n, axis=0)
        gq, gk = gq * q_gain_own, gk * k_gain_own
        inner = jnp.stack([jnp.sum(gq * q_n, -1), jnp.sum(gk * k_n, -1)])
        inner = lax.psum(inner, AXES, axis_index_groups=rows_of) / width
        gq = (q_root * (gq - q_n * inner[0][:, None])).astype(BF)
        gk = (k_root * (gk - k_n * inner[1][:, None])).astype(BF)
        gv = grad_values.reshape(-1, cols).astype(BF)
        grad_normed = ein("te,de->td", gq, wq) + ein("te,de->td", gk, wk)
        grad_normed = grad_normed + ein("te,de->td", gv, wv)
        grad_normed = group_scatter(grad_normed.astype(BF)).astype(F32)
        own_input = layer_input.astype(F32)
        in_root = inv_rms(own_input)
        in_n = own_input * in_root
        grad_attn_gain = jnp.sum(grad_normed * in_n, axis=0)
        dn = grad_normed * full_attn_gain
        grad_input = grad_residual + in_root * (
            dn - in_n * jnp.mean(dn * in_n, -1, keepdims=True)
        )
        grad_qkv = jnp.stack(
            [ein("td,te->de", normed, part) for part in (gq, gk, gv)]
        ).astype(BF)
        grad_qkv = grad_qkv.reshape(3, n_group, group, own, cols).transpose(1, 2, 0, 3, 4)
        grad_qkv = column_scatter(grad_qkv)
        grad_qkv = group_swap(grad_qkv).transpose(1, 2, 0, 3).reshape(3, own, width).astype(F32)
        grad_o = jnp.zeros((width, width), BF)
        grad_o = lax.dynamic_update_slice_in_dim(grad_o, grad_wo.astype(BF), rank * cols, 0)
        grad_o = lax.psum_scatter(grad_o, AXES, scatter_dimension=0, tiled=True).astype(F32)

        def spread(part):
            return lax.dynamic_update_slice_in_dim(jnp.zeros((width,), F32), part, rank * cols, 0)

        small_grads = jnp.concatenate(
            [
                jnp.stack(
                    [grad_attn_gain, spread(grad_q_gain), spread(grad_k_gain), grad_ffn_gain],
                    axis=1,
                ),
                grad_router,
            ],
            axis=1,
        )
        small_grads = lax.psum_scatter(small_grads, AXES, scatter_dimension=0, tiled=True)
        return (
            output, grad_input, small_grads[:, 0], grad_qkv[0], grad_qkv[1], grad_qkv[2],
            small_grads[:, 1], small_grads[:, 2], grad_o, small_grads[:, 3], small_grads[:, 4:],
            grad_w_gate, grad_w_up, grad_w_down,
        )

    return shards


def solution(mesh):
    row, vec = P(("ep", "dp"), None), P(("ep", "dp"))
    wide, deep = P("ep", None, "dp"), P("ep", "dp", None)
    in_specs = (
        row, row, vec, row, row, row, vec, vec, row, vec, row, wide, wide, deep, row,
    )
    out_specs = (
        row, row, vec, row, row, row, vec, vec, row, vec, row, wide, wide, deep,
    )
    shards = build(mesh.shape["ep"], mesh.shape["dp"])
    return jax.shard_map(shards, mesh=mesh, in_specs=in_specs, out_specs=out_specs, check_vma=False)
```

```python
import functools

import jax
import jax.numpy as jnp
from jax import lax
from jax.experimental import pallas as pl
from jax.experimental.pallas import tpu as pltpu
from jax.sharding import PartitionSpec as P

HEAD_DIM = 128
EPSILON = 1e-05
AXES = ("ep", "dp")
BF = jnp.bfloat16
F32 = jnp.float32
ANY = pl.BlockSpec(memory_space=pl.ANY)
VMEM = pl.BlockSpec(memory_space=pltpu.VMEM)
MESH = pl.DeviceIdType.MESH
STEP = 512
HOOKS = 8


def dot(left, right):
    return jnp.dot(left, right, preferred_element_type=F32)


def dot_t(left, right):
    return lax.dot_general(left, right, (((1,), (1,)), ((), ())), preferred_element_type=F32)


def tdot(left, right):
    return lax.dot_general(left, right, (((0,), (0,)), ((), ())), preferred_element_type=F32)


def flip(value, other, count):
    result, bit = 0, 1
    while bit < count:
        result = result + ((value // bit) % 2 + (other // bit) % 2) % 2 * bit
        bit *= 2
    return result


class Place:
    def __init__(self, n_dp):
        ep, dp = lax.axis_index("ep"), lax.axis_index("dp")
        half = n_dp // 2
        self.n_dp, self.half = n_dp, half
        self.layer, self.y = ep // 2, ep % 2
        self.x, self.core = dp // 2, dp % 2
        self.rank = self.y * n_dp + dp
        self.ep, self.dp = ep, dp
        self.sibling = (ep, self.x * 2 + 1 - self.core)
        self.over_x = (ep, (1 - self.x) * 2 + self.core)
        self.over_y = (self.layer * 2 + 1 - self.y, dp)

    def at_layer(self, layer):
        return (layer * 2 + self.y, self.dp)


def greet(partners):
    barrier = pltpu.get_barrier_semaphore()
    for partner in partners:
        pl.semaphore_signal(barrier, inc=1, device_id=partner, device_id_type=MESH)
    pl.semaphore_wait(barrier, len(partners))


def experts_kernel(
    n_dp, experts,
    x_own, all_g, table, wg_hbm, wu_hbm, wd_hbm,
    out_sum, grad_sum, x_out, g_out, acts_out, all_x,
    sib_o, sib_g, one_o, one_g, two_o, two_g, z_o, z_g,
    wg, wu, wd, xs, gs, gate_rows, acts, xin, gin, stage_o, stage_g, acc_o, acc_g, tmp_o, tmp_g,
    mine_o, mine_g,
    w_sem, in_sem, keep_sem, act_sem, own_sem, zx_send, zx_recv, ag_send, ag_recv,
    sib_send, sib_recv, one_send, one_recv, two_send, two_recv, z_send, z_recv, tmp_sem,
):
    n_dev, rows, wide = all_x.shape
    local, width, hid = wg.shape
    cap = xs.shape[2]
    group = 2 * n_dp
    layers = n_dev // group
    m = group * cap
    slots = xin.shape[0]
    half = width // 2
    here = Place(n_dp)
    rank, core, x, y = here.rank, here.core, here.x, here.y
    first = here.ep * local

    def remote(src, dst, send, recv, device):
        return pltpu.make_async_remote_copy(
            src_ref=src, dst_ref=dst, send_sem=send, recv_sem=recv,
            device_id=device, device_id_type=MESH,
        )

    def layer_of(i):
        return flip(here.layer, i, layers)

    def weights():
        return [
            pltpu.make_async_copy(s, d, w_sem.at[i])
            for i, (s, d) in enumerate(((wg_hbm, wg), (wu_hbm, wu), (wd_hbm, wd)))
        ]

    def z_copy(i):
        me = here.layer * group + rank
        return remote(
            x_own, all_x.at[me], zx_send.at[i], zx_recv.at[i], here.at_layer(layer_of(i))
        )

    def own_copy():
        return pltpu.make_async_copy(x_own, all_x.at[here.layer * group + rank], own_sem.at[0])

    over_x_rank = y * n_dp + (1 - x) * 2 + core
    over_y_rank = (1 - y) * n_dp + x * 2 + core
    across_rank = (1 - y) * n_dp + (1 - x) * 2 + core
    first_half, second_half = pl.ds(0, half), pl.ds(half, wide - half)

    def gather_copy(i, kind):
        base = layer_of(i) * group
        which, cols, device = {
            0: (rank, first_half, here.over_x),
            1: (rank, second_half, here.over_x),
            2: (rank, first_half, here.over_y),
            3: (rank, second_half, here.over_y),
            4: (over_x_rank, first_half, here.over_y),
            5: (over_y_rank, second_half, here.over_x),
            6: (rank, pl.ds(0, wide), here.sibling),
            7: (over_x_rank, pl.ds(0, wide), here.sibling),
            8: (over_y_rank, pl.ds(0, wide), here.sibling),
            9: (across_rank, pl.ds(0, wide), here.sibling),
        }[kind]
        ref = all_x.at[base + which, :, cols]
        return remote(ref, ref, ag_send.at[i, kind], ag_recv.at[i, kind], device)

    def gather_a(i):
        if isinstance(i, int) and i == 0:
            own_copy().wait()
        else:
            z_copy(i).wait_recv()
        for kind in (0, 3, 1, 2, 6):
            gather_copy(i, kind).start()

    def gather_b(i):
        for got, then in ((0, 4), (3, 5), (1, 7), (2, 8)):
            gather_copy(i, got).wait_recv()
            gather_copy(i, then).start()

    def gather_c(i):
        gather_copy(i, 4).wait_recv()
        gather_copy(i, 5).wait_recv()
        gather_copy(i, 9).start()

    def gather_d(i):
        for kind in (6, 7, 8, 9):
            gather_copy(i, kind).wait_recv()

    def sib_copy(i, q, slot):
        return (
            remote(stage_o.at[slot], sib_o.at[i, q], sib_send.at[0, slot], sib_recv.at[0, i, q],
                   here.sibling),
            remote(stage_g.at[slot], sib_g.at[i, q], sib_send.at[1, slot], sib_recv.at[1, i, q],
                   here.sibling),
        )

    def one_copy(i, j):
        return (
            remote(acc_o.at[j * 2 + 1 - x], one_o.at[i, j], one_send.at[0, j],
                   one_recv.at[0, i, j], here.over_x),
            remote(acc_g.at[(1 - y) * 2 + j], one_g.at[i, j], one_send.at[1, j],
                   one_recv.at[1, i, j], here.over_y),
        )

    def two_copy(i):
        return (
            remote(acc_o.at[(1 - y) * 2 + x], two_o.at[i], two_send.at[0], two_recv.at[0, i],
                   here.over_y),
            remote(acc_g.at[y * 2 + 1 - x], two_g.at[i], two_send.at[1], two_recv.at[1, i],
                   here.over_x),
        )

    def out_copy(i):
        device = here.at_layer(layer_of(i))
        own = y * 2 + x
        return (
            remote(acc_o.at[own], z_o.at[i], z_send.at[0], z_recv.at[0, i], device),
            remote(acc_g.at[own], z_g.at[i], z_send.at[1], z_recv.at[1, i], device),
        )

    def fetch(src_o, src_g, slot):
        return (
            pltpu.make_async_copy(src_o, tmp_o.at[slot], tmp_sem.at[0, slot]),
            pltpu.make_async_copy(src_g, tmp_g.at[slot], tmp_sem.at[1, slot]),
        )

    def start(copies):
        for copy in copies:
            copy.start()

    def finish(copies):
        for copy in copies:
            copy.wait()

    def add(dst, q, tmp, slot):
        total = dst[q].astype(F32) + tmp[slot].astype(F32)
        dst[q] = total.astype(BF)

    def sum_sibling(i):
        def bring(q, slot):
            for copy in sib_copy(i, q, 0):
                copy.wait_recv()
            start(fetch(sib_o.at[i, q], sib_g.at[i, q], slot))

        bring(0, 0)
        for q in range(4):
            if q < 3:
                bring(q + 1, (q + 1) % 2)
            finish(fetch(sib_o.at[i, q], sib_g.at[i, q], q % 2))
            add(acc_o, q, tmp_o, q % 2)
            add(acc_g, q, tmp_g, q % 2)
        for j in range(2):
            start(one_copy(i, j))

    def sum_one(i):
        def bring(j):
            for copy in one_copy(i, j):
                copy.wait_recv()
            start(fetch(one_o.at[i, j], one_g.at[i, j], j))

        bring(0)
        bring(1)
        for j in range(2):
            finish(fetch(one_o.at[i, j], one_g.at[i, j], j))
            add(acc_o, j * 2 + x, tmp_o, j)
            add(acc_g, y * 2 + j, tmp_g, j)
        start(two_copy(i))

    def sum_two(i):
        for copy in two_copy(i):
            copy.wait_recv()
        start(fetch(two_o.at[i], two_g.at[i], 0))
        finish(fetch(two_o.at[i], two_g.at[i], 0))
        own = y * 2 + x
        add(acc_o, own, tmp_o, 0)
        add(acc_g, own, tmp_g, 0)
        for j in range(2):
            for copy in one_copy(i, j):
                copy.wait_send()
        for copy in two_copy(i):
            copy.wait_send()

        @pl.when(i == 0)
        def _():
            mine_o[...] = acc_o[own]
            mine_g[...] = acc_g[own]

        @pl.when(i > 0)
        def _():
            start(out_copy(i))

    start(weights())
    greet([here.over_x, here.over_y, here.sibling]
          + [here.at_layer(layer_of(i)) for i in range(1, layers)])
    own_copy().start()
    for i in range(1, layers):
        z_copy(i).start()
    gather_a(0)
    gather_b(0)
    gather_c(0)
    gather_a(1)

    def chunk(i, carry):
        base = layer_of(i) * group

        @pl.when(i > 0)
        def _():
            sum_sibling(i - 1)

        gather_d(i)

        def load(b, slot):
            return (
                pltpu.make_async_copy(all_x.at[base + b], xin.at[slot], in_sem.at[0, slot]),
                pltpu.make_async_copy(
                    all_g.at[base + b, :, pl.ds(0, width)], gin.at[slot], in_sem.at[1, slot]
                ),
            )

        for b in range(slots - 1):
            start(load(b, b))

        def bring(b, c):
            slot = lax.rem(b, slots)
            finish(load(b, slot))

            @pl.when(b + slots - 1 < group)
            def _():
                start(load(b + slots - 1, lax.rem(b + slots - 1, slots)))

            hot = table[base + b]
            for src, dst in ((xin, xs), (gin, gs)):
                for n in range(0, width, STEP):
                    got = dot(hot, src[slot, :, n : n + STEP]).astype(BF)
                    dst[:, b, :, n : n + STEP] = got.reshape(local, cap, STEP)
            gates = dot(hot, xin[slot, :, width:wide])
            lanes = lax.broadcasted_iota(jnp.int32, gates.shape, 1) % experts
            expert = lax.broadcasted_iota(jnp.int32, gates.shape, 0) // cap + first
            gates = jnp.sum(jnp.where(lanes == expert, gates, 0.0), axis=1, keepdims=True)
            gate_rows[:, b] = jnp.broadcast_to(gates, (local * cap, 128)).reshape(local, cap, 128)
            return c

        lax.fori_loop(0, group, bring, 0)

        def keep(e):
            return (
                pltpu.make_async_copy(xs.at[e], x_out.at[e, pl.ds(base, group)], keep_sem.at[0, e]),
                pltpu.make_async_copy(gs.at[e], g_out.at[e, pl.ds(base, group)], keep_sem.at[1, e]),
            )

        def keep_acts(e, slot):
            return pltpu.make_async_copy(
                acts.at[slot], acts_out.at[:, e, pl.ds(base * cap, m)], act_sem.at[slot]
            )

        lax.fori_loop(0, local, lambda e, c: (start(keep(e)), c)[1], 0)

        @pl.when(i == 0)
        def _():
            finish(weights())

        def expert(e, c):
            def hook(number, when, action):
                @pl.when(jnp.logical_and(e == number * local // HOOKS, when))
                def _():
                    action()

            hook(1, i + 2 < layers, lambda: gather_a(i + 2))
            hook(2, i + 1 < layers, lambda: gather_b(i + 1))
            hook(4, i + 1 < layers, lambda: gather_c(i + 1))
            hook(5, i > 0, lambda: sum_one(i - 1))
            hook(7, i > 0, lambda: sum_two(i - 1))
            slot = lax.rem(e, 2)

            @pl.when(jnp.logical_or(i > 0, e >= 2))
            def _():
                keep_acts(e, slot).wait()

            xe = xs[e].reshape(m, width)
            ge = gs[e].reshape(m, width)
            gate_part = dot(xe, wg[e])
            up_part = dot(xe, wu[e])
            raw = dot_t(ge, wd[e])
            gate = gate_rows[e].reshape(m, 128)[:, :1]
            sig = 1.0 / (1.0 + jnp.exp(-gate_part))
            silu = gate_part * sig
            hidden = silu * up_part
            own = jnp.sum(hidden * raw, axis=1, keepdims=True)
            lanes = lax.broadcasted_iota(jnp.int32, (m, 128), 1)
            grad_hidden = raw * gate
            hg = (hidden * gate).astype(BF)
            dg = (grad_hidden * up_part * sig * (1.0 + gate_part * (1.0 - sig))).astype(BF)
            du = (grad_hidden * silu).astype(BF)
            gate_rows[e] = jnp.where(lanes == first + e, own, 0.0).reshape(group, cap, 128)
            acts[slot, 0] = hg
            acts[slot, 1] = dg
            acts[slot, 2] = du
            keep_acts(e, slot).start()
            finish(keep(e))
            for n in range(0, width, STEP):
                out = dot(hg, wd[e, :, n : n + STEP]).astype(BF)
                gs[e, :, :, n : n + STEP] = out.reshape(group, cap, STEP)
                back = dot_t(dg, wg[e, n : n + STEP, :]) + dot_t(du, wu[e, n : n + STEP, :])
                xs[e, :, :, n : n + STEP] = back.astype(BF).reshape(group, cap, STEP)
            return c

        lax.fori_loop(0, local, expert, 0)

        def combine(b, put_o, put_g):
            hot = table[base + b]
            for n in range(0, width, STEP):
                got = gs[:, b, :, n : n + STEP].reshape(local * cap, STEP)
                put_o(n, STEP, tdot(hot, got).astype(BF))
                got = xs[:, b, :, n : n + STEP].reshape(local * cap, STEP)
                put_g(n, STEP, tdot(hot, got).astype(BF))
            got = gate_rows[:, b].reshape(local * cap, 128).astype(BF)
            put_g(width, 128, tdot(hot, got).astype(BF))

        def give(q, c):
            slot = lax.rem(q, 2)

            @pl.when(jnp.logical_or(i > 0, q >= 2))
            def _():
                for copy in sib_copy(i, q, slot):
                    copy.wait_send()

            def put_o(n, size, value):
                stage_o[slot, :, pl.ds(n, size)] = value

            def put_g(n, size, value):
                stage_g[slot, :, pl.ds(n, size)] = value

            combine(q * 2 + 1 - core, put_o, put_g)
            start(sib_copy(i, q, slot))
            return c

        lax.fori_loop(0, 4, give, 0)

        @pl.when(i > 1)
        def _():
            for copy in out_copy(i - 1):
                copy.wait_send()

        def hold(q, c):
            def put_o(n, size, value):
                acc_o[q, :, pl.ds(n, size)] = value

            def put_g(n, size, value):
                acc_g[q, :, pl.ds(n, size)] = value

            combine(q * 2 + core, put_o, put_g)
            return c

        lax.fori_loop(0, 4, hold, 0)
        return carry

    lax.fori_loop(0, layers, chunk, 0)
    last = layers - 1
    sum_sibling(last)
    sum_one(last)
    sum_two(last)
    out_sum[...] = mine_o[...].astype(F32)
    grad_sum[...] = mine_g[...].astype(F32)

    def last_sum(i, c):
        for copy in out_copy(i):
            copy.wait_recv()
        start(fetch(z_o.at[i], z_g.at[i], 0))
        finish(fetch(z_o.at[i], z_g.at[i], 0))
        out_sum[...] += tmp_o[0].astype(F32)
        grad_sum[...] += tmp_g[0].astype(F32)
        return c

    lax.fori_loop(1, layers, last_sum, 0)
    for copy in out_copy(last):
        copy.wait_send()
    for slot in range(2):
        for copy in sib_copy(last, slot, slot):
            copy.wait_send()
        pltpu.make_async_copy(
            acts.at[slot], acts_out.at[:, 0, pl.ds(0, m)], act_sem.at[slot]
        ).wait()

    def drain(i, c):
        for kind in range(10):
            gather_copy(i, kind).wait_send()
        return c

    lax.fori_loop(0, layers, drain, 0)
    lax.fori_loop(1, layers, lambda i, c: (z_copy(i).wait_send(), c)[1], 0)


def run_experts(x_own, all_g, table, wg, wu, wd, n_dp, experts, cap):
    rows, wide = x_own.shape
    n_dev = all_g.shape[0]
    local, width, hid = wg.shape
    group = 2 * n_dp
    layers = n_dev // group
    m = group * cap
    wide_g = width + 128
    slots = 3
    dma = pltpu.SemaphoreType.DMA
    shape = jax.ShapeDtypeStruct
    slot_rows = shape((local, n_dev, cap, width), BF)
    flops = 12 * n_dev * cap * local * width * hid
    result = pl.pallas_call(
        functools.partial(experts_kernel, n_dp, experts),
        out_shape=(
            shape((rows, width), F32), shape((rows, wide_g), F32),
            slot_rows, slot_rows,
            shape((3, local, n_dev * cap, hid), BF),
            shape((n_dev, rows, wide), BF),
            shape((layers, 4, rows, width), BF), shape((layers, 4, rows, wide_g), BF),
            shape((layers, 2, rows, width), BF), shape((layers, 2, rows, wide_g), BF),
            shape((layers, rows, width), BF), shape((layers, rows, wide_g), BF),
            shape((layers, rows, width), BF), shape((layers, rows, wide_g), BF),
        ),
        in_specs=[ANY, ANY, VMEM, ANY, ANY, ANY],
        out_specs=(VMEM, VMEM) + (ANY,) * 12,
        scratch_shapes=[
            pltpu.VMEM(wg.shape, BF), pltpu.VMEM(wu.shape, BF), pltpu.VMEM(wd.shape, BF),
            pltpu.VMEM((local, group, cap, width), BF),
            pltpu.VMEM((local, group, cap, width), BF),
            pltpu.VMEM((local, group, cap, 128), F32),
            pltpu.VMEM((2, 3, m, hid), BF),
            pltpu.VMEM((slots, rows, wide), BF),
            pltpu.VMEM((slots, rows, width), BF),
            pltpu.VMEM((2, rows, width), BF), pltpu.VMEM((2, rows, wide_g), BF),
            pltpu.VMEM((4, rows, width), BF), pltpu.VMEM((4, rows, wide_g), BF),
            pltpu.VMEM((2, rows, width), BF), pltpu.VMEM((2, rows, wide_g), BF),
            pltpu.VMEM((rows, width), BF), pltpu.VMEM((rows, wide_g), BF),
            dma((3,)), dma((2, slots)), dma((2, local)), dma((2,)), dma((1,)),
            dma((layers,)), dma((layers,)), dma((layers, 10)), dma((layers, 10)),
            dma((2, 2)), dma((2, layers, 4)), dma((2, 2)), dma((2, layers, 2)),
            dma((2,)), dma((2, layers)), dma((2,)), dma((2, layers)), dma((2, 2)),
        ],
        compiler_params=pltpu.CompilerParams(
            collective_id=1, has_side_effects=True, vmem_limit_bytes=64 * 2**20
        ),
        cost_estimate=pl.CostEstimate(flops=flops, bytes_accessed=200 * 2**20, transcendentals=0),
    )(x_own, all_g, table, wg, wu, wd)
    return result[:5]


def weights_kernel(x, g, acts, grad_g, grad_u, grad_d):
    first = pl.program_id(1) == 0
    xe, ge = x[0], g[0]

    def put(ref, n, size, value, axis):
        at = (0, pl.ds(n, size), slice(None)) if axis == 0 else (0, slice(None), pl.ds(n, size))

        @pl.when(first)
        def _():
            ref[at] = value

        @pl.when(jnp.logical_not(first))
        def _():
            ref[at] += value

    hg, dg, du = acts[0, 0], acts[1, 0], acts[2, 0]
    for n in range(0, xe.shape[1], STEP):
        part = xe[:, n : n + STEP]
        put(grad_g, n, STEP, tdot(part, dg), 0)
        put(grad_u, n, STEP, tdot(part, du), 0)
        put(grad_d, n, STEP, tdot(hg, ge[:, n : n + STEP]), 1)


def run_weights(x_slots, g_slots, acts):
    local, n_dev, cap, width = x_slots.shape
    hid = acts.shape[-1]
    total = n_dev * cap
    tile = min(1024, total)
    x_slots = x_slots.reshape(local, total, width)
    g_slots = g_slots.reshape(local, total, width)
    row = pl.BlockSpec((1, tile, width), lambda e, k: (e, k, 0))
    wide = pl.BlockSpec((1, width, hid), lambda e, k: (e, 0, 0))
    deep = pl.BlockSpec((1, hid, width), lambda e, k: (e, 0, 0))
    return pl.pallas_call(
        weights_kernel,
        grid=(local, total // tile),
        out_shape=(
            jax.ShapeDtypeStruct((local, width, hid), F32),
            jax.ShapeDtypeStruct((local, width, hid), F32),
            jax.ShapeDtypeStruct((local, hid, width), F32),
        ),
        in_specs=[row, row, pl.BlockSpec((3, 1, tile, hid), lambda e, k: (0, e, k, 0))],
        out_specs=(wide, wide, deep),
        compiler_params=pltpu.CompilerParams(vmem_limit_bytes=60 * 2**20),
        cost_estimate=pl.CostEstimate(
            flops=6 * local * total * width * hid, bytes_accessed=130 * 2**20, transcendentals=0
        ),
    )(x_slots, g_slots, acts)


def peer(here, rank):
    return (here.layer * 2 + rank // here.n_dp, rank % here.n_dp)


def others(here, group):
    return [lax.rem(here.rank + k, group) for k in range(1, group)]


def remote(src, dst, send, recv, device):
    return pltpu.make_async_remote_copy(
        src_ref=src, dst_ref=dst, send_sem=send, recv_sem=recv,
        device_id=device, device_id_type=MESH,
    )


class LayerGather:
    def __init__(self, here, own, buf, own_sem, send, recv):
        self.here, self.own, self.buf = here, own, buf
        self.own_sem, self.send, self.recv = own_sem, send, recv

    def copy(self, kind):
        here, buf = self.here, self.buf
        wide = buf.shape[-1]
        half = wide // 256 * 128
        low, high, full = pl.ds(0, half), pl.ds(half, wide - half), pl.ds(0, wide)
        n_dp, x, y, core = here.n_dp, here.x, here.y, here.core
        over_x = y * n_dp + (1 - x) * 2 + core
        over_y = (1 - y) * n_dp + x * 2 + core
        across = (1 - y) * n_dp + (1 - x) * 2 + core
        which, cols, device = {
            0: (here.rank, low, here.over_x),
            1: (here.rank, high, here.over_x),
            2: (here.rank, low, here.over_y),
            3: (here.rank, high, here.over_y),
            4: (over_x, low, here.over_y),
            5: (over_y, high, here.over_x),
            6: (here.rank, full, here.sibling),
            7: (over_x, full, here.sibling),
            8: (over_y, full, here.sibling),
            9: (across, full, here.sibling),
        }[kind]
        dst = buf.at[which, :, cols]
        src = self.own.at[:, cols] if kind in (0, 1, 2, 3, 6) else dst
        return remote(src, dst, self.send.at[kind], self.recv.at[kind], device)

    def keep(self):
        return pltpu.make_async_copy(self.own, self.buf.at[self.here.rank], self.own_sem.at[0])

    def begin(self):
        self.keep().start()
        for kind in (0, 3, 1, 2, 6):
            self.copy(kind).start()

    def forward(self):
        for got, then in ((0, 4), (3, 5), (1, 7), (2, 8)):
            self.copy(got).wait_recv()
            self.copy(then).start()

    def across(self):
        self.copy(4).wait_recv()
        self.copy(5).wait_recv()
        self.copy(9).start()

    def end(self):
        for kind in (6, 7, 8, 9):
            self.copy(kind).wait_recv()
        for kind in range(10):
            self.copy(kind).wait_send()
        self.keep().wait()


class LayerSum:
    def __init__(self, here, part, acc, sib, one, two, load, send, recv):
        self.here, self.part, self.acc, self.sib = here, part, acc, sib
        self.one, self.two, self.load_sem, self.send, self.recv = one, two, load, send, recv
        wide = acc.shape[-1]
        half = wide // 256 * 128
        self.cols = (pl.ds(0, half), pl.ds(half, wide - half))

    def load(self, q):
        return pltpu.make_async_copy(
            self.part.at[q * 2 + self.here.core], self.acc.at[q], self.load_sem.at[q]
        )

    def copy(self, kind):
        here, acc = self.here, self.acc
        x, y = here.x, here.y
        low, high = self.cols
        if kind < 4:
            src, dst = self.part.at[kind * 2 + 1 - here.core], self.sib.at[kind]
            device = here.sibling
        elif kind < 6:
            j = kind - 4
            src, dst, device = acc.at[j * 2 + 1 - x, :, low], self.one.at[j, :, low], here.over_x
        elif kind < 8:
            j = kind - 6
            src, dst = acc.at[(1 - y) * 2 + j, :, high], self.one.at[j, :, high]
            device = here.over_y
        elif kind == 8:
            src, dst, device = acc.at[(1 - y) * 2 + x, :, low], self.two.at[:, low], here.over_y
        else:
            src, dst, device = acc.at[y * 2 + 1 - x, :, high], self.two.at[:, high], here.over_x
        return remote(src, dst, self.send.at[kind], self.recv.at[kind], device)

    def add(self, q, cols, got):
        total = self.acc[q, :, cols].astype(F32) + got.astype(F32)
        self.acc[q, :, cols] = total.astype(BF)

    def begin(self):
        for q in range(4):
            self.copy(q).start()
            self.load(q).start()

    def first(self):
        for q in range(4):
            self.load(q).wait()
            self.copy(q).wait_recv()
            for cols in self.cols:
                self.add(q, cols, self.sib[q, :, cols])
        for kind in (4, 5, 6, 7):
            self.copy(kind).start()

    def second(self):
        x, y = self.here.x, self.here.y
        low, high = self.cols
        for j in range(2):
            self.copy(4 + j).wait_recv()
            self.add(j * 2 + x, low, self.one[j, :, low])
            self.copy(6 + j).wait_recv()
            self.add(y * 2 + j, high, self.one[j, :, high])
        self.copy(8).start()
        self.copy(9).start()

    def third(self, out):
        own = self.here.y * 2 + self.here.x
        for kind, cols in zip((8, 9), self.cols):
            self.copy(kind).wait_recv()
            out[:, cols] = self.acc[own, :, cols].astype(F32) + self.two[:, cols].astype(F32)
        for kind in range(10):
            self.copy(kind).wait_send()

    @staticmethod
    def scratch(rows, wide):
        return [
            pltpu.VMEM((4, rows, wide), BF), pltpu.VMEM((4, rows, wide), BF),
            pltpu.VMEM((2, rows, wide), BF), pltpu.VMEM((rows, wide), BF),
            pltpu.SemaphoreType.DMA((4,)),
            pltpu.SemaphoreType.DMA((10,)), pltpu.SemaphoreType.DMA((10,)),
        ]


def comm_params(number):
    return pltpu.CompilerParams(
        collective_id=number, has_side_effects=True, vmem_limit_bytes=48 * 2**20
    )


def gather_kernel(n_dp, own, buf, own_sem, send, recv):
    here = Place(n_dp)
    greet([here.over_x, here.over_y, here.sibling])
    job = LayerGather(here, own, buf, own_sem, send, recv)
    job.begin()
    job.forward()
    job.across()
    job.end()


def layer_gather(value, n_dp):
    rows, wide = value.shape
    dma = pltpu.SemaphoreType.DMA
    return pl.pallas_call(
        functools.partial(gather_kernel, n_dp),
        out_shape=jax.ShapeDtypeStruct((2 * n_dp, rows, wide), value.dtype),
        in_specs=[ANY],
        out_specs=ANY,
        scratch_shapes=[dma((1,)), dma((10,)), dma((10,))],
        compiler_params=comm_params(2),
    )(value)


def sum_kernel(n_dp, part, out, *scratch):
    here = Place(n_dp)
    greet([here.over_x, here.over_y, here.sibling])
    job = LayerSum(here, part, *scratch)
    job.begin()
    job.first()
    job.second()
    job.third(out)


def layer_sum(part, n_dp):
    group, rows, wide = part.shape
    return pl.pallas_call(
        functools.partial(sum_kernel, n_dp),
        out_shape=jax.ShapeDtypeStruct((rows, wide), F32),
        in_specs=[ANY],
        out_specs=VMEM,
        scratch_shapes=LayerSum.scratch(rows, wide),
        compiler_params=comm_params(3),
    )(part)


def stats_kernel(n_dp, value, out, land, send, recv):
    here = Place(n_dp)
    group = 2 * n_dp
    ranks = others(here, group)
    greet([peer(here, rank) for rank in ranks])

    def copy(k):
        return remote(
            value, land.at[k], send.at[k], recv.at[k], peer(here, ranks[k])
        )

    for k in range(group - 1):
        copy(k).start()
    total = value[...]
    for k in range(group - 1):
        copy(k).wait_recv()
        total += land[k]
    out[...] = total
    for k in range(group - 1):
        copy(k).wait_send()


def layer_stats(value, n_dp):
    dma = pltpu.SemaphoreType.DMA
    peers = 2 * n_dp - 1
    flat = value.reshape(-1, 128)
    out = pl.pallas_call(
        functools.partial(stats_kernel, n_dp),
        out_shape=jax.ShapeDtypeStruct(flat.shape, F32),
        in_specs=[VMEM],
        out_specs=VMEM,
        scratch_shapes=[pltpu.VMEM((peers,) + flat.shape, F32), dma((peers,)), dma((peers,))],
        compiler_params=comm_params(4),
    )(flat)
    return out.reshape(value.shape)


def front_kernel(
    n_dp, layers, x_own, w_q, w_k, w_v, w_o, small,
    x_all, qkv, wo, small_all, wo_col,
    own_sem, x_send, x_recv, a_keep, a_send, a_recv, up_send, up_recv, down_send, down_recv,
    o_keep, o_send, o_recv, s_send, s_recv, t_send, t_recv,
):
    here = Place(n_dp)
    group = 2 * n_dp
    layer, rank = here.layer, here.rank
    own = w_q.shape[0]
    cols = qkv.shape[-1]
    ranks = others(here, group)
    away = [flip(layer, i, layers) for i in range(1, layers)]
    greet([peer(here, r) for r in ranks] + [here.at_layer(z) for z in away])
    gather = LayerGather(here, x_own, x_all, own_sem, x_send, x_recv)
    weights = (w_q, w_k, w_v)

    def rows_at(index):
        return pl.ds(pl.multiple_of(index * own, own), own)

    def block_cols(index):
        return pl.ds(pl.multiple_of(index * cols, cols), cols)

    def swap(w, k):
        return remote(
            weights[w].at[:, block_cols(ranks[k])], qkv.at[w, layer, rows_at(rank)],
            a_send.at[w, k], a_recv.at[w, k], peer(here, ranks[k]),
        )

    def swap_own(w):
        return pltpu.make_async_copy(
            weights[w].at[:, block_cols(rank)], qkv.at[w, layer, rows_at(rank)], a_keep.at[w]
        )

    def small_out(i):
        ref = small_all.at[layer, rank]
        return remote(small, ref, s_send.at[i], s_recv.at[i], here.at_layer(away[i]))

    def small_keep():
        return pltpu.make_async_copy(small, small_all.at[layer, rank], a_keep.at[3])

    def small_share(k):
        ref = small_all.at[:, rank]
        return remote(ref, ref, t_send.at[k], t_recv.at[k], peer(here, ranks[k]))

    def o_own():
        return pltpu.make_async_copy(w_o, wo_col.at[layer], a_keep.at[4])

    for w in range(3):
        swap_own(w).start()
        for k in range(group - 1):
            swap(w, k).start()
    o_own().start()
    small_keep().start()
    for i in range(layers - 1):
        small_out(i).start()
    gather.begin()
    for w in range(3):
        swap_own(w).wait()
        for k in range(group - 1):
            swap(w, k).wait_recv()
    o_own().wait()

    def chain(which, up, s):
        block = layer - s if up else layer + s
        ref = qkv.at[:, block] if which == 0 else wo_col.at[block]
        device = here.at_layer(layer + 1 if up else layer - 1)
        sems = (up_send, up_recv) if up else (down_send, down_recv)
        return remote(ref, ref, sems[0].at[which, s], sems[1].at[which, s], device)

    def step(which, s, wait):
        for up in (True, False):
            leaves = (
                jnp.logical_and(layer + 1 < layers, layer - s >= 0) if up
                else jnp.logical_and(layer >= 1, layer + s < layers)
            )
            comes = layer - 1 - s >= 0 if up else layer + 1 + s < layers
            if wait:
                @pl.when(comes)
                def _():
                    chain(which, up, s).wait_recv()
            else:
                @pl.when(leaves)
                def _():
                    chain(which, up, s).start()

    step(0, 0, False)
    gather.forward()
    step(1, 0, False)
    gather.across()
    small_keep().wait()
    for i in range(layers - 1):
        small_out(i).wait_recv()
    for k in range(group - 1):
        small_share(k).start()
    for s in range(layers - 1):
        step(0, s, True)
        if s + 1 < layers - 1:
            step(0, s + 1, False)
        step(1, s, True)
        if s + 1 < layers - 1:
            step(1, s + 1, False)

    def share(z):
        number = z * group + rank
        target, index = number // layers, number % layers

        def far():
            return remote(
                wo_col.at[z], wo.at[index], o_send.at[z], o_recv.at[index], peer(here, target)
            )

        def near():
            return pltpu.make_async_copy(wo_col.at[z], wo.at[index], o_keep.at[index])

        return target, far, near

    def source(index):
        number = rank * layers + index
        return number % group

    for z in range(layers):
        target, far, near = share(z)

        @pl.when(target != rank)
        def _():
            far().start()

        @pl.when(target == rank)
        def _():
            near().start()

    for index in range(layers):
        @pl.when(source(index) != rank)
        def _():
            remote(
                wo_col.at[0], wo.at[index], o_send.at[0], o_recv.at[index], here.sibling
            ).wait_recv()

        @pl.when(source(index) == rank)
        def _():
            pltpu.make_async_copy(wo_col.at[0], wo.at[index], o_keep.at[index]).wait()

    gather.end()
    for k in range(group - 1):
        small_share(k).wait_recv()
    for w in range(3):
        for k in range(group - 1):
            swap(w, k).wait_send()
    for i in range(layers - 1):
        small_out(i).wait_send()
    for k in range(group - 1):
        small_share(k).wait_send()
    for z in range(layers):
        target, far, near = share(z)

        @pl.when(target != rank)
        def _():
            far().wait_send()

    for which in range(2):
        for s in range(layers - 1):
            @pl.when(jnp.logical_and(layer + 1 < layers, layer - s >= 0))
            def _():
                chain(which, True, s).wait_send()

            @pl.when(jnp.logical_and(layer >= 1, layer + s < layers))
            def _():
                chain(which, False, s).wait_send()


def run_front(x_own, w_q, w_k, w_v, w_o, small, n_dp, n_dev):
    rows, width = x_own.shape
    own = w_q.shape[0]
    group = 2 * n_dp
    layers = n_dev // group
    cols = width // group
    dma = pltpu.SemaphoreType.DMA
    shape = jax.ShapeDtypeStruct
    chain = dma((2, layers))
    result = pl.pallas_call(
        functools.partial(front_kernel, n_dp, layers),
        out_shape=(
            shape((group, rows, width), BF),
            shape((3, layers, group * own, cols), BF),
            shape((layers, own, width), BF),
            shape((layers, group) + small.shape, BF),
            shape((layers, own, width), BF),
        ),
        in_specs=[ANY] * 6,
        out_specs=(ANY,) * 5,
        scratch_shapes=[
            dma((1,)), dma((10,)), dma((10,)), dma((5,)),
            dma((3, group - 1)), dma((3, group - 1)), chain, chain, chain, chain,
            dma((layers,)), dma((layers,)), dma((layers,)),
            dma((layers,)), dma((layers,)), dma((group,)), dma((group,)),
        ],
        compiler_params=comm_params(5),
    )(x_own, w_q, w_k, w_v, w_o, small)
    x_all, qkv, wo, small_all, _ = result
    return (
        x_all.reshape(group * rows, width), qkv.reshape(3, width, cols),
        wo.reshape(cols, width), small_all.reshape(width, -1),
    )


def back_kernel(
    n_dp, layers, part, gw, go, small,
    out, grad_w, grad_o, small_out,
    acc, sib, one, two, load_sem, n_send, n_recv,
    acc_w, acc_o, up_w, up_o, down_w, down_o, swapped, s_own, s_land, s_sum, s_far,
    w_load, o_keep, o_send, o_recv, up_send, up_recv, down_send, down_recv,
    a_keep, a_send, a_recv, s_keep, s_send, s_recv, t_send, t_recv,
):
    here = Place(n_dp)
    group = 2 * n_dp
    layer, rank = here.layer, here.rank
    own = grad_w.shape[1]
    cols = gw.shape[-1]
    ranks = others(here, group)
    away = [flip(layer, i, layers) for i in range(1, layers)]
    greet([peer(here, r) for r in ranks] + [here.at_layer(z) for z in away])
    job = LayerSum(here, part, acc, sib, one, two, load_sem, n_send, n_recv)

    def bring():
        return pltpu.make_async_copy(gw, acc_w, w_load.at[0])

    def share(i):
        number = rank * layers + i
        z, target = number // group, number % group

        def far():
            return remote(
                go.at[i], acc_o.at[z], o_send.at[i], o_recv.at[z], peer(here, target)
            )

        def near():
            return pltpu.make_async_copy(go.at[i], acc_o.at[z], o_keep.at[z])

        return target, far, near

    def small_swap(k):
        return remote(
            small.at[:, ranks[k]], s_land.at[k], s_send.at[k], s_recv.at[k], peer(here, ranks[k])
        )

    def small_keep():
        return pltpu.make_async_copy(small.at[:, rank], s_own, s_keep.at[0])

    bring().start()
    job.begin()
    for i in range(layers):
        target, far, near = share(i)

        @pl.when(target != rank)
        def _():
            far().start()

        @pl.when(target == rank)
        def _():
            near().start()
    small_keep().start()
    for k in range(group - 1):
        small_swap(k).start()

    def chain(which, up, z):
        acc_ref = (acc_w.at[:, z], acc_o.at[z])[which]
        land = ((up_w, up_o) if up else (down_w, down_o))[which].at[z]
        sems = (up_send, up_recv) if up else (down_send, down_recv)
        device = here.at_layer(layer + 1 if up else layer - 1)
        return remote(acc_ref, land, sems[0].at[which, z], sems[1].at[which, z], device)

    def take(which, up, z):
        chain(which, up, z).wait_recv()
        if which == 0:
            land = up_w if up else down_w
            for w in range(3):
                total = acc_w[w, z].astype(F32) + land[z, w].astype(F32)
                acc_w[w, z] = total.astype(BF)
        else:
            land = up_o if up else down_o
            acc_o[z] = (acc_o[z].astype(F32) + land[z].astype(F32)).astype(BF)

    def hop(which, d):
        @pl.when(layer + d < layers)
        def _():
            @pl.when(layer > 0)
            def _():
                take(which, True, layer + d)
            chain(which, True, layer + d).start()

        @pl.when(layer - d >= 0)
        def _():
            @pl.when(layer + 1 < layers)
            def _():
                take(which, False, layer - d)
            chain(which, False, layer - d).start()

    bring().wait()
    hop(0, layers - 1)
    job.first()
    for z in range(layers):
        source = (z * group + rank) // layers

        @pl.when(source != rank)
        def _():
            remote(
                go.at[0], acc_o.at[z], o_send.at[0], o_recv.at[z], here.sibling
            ).wait_recv()

        @pl.when(source == rank)
        def _():
            pltpu.make_async_copy(go.at[0], acc_o.at[z], o_keep.at[z]).wait()
    hop(1, layers - 1)
    small_keep().wait()
    total = s_own[...]
    for k in range(group - 1):
        small_swap(k).wait_recv()
        total += s_land[k]
    s_sum[...] = total

    def small_far(i):
        return remote(
            s_sum.at[away[i]], s_far.at[i], t_send.at[i], t_recv.at[i], here.at_layer(away[i])
        )

    for i in range(layers - 1):
        small_far(i).start()
    job.second()
    for d in range(layers - 2, 0, -1):
        hop(0, d)
        hop(1, d)
    job.third(out)
    total = s_sum[layer]
    for i in range(layers - 1):
        small_far(i).wait_recv()
        total += s_far[i]
    small_out[...] = total

    for which in range(2):
        @pl.when(layer > 0)
        def _():
            take(which, True, layer)

        @pl.when(layer + 1 < layers)
        def _():
            take(which, False, layer)

    def rows_at(index):
        return pl.ds(pl.multiple_of(index * own, own), own)

    def swap(k):
        return remote(
            acc_w.at[:, layer, rows_at(ranks[k])], swapped.at[rank],
            a_send.at[k], a_recv.at[k], peer(here, ranks[k]),
        )

    def swap_own():
        return pltpu.make_async_copy(
            acc_w.at[:, layer, rows_at(rank)], swapped.at[rank], a_keep.at[0]
        )

    swap_own().start()
    for k in range(group - 1):
        swap(k).start()
    grad_o[...] = acc_o[layer].astype(F32)
    swap_own().wait()
    for k in range(group - 1):
        swap(k).wait_recv()
    for r in range(group):
        for w in range(3):
            grad_w[w, :, r * cols : (r + 1) * cols] = swapped[r, w].astype(F32)

    for k in range(group - 1):
        swap(k).wait_send()
        small_swap(k).wait_send()
    for i in range(layers - 1):
        small_far(i).wait_send()
    for i in range(layers):
        target, far, near = share(i)

        @pl.when(target != rank)
        def _():
            far().wait_send()
    for which in range(2):
        for d in range(1, layers):
            @pl.when(layer + d < layers)
            def _():
                chain(which, True, layer + d).wait_send()

            @pl.when(layer - d >= 0)
            def _():
                chain(which, False, layer - d).wait_send()


def run_back(part, gw, go, small, n_dp):
    group, rows, width = part.shape
    cols = gw.shape[-1]
    layers = small.shape[0]
    own = small.shape[2]
    dma = pltpu.SemaphoreType.DMA
    shape = jax.ShapeDtypeStruct
    deep = pltpu.VMEM((layers, 3, group * own, cols), BF)
    flat = pltpu.VMEM((layers, own, width), BF)
    chain = dma((2, layers))
    tiny = small.shape[2:]
    return pl.pallas_call(
        functools.partial(back_kernel, n_dp, layers),
        out_shape=(
            shape((rows, width), F32), shape((3, own, width), F32),
            shape((own, width), F32), shape(tiny, F32),
        ),
        in_specs=[ANY] * 4,
        out_specs=(VMEM,) * 4,
        scratch_shapes=LayerSum.scratch(rows, width) + [
            pltpu.VMEM((3, layers, group * own, cols), BF), flat, deep, flat, deep, flat,
            pltpu.VMEM((group, 3, own, cols), BF),
            pltpu.VMEM((layers,) + tiny, F32), pltpu.VMEM((group - 1, layers) + tiny, F32),
            pltpu.VMEM((layers,) + tiny, F32), pltpu.VMEM((layers,) + tiny, F32),
            dma((1,)), dma((layers,)), dma((layers,)), dma((layers,)),
            chain, chain, chain, chain,
            dma((1,)), dma((group - 1,)), dma((group - 1,)),
            dma((1,)), dma((group - 1,)), dma((group - 1,)), dma((layers,)), dma((layers,)),
        ],
        compiler_params=comm_params(6),
    )(
        part, gw.reshape(3, layers, group * own, cols), go.reshape(layers, own, width), small
    )


def ein(spec, left, right):
    return jnp.einsum(spec, left, right, preferred_element_type=F32)


def inv_rms(value):
    return lax.rsqrt(jnp.mean(value * value, axis=-1, keepdims=True) + EPSILON)


def half_turn(value):
    half = value.shape[-1] // 2
    return jnp.concatenate([-value[..., half:], value[..., :half]], axis=-1)


def half_turn_back(value):
    half = value.shape[-1] // 2
    return jnp.concatenate([value[..., half:], -value[..., :half]], axis=-1)


def build(n_ep, n_dp):
    n_dev = n_ep * n_dp
    group = 2 * n_dp
    layers = n_dev // group

    def shards(
        layer_input, grad_out, attn_gain, w_q, w_k, w_v, q_gain, k_gain, w_o, ffn_gain,
        router, w_gate, w_up, w_down, routes,
    ):
        rows, width = layer_input.shape
        cols = width // group
        heads = cols // HEAD_DIM
        seqs = 2
        seq_len = rows * n_dp
        scale = HEAD_DIM ** (-0.5)
        own = width // n_dev
        rank = (lax.axis_index("ep") % 2) * n_dp + lax.axis_index("dp")
        local_experts = w_gate.shape[0]
        experts = router.shape[1]
        top = routes.shape[1]
        cap = 2 * rows * top // experts

        gains = jnp.stack([attn_gain, q_gain, k_gain, ffn_gain], axis=1)
        small = jnp.concatenate(
            [router, gains, jnp.zeros((own, 128 - experts - 4), BF)], axis=1
        )
        group_input, qkv, wo, small = run_front(
            layer_input, w_q, w_k, w_v, w_o, small, n_dp, n_dev
        )
        wq, wk, wv = qkv[0], qkv[1], qkv[2]
        full_router = small[:, :experts]
        full_attn_gain = small[:, experts].astype(F32)
        full_ffn_gain = small[:, experts + 3].astype(F32)
        head_gains = lax.dynamic_slice_in_dim(small, rank * cols, cols, 0).astype(F32)
        q_gain_own, k_gain_own = head_gains[:, experts + 1], head_gains[:, experts + 2]

        group_input = group_input.astype(F32)
        group_root = inv_rms(group_input)
        normed = (group_input * group_root * full_attn_gain).astype(BF)
        q_raw, k_raw = dot(normed, wq), dot(normed, wk)
        v_low = dot(normed, wv).astype(BF)
        squares = jnp.stack([jnp.sum(q_raw * q_raw, -1), jnp.sum(k_raw * k_raw, -1)])
        squares = layer_stats(squares, n_dp)
        roots = lax.rsqrt(squares / width + EPSILON)
        q_root, k_root = roots[0][:, None], roots[1][:, None]
        half_dim = HEAD_DIM // 2
        frequency = 10000.0 ** (-jnp.arange(half_dim, dtype=F32) * 2.0 / HEAD_DIM)
        angle = jnp.arange(seq_len, dtype=F32)[:, None] * frequency[None, :]
        cosine = jnp.concatenate([jnp.cos(angle)] * 2, axis=-1)[None, :, None, :]
        sine = jnp.concatenate([jnp.sin(angle)] * 2, axis=-1)[None, :, None, :]
        by_head = (seqs, seq_len, heads, HEAD_DIM)

        def rope(value):
            value = value.reshape(by_head)
            return (value * cosine + half_turn(value) * sine).astype(BF)

        def rope_back(value):
            return (value * cosine + half_turn_back(value * sine)).reshape(seqs * seq_len, cols)

        q_n, k_n = q_raw * q_root, k_raw * k_root
        q_rot, k_rot = rope(q_n * q_gain_own), rope(k_n * k_gain_own)
        values = v_low.reshape(by_head)
        causal = jnp.arange(seq_len)[:, None] >= jnp.arange(seq_len)[None, :]
        scores = jnp.where(causal, ein("bqhd,bkhd->bhqk", q_rot, k_rot) * scale, -1e30)
        probs = jax.nn.softmax(scores, axis=-1)
        probs_low = probs.astype(BF)
        mixed = ein("bhqk,bkhd->bqhd", probs_low, values).astype(BF).reshape(-1, cols)
        attn_out = layer_sum(dot(mixed, wo).astype(BF).reshape(group, rows, width), n_dp)
        residual = layer_input.astype(F32) + attn_out
        res_root = inv_rms(residual)
        res_n = residual * res_root
        normed2 = (res_n * full_ffn_gain).astype(BF)

        logits = dot(normed2, full_router)
        expert_ids = jnp.arange(experts, dtype=jnp.int32)
        picked = routes[:, :, None] == expert_ids
        chosen = jnp.sum(jnp.where(picked, logits[:, None, :], 0.0), axis=-1)
        gates = jax.nn.softmax(chosen, axis=-1)
        gates_dense = jnp.sum(jnp.where(picked, gates[:, :, None], 0.0), axis=1)
        hits = jnp.any(picked, axis=1)

        before = jnp.cumsum(hits.astype(jnp.int32), axis=0) - hits.astype(jnp.int32)
        place = jnp.where(hits, before, -1).astype(BF)
        sent = jnp.concatenate([grad_out, place, jnp.zeros((rows, 128 - experts), BF)], axis=1)
        all_g = lax.all_gather(sent, AXES, axis=0, tiled=True).reshape(n_dev, rows, -1)
        first = lax.axis_index("ep") * local_experts
        own_place = lax.dynamic_slice_in_dim(all_g, width + first, local_experts, 2)
        table = (
            own_place.transpose(0, 2, 1)[:, :, None, :]
            == jnp.arange(cap, dtype=jnp.int32).astype(BF)[None, None, :, None]
        )
        table = table.astype(BF).reshape(n_dev, local_experts * cap, rows)

        gates_high = gates_dense.astype(BF)
        gates_rest = (gates_dense - gates_high.astype(F32)).astype(BF)
        x_own = jnp.concatenate([normed2, gates_high, gates_rest], axis=1)
        expert_sum, grad_sum, x_slots, g_slots, acts = run_experts(
            x_own, all_g, table, w_gate, w_up, w_down, n_dp, experts, cap
        )
        grad_w_gate, grad_w_up, grad_w_down = run_weights(x_slots, g_slots, acts)
        output = (residual + expert_sum).astype(BF)
        gate_grads = jnp.where(hits, grad_sum[:, width : width + experts], 0.0)
        weighted = jnp.sum(gates_dense * gate_grads, axis=-1, keepdims=True)
        grad_logits = (gates_dense * (gate_grads - weighted)).astype(BF)

        grad_n2 = grad_sum[:, :width] + ein("te,de->td", grad_logits, full_router)
        grad_router = ein("td,te->de", normed2, grad_logits)
        grad_y = grad_out.astype(F32)
        grad_ffn_gain = jnp.sum(grad_n2 * res_n, axis=0)
        dn = grad_n2 * full_ffn_gain
        grad_residual = grad_y + res_root * (dn - res_n * jnp.mean(dn * res_n, -1, keepdims=True))

        gao = layer_gather(grad_residual.astype(BF), n_dp).reshape(group * rows, width)
        grad_wo = ein("td,te->de", mixed, gao)
        grad_mixed = ein("te,de->td", gao, wo).astype(BF).reshape(by_head)
        grad_values = ein("bhqk,bqhd->bkhd", probs_low, grad_mixed)
        grad_probs = ein("bqhd,bkhd->bhqk", grad_mixed, values)
        delta = jnp.sum(probs * grad_probs, axis=-1, keepdims=True)
        grad_scores = (probs * (grad_probs - delta)).astype(BF)
        grad_q_rot = ein("bhqk,bkhd->bqhd", grad_scores, k_rot) * scale
        grad_k_rot = ein("bhqk,bqhd->bkhd", grad_scores, q_rot) * scale
        gq, gk = rope_back(grad_q_rot), rope_back(grad_k_rot)
        grad_q_gain, grad_k_gain = jnp.sum(gq * q_n, axis=0), jnp.sum(gk * k_n, axis=0)
        gq, gk = gq * q_gain_own, gk * k_gain_own
        inner = jnp.stack([jnp.sum(gq * q_n, -1), jnp.sum(gk * k_n, -1)])
        inner = layer_stats(inner, n_dp) / width
        gq = (q_root * (gq - q_n * inner[0][:, None])).astype(BF)
        gk = (k_root * (gk - k_n * inner[1][:, None])).astype(BF)
        gv = grad_values.reshape(-1, cols).astype(BF)
        grad_normed = ein("te,de->td", gq, wq) + ein("te,de->td", gk, wk)
        grad_normed = grad_normed + ein("te,de->td", gv, wv)
        grad_attn_gain = jnp.sum(grad_normed * (group_input * group_root), axis=0)
        grad_qkv = jnp.stack([ein("td,te->de", normed, part) for part in (gq, gk, gv)]).astype(BF)

        def spread(part):
            return lax.dynamic_update_slice_in_dim(jnp.zeros((width,), F32), part, rank * cols, 0)

        gain_grads = jnp.stack(
            [grad_attn_gain, spread(grad_q_gain), spread(grad_k_gain), grad_ffn_gain], axis=1
        )
        small_grads = jnp.concatenate(
            [grad_router, gain_grads, jnp.zeros((width, 128 - experts - 4), F32)], axis=1
        )
        grad_normed, grad_qkv, grad_o, small_grads = run_back(
            grad_normed.astype(BF).reshape(group, rows, width), grad_qkv, grad_wo.astype(BF),
            small_grads.reshape(layers, group, own, 128), n_dp,
        )
        own_input = layer_input.astype(F32)
        in_root = inv_rms(own_input)
        in_n = own_input * in_root
        dn = grad_normed * full_attn_gain
        grad_input = grad_residual + in_root * (
            dn - in_n * jnp.mean(dn * in_n, -1, keepdims=True)
        )
        gain_grads = small_grads[:, experts : experts + 4]
        return (
            output, grad_input, gain_grads[:, 0], grad_qkv[0], grad_qkv[1], grad_qkv[2],
            gain_grads[:, 1], gain_grads[:, 2], grad_o, gain_grads[:, 3],
            small_grads[:, :experts], grad_w_gate, grad_w_up, grad_w_down,
        )

    return shards


def solution(mesh):
    row, vec = P(("ep", "dp"), None), P(("ep", "dp"))
    wide, deep = P("ep", None, "dp"), P("ep", "dp", None)
    in_specs = (
        row, row, vec, row, row, row, vec, vec, row, vec, row, wide, wide, deep, row,
    )
    out_specs = (
        row, row, vec, row, row, row, vec, vec, row, vec, row, wide, wide, deep,
    )
    shards = build(mesh.shape["ep"], mesh.shape["dp"])
    return jax.shard_map(shards, mesh=mesh, in_specs=in_specs, out_specs=out_specs, check_vma=False)
```

```python
import functools

import jax
import jax.numpy as jnp
from jax import lax
from jax.experimental import pallas as pl
from jax.experimental.pallas import tpu as pltpu
from jax.sharding import PartitionSpec as P

HEAD_DIM = 128
EPSILON = 1e-05
AXES = ("ep", "dp")
BF = jnp.bfloat16
F32 = jnp.float32
ANY = pl.BlockSpec(memory_space=pl.ANY)
VMEM = pl.BlockSpec(memory_space=pltpu.VMEM)
MESH = pl.DeviceIdType.MESH
STEP = 512
HOOKS = 8


def dot(left, right):
    return jnp.dot(left, right, preferred_element_type=F32)


def dot_t(left, right):
    return lax.dot_general(left, right, (((1,), (1,)), ((), ())), preferred_element_type=F32)


def tdot(left, right):
    return lax.dot_general(left, right, (((0,), (0,)), ((), ())), preferred_element_type=F32)


def flip(value, other, count):
    result, bit = 0, 1
    while bit < count:
        result = result + ((value // bit) % 2 + (other // bit) % 2) % 2 * bit
        bit *= 2
    return result


def nearby(z, i, count):
    both = jnp.minimum(z, count - 1 - z)
    first = 1 - 2 * (z % 2)
    paired = z + first * (1 - 2 * (i % 2)) * (i // 2 + 1)
    side = jnp.where(2 * z < count, 1, -1)
    single = z + side * (i - both + 1)
    return jnp.where(i == count - 1, z, jnp.where(i < 2 * both, paired, single))


class Place:
    def __init__(self, n_dp):
        ep, dp = lax.axis_index("ep"), lax.axis_index("dp")
        half = n_dp // 2
        self.n_dp, self.half = n_dp, half
        self.layer, self.y = ep // 2, ep % 2
        self.x, self.core = dp // 2, dp % 2
        self.rank = self.y * n_dp + dp
        self.ep, self.dp = ep, dp
        self.sibling = (ep, self.x * 2 + 1 - self.core)
        self.over_x = (ep, (1 - self.x) * 2 + self.core)
        self.over_y = (self.layer * 2 + 1 - self.y, dp)

    def at_layer(self, layer):
        return (layer * 2 + self.y, self.dp)


def greet(partners):
    barrier = pltpu.get_barrier_semaphore()
    for partner in partners:
        pl.semaphore_signal(barrier, inc=1, device_id=partner, device_id_type=MESH)
    pl.semaphore_wait(barrier, len(partners))


def experts_kernel(
    n_dp, experts,
    x_own, all_g, near_g, wg_hbm, wu_hbm, wd_hbm,
    out_sum, grad_sum, x_out, g_out, acts_out, all_x,
    sib_o, sib_g, one_o, one_g, two_o, two_g, z_o, z_g,
    wg, wu, wd, xs, gs, gate_rows, acts, xin, gin, stage_o, stage_g, acc_o, acc_g, tmp_o, tmp_g,
    leave_o, leave_g, pin, table,
    w_sem, in_sem, keep_sem, act_sem, own_sem, zx_send, zx_recv, ag_send, ag_recv,
    sib_send, sib_recv, one_send, one_recv, two_send, two_recv, z_send, z_recv, tmp_sem,
):
    n_dev, rows, wide = all_x.shape
    local, width, hid = wg.shape
    cap = xs.shape[2]
    group = 2 * n_dp
    layers = n_dev // group
    m = group * cap
    slots = xin.shape[0]
    half = width // 2
    here = Place(n_dp)
    rank, core, x, y = here.rank, here.core, here.x, here.y
    first = here.ep * local

    def remote(src, dst, send, recv, device):
        return pltpu.make_async_remote_copy(
            src_ref=src, dst_ref=dst, send_sem=send, recv_sem=recv,
            device_id=device, device_id_type=MESH,
        )

    def layer_of(i):
        return nearby(here.layer, i, layers)

    def weights():
        return [
            pltpu.make_async_copy(s, d, w_sem.at[i])
            for i, (s, d) in enumerate(((wg_hbm, wg), (wu_hbm, wu), (wd_hbm, wd)))
        ]

    def z_copy(block, up):
        at = all_x.at[block * group + rank]
        device = here.at_layer(here.layer + 1 if up else here.layer - 1)
        return remote(at, at, zx_send.at[block], zx_recv.at[block], device)

    def z_own(act):
        @pl.when(here.layer + 1 < layers)
        def _():
            act(own_z(True))

        @pl.when(here.layer >= 1)
        def _():
            act(own_z(False))

    def own_z(up):
        device = here.at_layer(here.layer + 1 if up else here.layer - 1)
        return remote(
            x_own, all_x.at[here.layer * group + rank],
            zx_send.at[here.layer if up else layers], zx_recv.at[here.layer], device,
        )

    def passes(i):
        block = layer_of(i)
        up = jnp.logical_and(block < here.layer, here.layer + 1 < layers)
        down = jnp.logical_and(block > here.layer, here.layer >= 1)
        return block, up, down

    def z_pass(i):
        block, up, down = passes(i)

        @pl.when(up)
        def _():
            z_copy(block, True).wait_recv()
            z_copy(block, True).start()

        @pl.when(down)
        def _():
            z_copy(block, False).wait_recv()
            z_copy(block, False).start()

    def z_arrive(i):
        block, up, down = passes(i)

        @pl.when(jnp.logical_not(jnp.logical_or(up, down)))
        def _():
            z_copy(block, True).wait_recv()

    def z_drain(i):
        block, up, down = passes(i)

        @pl.when(up)
        def _():
            z_copy(block, True).wait_send()

        @pl.when(down)
        def _():
            z_copy(block, False).wait_send()

    def own_copy():
        return pltpu.make_async_copy(x_own, all_x.at[here.layer * group + rank], own_sem.at[0])

    over_x_rank = y * n_dp + (1 - x) * 2 + core
    over_y_rank = (1 - y) * n_dp + x * 2 + core
    across_rank = (1 - y) * n_dp + (1 - x) * 2 + core
    first_half, second_half = pl.ds(0, half), pl.ds(half, wide - half)

    def gather_copy(i, kind):
        base = layer_of(i) * group
        which, cols, device = {
            0: (rank, first_half, here.over_x),
            1: (rank, second_half, here.over_x),
            2: (rank, first_half, here.over_y),
            3: (rank, second_half, here.over_y),
            4: (over_x_rank, first_half, here.over_y),
            5: (over_y_rank, second_half, here.over_x),
            6: (rank, pl.ds(0, wide), here.sibling),
            7: (over_x_rank, pl.ds(0, wide), here.sibling),
            8: (over_y_rank, pl.ds(0, wide), here.sibling),
            9: (across_rank, pl.ds(0, wide), here.sibling),
        }[kind]
        ref = all_x.at[base + which, :, cols]
        return remote(ref, ref, ag_send.at[i, kind], ag_recv.at[i, kind], device)

    def gather_a(i):
        @pl.when(i < layers - 1)
        def _():
            z_arrive(i)

        @pl.when(i == layers - 1)
        def _():
            own_copy().wait()

        for kind in (0, 3, 1, 2, 6):
            gather_copy(i, kind).start()

    def gather_b(i):
        for got, then in ((0, 4), (3, 5), (1, 7), (2, 8)):
            gather_copy(i, got).wait_recv()
            gather_copy(i, then).start()

    def gather_c(i):
        gather_copy(i, 4).wait_recv()
        gather_copy(i, 5).wait_recv()
        gather_copy(i, 9).start()

    def gather_d(i):
        for kind in (6, 7, 8, 9):
            gather_copy(i, kind).wait_recv()

    def sib_copy(i, q, slot):
        return (
            remote(stage_o.at[slot], sib_o.at[i, q], sib_send.at[0, slot], sib_recv.at[0, i, q],
                   here.sibling),
            remote(stage_g.at[slot], sib_g.at[i, q], sib_send.at[1, slot], sib_recv.at[1, i, q],
                   here.sibling),
        )

    def one_copy_o(i, j):
        return remote(acc_o.at[j * 2 + 1 - x], one_o.at[i, j], one_send.at[0, j],
                      one_recv.at[0, i, j], here.over_x)

    def one_copy_g(i, j):
        return remote(acc_g.at[(1 - y) * 2 + j], one_g.at[i, j], one_send.at[1, j],
                      one_recv.at[1, i, j], here.over_y)

    def two_copy(i):
        return (
            remote(acc_o.at[(1 - y) * 2 + x], two_o.at[i], two_send.at[0], two_recv.at[0, i],
                   here.over_y),
            remote(acc_g.at[y * 2 + 1 - x], two_g.at[i], two_send.at[1], two_recv.at[1, i],
                   here.over_x),
        )

    def out_copy(i):
        at, device = here.layer, here.at_layer(layer_of(i))
        return (
            remote(leave_o, z_o.at[at], z_send.at[0], z_recv.at[0, at], device),
            remote(leave_g, z_g.at[at], z_send.at[1], z_recv.at[1, at], device),
        )

    def fetch(src_o, src_g, slot):
        return (
            pltpu.make_async_copy(src_o, tmp_o.at[slot], tmp_sem.at[0, slot]),
            pltpu.make_async_copy(src_g, tmp_g.at[slot], tmp_sem.at[1, slot]),
        )

    def start(copies):
        for copy in copies:
            copy.start()

    def finish(copies):
        for copy in copies:
            copy.wait()

    def add(dst, q, tmp, slot):
        total = dst[q].astype(F32) + tmp[slot].astype(F32)
        dst[q] = total.astype(BF)

    def sum_one(i):
        o, g = one_copy_o(i, 1 - y), one_copy_g(i, 1 - x)
        o.wait_recv()
        g.wait_recv()
        copies = fetch(one_o.at[i, 1 - y], one_g.at[i, 1 - x], 0)
        start(copies)
        finish(copies)
        add(acc_o, (1 - y) * 2 + x, tmp_o, 0)
        add(acc_g, y * 2 + 1 - x, tmp_g, 0)
        start(two_copy(i))

    def sum_two(i):
        own = y * 2 + x
        one_copy_o(i, y).wait_recv()
        one_copy_g(i, x).wait_recv()
        ones = fetch(one_o.at[i, y], one_g.at[i, x], 0)
        start(ones)
        for copy in two_copy(i):
            copy.wait_recv()
        twos = fetch(two_o.at[i], two_g.at[i], 1)
        start(twos)
        finish(ones)
        finish(twos)

        @pl.when(i > 0)
        def _():
            for copy in out_copy(i - 1):
                copy.wait_send()

        for acc, tmp, leave in ((acc_o, tmp_o, leave_o), (acc_g, tmp_g, leave_g)):
            total = acc[own].astype(F32) + tmp[0].astype(F32) + tmp[1].astype(F32)
            leave[...] = total.astype(BF)
        for j in range(2):
            one_copy_o(i, j).wait_send()
            one_copy_g(i, j).wait_send()
        for copy in two_copy(i):
            copy.wait_send()

        @pl.when(i < layers - 1)
        def _():
            start(out_copy(i))

    start(weights())
    greet([here.over_x, here.over_y, here.sibling]
          + [here.at_layer(flip(here.layer, i, layers)) for i in range(1, layers)])
    own_copy().start()
    z_own(lambda copy: copy.start())
    z_pass(0)
    gather_a(0)
    z_pass(1)
    gather_b(0)
    for i in range(2, layers - 1):
        z_pass(i)
    gather_c(0)
    gather_a(1)

    def chunk(i, carry):
        base = layer_of(i) * group

        gather_d(i)

        def load(b, slot):
            return (
                pltpu.make_async_copy(all_x.at[base + b], xin.at[slot], in_sem.at[0, slot]),
                pltpu.make_async_copy(
                    all_g.at[base + b, pl.ds(0, experts), pl.ds(width, rows)], pin.at[slot],
                    in_sem.at[2, slot],
                ),
            )

        def load_g(b, slot, act):
            @pl.when(i < layers - 1)
            def _():
                act(pltpu.make_async_copy(
                    all_g.at[base + b, :, pl.ds(0, width)], gin.at[slot], in_sem.at[1, slot]
                ))

            @pl.when(i == layers - 1)
            def _():
                act(pltpu.make_async_copy(near_g.at[b], gin.at[slot], in_sem.at[1, slot]))

        def begin_load(b, slot):
            start(load(b, slot))
            load_g(b, slot, lambda copy: copy.start())

        for b in range(slots - 1):
            begin_load(b, b)

        def bring(b, c):
            slot = lax.rem(b, slots)
            finish(load(b, slot))
            load_g(b, slot, lambda copy: copy.wait())

            @pl.when(b + slots - 1 < group)
            def _():
                begin_load(b + slots - 1, lax.rem(b + slots - 1, slots))

            size = local * cap
            chooses = (
                lax.broadcasted_iota(jnp.int32, (size, experts), 1)
                == lax.broadcasted_iota(jnp.int32, (size, experts), 0) // cap + first
            )
            places = dot(jnp.where(chooses, 1.0, 0.0).astype(BF), pin[slot])
            seat = lax.broadcasted_iota(jnp.int32, (size, rows), 0) % cap
            hot = jnp.where(places == seat.astype(F32), 1.0, 0.0).astype(BF)
            table[b] = hot
            for src, dst in ((xin, xs), (gin, gs)):
                for n in range(0, width, STEP):
                    got = dot(hot, src[slot, :, n : n + STEP]).astype(BF)
                    dst[:, b, :, n : n + STEP] = got.reshape(local, cap, STEP)
            gates = dot(hot, xin[slot, :, width:wide])
            lanes = lax.broadcasted_iota(jnp.int32, gates.shape, 1) % experts
            expert = lax.broadcasted_iota(jnp.int32, gates.shape, 0) // cap + first
            gates = jnp.sum(jnp.where(lanes == expert, gates, 0.0), axis=1, keepdims=True)
            gate_rows[:, b] = jnp.broadcast_to(gates, (local * cap, 128)).reshape(local, cap, 128)
            return c

        lax.fori_loop(0, group, bring, 0)

        def keep(e):
            return (
                pltpu.make_async_copy(xs.at[e], x_out.at[e, pl.ds(base, group)], keep_sem.at[0, e]),
                pltpu.make_async_copy(gs.at[e], g_out.at[e, pl.ds(base, group)], keep_sem.at[1, e]),
            )

        def keep_acts(e, slot):
            return pltpu.make_async_copy(
                acts.at[slot], acts_out.at[:, e, pl.ds(base * cap, m)], act_sem.at[slot]
            )

        lax.fori_loop(0, local, lambda e, c: (start(keep(e)), c)[1], 0)

        @pl.when(i == 0)
        def _():
            finish(weights())

        def expert(e, c):
            def hook(number, when, action):
                @pl.when(jnp.logical_and(e == number * local // HOOKS, when))
                def _():
                    action()

            hook(6, i + 2 < layers, lambda: gather_a(i + 2))
            hook(4, i + 1 < layers, lambda: gather_b(i + 1))
            hook(7, i + 1 < layers, lambda: gather_c(i + 1))
            hook(4, i > 0, lambda: sum_one(i - 1))
            slot = lax.rem(e, 2)

            @pl.when(jnp.logical_or(i > 0, e >= 2))
            def _():
                keep_acts(e, slot).wait()

            xe = xs[e].reshape(m, width)
            ge = gs[e].reshape(m, width)
            gate_part = dot(xe, wg[e])
            up_part = dot(xe, wu[e])
            raw = dot_t(ge, wd[e])
            gate = gate_rows[e].reshape(m, 128)[:, :1]
            sig = 1.0 / (1.0 + jnp.exp(-gate_part))
            silu = gate_part * sig
            hidden = silu * up_part
            own = jnp.sum(hidden * raw, axis=1, keepdims=True)
            lanes = lax.broadcasted_iota(jnp.int32, (m, 128), 1)
            grad_hidden = raw * gate
            hg = (hidden * gate).astype(BF)
            dg = (grad_hidden * up_part * sig * (1.0 + gate_part * (1.0 - sig))).astype(BF)
            du = (grad_hidden * silu).astype(BF)
            gate_rows[e] = jnp.where(lanes == first + e, own, 0.0).reshape(group, cap, 128)
            acts[slot, 0] = hg
            acts[slot, 1] = dg
            acts[slot, 2] = du
            keep_acts(e, slot).start()
            finish(keep(e))
            for n in range(0, width, STEP):
                out = dot(hg, wd[e, :, n : n + STEP]).astype(BF)
                gs[e, :, :, n : n + STEP] = out.reshape(group, cap, STEP)
                back = dot_t(dg, wg[e, n : n + STEP, :]) + dot_t(du, wu[e, n : n + STEP, :])
                xs[e, :, :, n : n + STEP] = back.astype(BF).reshape(group, cap, STEP)
            return c

        lax.fori_loop(0, local, expert, 0)

        def combine(b, put_o, put_g):
            hot = table[b]
            for n in range(0, width, STEP):
                got = gs[:, b, :, n : n + STEP].reshape(local * cap, STEP)
                put_o(n, STEP, tdot(hot, got))
                got = xs[:, b, :, n : n + STEP].reshape(local * cap, STEP)
                put_g(n, STEP, tdot(hot, got))
            got = gate_rows[:, b].reshape(local * cap, 128).astype(BF)
            put_g(width, 128, tdot(hot, got))

        def square(k):
            return (y + 1 - k % 2) % 2, (x + 1 - k // 2) % 2

        def give(k, c):
            slot = lax.rem(k, 2)
            to_y, to_x = square(k)
            q = to_y * 2 + to_x

            @pl.when(jnp.logical_or(i > 0, k >= 2))
            def _():
                for copy in sib_copy(i, q, slot):
                    copy.wait_send()

            def put_o(n, size, value):
                stage_o[slot, :, pl.ds(n, size)] = value.astype(BF)

            def put_g(n, size, value):
                stage_g[slot, :, pl.ds(n, size)] = value.astype(BF)

            combine(q * 2 + 1 - core, put_o, put_g)
            start(sib_copy(i, q, slot))
            return c

        lax.fori_loop(0, 4, give, 0)

        def from_sibling(k):
            to_y, to_x = square(k)
            q = to_y * 2 + to_x
            return fetch(sib_o.at[i, q], sib_g.at[i, q], lax.rem(k, 2))

        def bring_sibling(k):
            to_y, to_x = square(k)
            for copy in sib_copy(i, to_y * 2 + to_x, 0):
                copy.wait_recv()
            start(from_sibling(k))

        @pl.when(i > 0)
        def _():
            sum_two(i - 1)

        bring_sibling(0)

        def hold(k, c):
            slot = lax.rem(k, 2)
            to_y, to_x = square(k)
            q = to_y * 2 + to_x

            @pl.when(k < 3)
            def _():
                bring_sibling(k + 1)

            finish(from_sibling(k))

            def put_o(n, size, value):
                cols = pl.ds(n, size)
                acc_o[q, :, cols] = (value + tmp_o[slot, :, cols].astype(F32)).astype(BF)

            def put_g(n, size, value):
                cols = pl.ds(n, size)
                acc_g[q, :, cols] = (value + tmp_g[slot, :, cols].astype(F32)).astype(BF)

            combine(q * 2 + core, put_o, put_g)

            @pl.when(k < 2)
            def _():
                one_copy_o(i, to_y).start()

            @pl.when(k % 2 == 0)
            def _():
                one_copy_g(i, to_x).start()

            return c

        lax.fori_loop(0, 4, hold, 0)
        return carry

    lax.fori_loop(0, layers, chunk, 0)
    last = layers - 1
    sum_one(last)
    sum_two(last)
    out_sum[...] = leave_o[...].astype(F32)
    grad_sum[...] = leave_g[...].astype(F32)

    def arrive(i):
        at = layer_of(i)
        for copy in (
            remote(leave_o, z_o.at[at], z_send.at[0], z_recv.at[0, at], here.sibling),
            remote(leave_g, z_g.at[at], z_send.at[1], z_recv.at[1, at], here.sibling),
        ):
            copy.wait_recv()
        start(fetch(z_o.at[at], z_g.at[at], i % 2))

    arrive(0)
    for i in range(last):
        if i + 1 < last:
            arrive(i + 1)
        finish(fetch(z_o.at[layer_of(i)], z_g.at[layer_of(i)], i % 2))
        out_sum[...] += tmp_o[i % 2].astype(F32)
        grad_sum[...] += tmp_g[i % 2].astype(F32)
    for slot in range(2):
        for copy in sib_copy(last, slot, slot):
            copy.wait_send()
        pltpu.make_async_copy(
            acts.at[slot], acts_out.at[:, 0, pl.ds(0, m)], act_sem.at[slot]
        ).wait()

    def drain(i, c):
        for kind in range(10):
            gather_copy(i, kind).wait_send()
        return c

    lax.fori_loop(0, layers, drain, 0)
    z_own(lambda copy: copy.wait_send())
    for i in range(last):
        z_drain(i)


def run_experts(x_own, all_g, near_g, wg, wu, wd, n_dp, experts, cap):
    rows, wide = x_own.shape
    n_dev = all_g.shape[0]
    local, width, hid = wg.shape
    group = 2 * n_dp
    layers = n_dev // group
    m = group * cap
    wide_g = width + 128
    slots = 3
    dma = pltpu.SemaphoreType.DMA
    shape = jax.ShapeDtypeStruct
    slot_rows = shape((local, n_dev, cap, width), BF)
    flops = 12 * n_dev * cap * local * width * hid
    result = pl.pallas_call(
        functools.partial(experts_kernel, n_dp, experts),
        out_shape=(
            shape((rows, width), F32), shape((rows, wide_g), F32),
            slot_rows, slot_rows,
            shape((3, local, n_dev * cap, hid), BF),
            shape((n_dev, rows, wide), BF),
            shape((layers, 4, rows, width), BF), shape((layers, 4, rows, wide_g), BF),
            shape((layers, 2, rows, width), BF), shape((layers, 2, rows, wide_g), BF),
            shape((layers, rows, width), BF), shape((layers, rows, wide_g), BF),
            shape((layers, rows, width), BF), shape((layers, rows, wide_g), BF),
        ),
        in_specs=[ANY] * 6,
        out_specs=(VMEM, VMEM) + (ANY,) * 12,
        scratch_shapes=[
            pltpu.VMEM(wg.shape, BF), pltpu.VMEM(wu.shape, BF), pltpu.VMEM(wd.shape, BF),
            pltpu.VMEM((local, group, cap, width), BF),
            pltpu.VMEM((local, group, cap, width), BF),
            pltpu.VMEM((local, group, cap, 128), F32),
            pltpu.VMEM((2, 3, m, hid), BF),
            pltpu.VMEM((slots, rows, wide), BF),
            pltpu.VMEM((slots, rows, width), BF),
            pltpu.VMEM((2, rows, width), BF), pltpu.VMEM((2, rows, wide_g), BF),
            pltpu.VMEM((4, rows, width), BF), pltpu.VMEM((4, rows, wide_g), BF),
            pltpu.VMEM((2, rows, width), BF), pltpu.VMEM((2, rows, wide_g), BF),
            pltpu.VMEM((rows, width), BF), pltpu.VMEM((rows, wide_g), BF),
            pltpu.VMEM((slots, experts, rows), BF), pltpu.VMEM((group, local * cap, rows), BF),
            dma((3,)), dma((3, slots)), dma((2, local)), dma((2,)), dma((1,)),
            dma((layers + 1,)), dma((layers,)), dma((layers, 10)), dma((layers, 10)),
            dma((2, 2)), dma((2, layers, 4)), dma((2, 2)), dma((2, layers, 2)),
            dma((2,)), dma((2, layers)), dma((2,)), dma((2, layers)), dma((2, 2)),
        ],
        compiler_params=pltpu.CompilerParams(
            collective_id=1, has_side_effects=True, vmem_limit_bytes=64 * 2**20
        ),
        cost_estimate=pl.CostEstimate(flops=flops, bytes_accessed=200 * 2**20, transcendentals=0),
    )(x_own, all_g, near_g, wg, wu, wd)
    return result[:5]


def weights_kernel(x, g, acts, grad_g, grad_u, grad_d):
    first = pl.program_id(1) == 0
    xe, ge = x[0], g[0]

    def put(ref, n, size, value, axis):
        at = (0, pl.ds(n, size), slice(None)) if axis == 0 else (0, slice(None), pl.ds(n, size))

        @pl.when(first)
        def _():
            ref[at] = value

        @pl.when(jnp.logical_not(first))
        def _():
            ref[at] += value

    hg, dg, du = acts[0, 0], acts[1, 0], acts[2, 0]
    for n in range(0, xe.shape[1], STEP):
        part = xe[:, n : n + STEP]
        put(grad_g, n, STEP, tdot(part, dg), 0)
        put(grad_u, n, STEP, tdot(part, du), 0)
        put(grad_d, n, STEP, tdot(hg, ge[:, n : n + STEP]), 1)


def run_weights(x_slots, g_slots, acts):
    local, n_dev, cap, width = x_slots.shape
    hid = acts.shape[-1]
    total = n_dev * cap
    tile = min(1024, total)
    x_slots = x_slots.reshape(local, total, width)
    g_slots = g_slots.reshape(local, total, width)
    row = pl.BlockSpec((1, tile, width), lambda e, k: (e, k, 0))
    wide = pl.BlockSpec((1, width, hid), lambda e, k: (e, 0, 0))
    deep = pl.BlockSpec((1, hid, width), lambda e, k: (e, 0, 0))
    return pl.pallas_call(
        weights_kernel,
        grid=(local, total // tile),
        out_shape=(
            jax.ShapeDtypeStruct((local, width, hid), F32),
            jax.ShapeDtypeStruct((local, width, hid), F32),
            jax.ShapeDtypeStruct((local, hid, width), F32),
        ),
        in_specs=[row, row, pl.BlockSpec((3, 1, tile, hid), lambda e, k: (0, e, k, 0))],
        out_specs=(wide, wide, deep),
        compiler_params=pltpu.CompilerParams(vmem_limit_bytes=60 * 2**20),
        cost_estimate=pl.CostEstimate(
            flops=6 * local * total * width * hid, bytes_accessed=130 * 2**20, transcendentals=0
        ),
    )(x_slots, g_slots, acts)


def peer(here, rank):
    return (here.layer * 2 + rank // here.n_dp, rank % here.n_dp)


def others(here, group):
    return [lax.rem(here.rank + k, group) for k in range(1, group)]


def remote(src, dst, send, recv, device):
    return pltpu.make_async_remote_copy(
        src_ref=src, dst_ref=dst, send_sem=send, recv_sem=recv,
        device_id=device, device_id_type=MESH,
    )


class LayerGather:
    def __init__(self, here, own, buf, own_sem, send, recv):
        self.here, self.own, self.buf = here, own, buf
        self.own_sem, self.send, self.recv = own_sem, send, recv

    def copy(self, kind):
        here, buf = self.here, self.buf
        wide = buf.shape[-1]
        half = wide // 256 * 128
        low, high, full = pl.ds(0, half), pl.ds(half, wide - half), pl.ds(0, wide)
        n_dp, x, y, core = here.n_dp, here.x, here.y, here.core
        over_x = y * n_dp + (1 - x) * 2 + core
        over_y = (1 - y) * n_dp + x * 2 + core
        across = (1 - y) * n_dp + (1 - x) * 2 + core
        which, cols, device = {
            0: (here.rank, low, here.over_x),
            1: (here.rank, high, here.over_x),
            2: (here.rank, low, here.over_y),
            3: (here.rank, high, here.over_y),
            4: (over_x, low, here.over_y),
            5: (over_y, high, here.over_x),
            6: (here.rank, full, here.sibling),
            7: (over_x, full, here.sibling),
            8: (over_y, full, here.sibling),
            9: (across, full, here.sibling),
        }[kind]
        dst = buf.at[which, :, cols]
        src = self.own.at[:, cols] if kind in (0, 1, 2, 3, 6) else dst
        return remote(src, dst, self.send.at[kind], self.recv.at[kind], device)

    def keep(self):
        return pltpu.make_async_copy(self.own, self.buf.at[self.here.rank], self.own_sem.at[0])

    def begin(self):
        self.keep().start()
        for kind in (0, 3, 1, 2, 6):
            self.copy(kind).start()

    def forward(self):
        for got, then in ((0, 4), (3, 5), (1, 7), (2, 8)):
            self.copy(got).wait_recv()
            self.copy(then).start()

    def across(self):
        self.copy(4).wait_recv()
        self.copy(5).wait_recv()
        self.copy(9).start()

    def end(self):
        for kind in (6, 7, 8, 9):
            self.copy(kind).wait_recv()
        for kind in range(10):
            self.copy(kind).wait_send()
        self.keep().wait()


class WideGather:
    def __init__(self, here, layers, own, buf, own_sem, z_send, z_recv, send, recv):
        self.here, self.layers, self.own, self.buf = here, layers, own, buf
        self.own_sem, self.z_send, self.z_recv = own_sem, z_send, z_recv
        self.send, self.recv = send, recv
        self.last = layers - 1

    def layer_of(self, i):
        return nearby(self.here.layer, i, self.layers)

    def keep(self):
        return pltpu.make_async_copy(
            self.own, self.buf.at[self.here.layer, self.here.rank], self.own_sem.at[0]
        )

    def over_z(self, block, up, own=False):
        here = self.here
        at = self.buf.at[block, here.rank]
        return remote(
            self.own if own else at, at,
            self.z_send.at[self.layers if own and not up else block], self.z_recv.at[block],
            here.at_layer(here.layer + 1 if up else here.layer - 1),
        )

    def own_z(self, act):
        layer = self.here.layer

        @pl.when(layer + 1 < self.layers)
        def _():
            act(self.over_z(layer, True, True))

        @pl.when(layer >= 1)
        def _():
            act(self.over_z(layer, False, True))

    def passes(self, i):
        layer, block = self.here.layer, self.layer_of(i)
        up = jnp.logical_and(block < layer, layer + 1 < self.layers)
        down = jnp.logical_and(block > layer, layer >= 1)
        return block, up, down

    def pass_on(self, i):
        block, up, down = self.passes(i)

        @pl.when(up)
        def _():
            self.over_z(block, True).wait_recv()
            self.over_z(block, True).start()

        @pl.when(down)
        def _():
            self.over_z(block, False).wait_recv()
            self.over_z(block, False).start()

    def copy(self, i, kind):
        here = self.here
        block = self.buf.at[self.layer_of(i)]
        job = LayerGather(here, block.at[here.rank], block, None, self.send.at[i], self.recv.at[i])
        return job.copy(kind)

    def begin(self):
        self.keep().start()
        self.own_z(lambda copy: copy.start())

    def enter(self, i):
        block, up, down = self.passes(i)

        @pl.when(jnp.logical_not(jnp.logical_or(up, down)))
        def _():
            self.over_z(block, True).wait_recv()

        for kind in (0, 3, 1, 2, 6):
            self.copy(i, kind).start()

    def forward(self, i):
        for got, then in ((0, 4), (3, 5), (1, 7), (2, 8)):
            self.copy(i, got).wait_recv()
            self.copy(i, then).start()

    def across(self, i):
        self.copy(i, 4).wait_recv()
        self.copy(i, 5).wait_recv()
        self.copy(i, 9).start()

    def end(self):
        self.keep().wait()
        for i in range(self.last):
            for kind in (6, 7, 8, 9):
                self.copy(i, kind).wait_recv()
        for i in range(self.last):
            for kind in range(10):
                self.copy(i, kind).wait_send()
        self.own_z(lambda copy: copy.wait_send())
        for i in range(self.last):
            block, up, down = self.passes(i)

            @pl.when(up)
            def _():
                self.over_z(block, True).wait_send()

            @pl.when(down)
            def _():
                self.over_z(block, False).wait_send()


class LayerSum:
    def __init__(self, here, part, acc, sib, one, two, load, send, recv):
        self.here, self.part, self.acc, self.sib = here, part, acc, sib
        self.one, self.two, self.load_sem, self.send, self.recv = one, two, load, send, recv
        wide = acc.shape[-1]
        half = wide // 256 * 128
        self.cols = (pl.ds(0, half), pl.ds(half, wide - half))

    def load(self, q):
        return pltpu.make_async_copy(
            self.part.at[q * 2 + self.here.core], self.acc.at[q], self.load_sem.at[q]
        )

    def copy(self, kind):
        here, acc = self.here, self.acc
        x, y = here.x, here.y
        low, high = self.cols
        if kind < 4:
            src, dst = self.part.at[kind * 2 + 1 - here.core], self.sib.at[kind]
            device = here.sibling
        elif kind < 6:
            j = kind - 4
            src, dst, device = acc.at[j * 2 + 1 - x, :, low], self.one.at[j, :, low], here.over_x
        elif kind < 8:
            j = kind - 6
            src, dst = acc.at[(1 - y) * 2 + j, :, high], self.one.at[j, :, high]
            device = here.over_y
        elif kind == 8:
            src, dst, device = acc.at[(1 - y) * 2 + x, :, low], self.two.at[:, low], here.over_y
        else:
            src, dst, device = acc.at[y * 2 + 1 - x, :, high], self.two.at[:, high], here.over_x
        return remote(src, dst, self.send.at[kind], self.recv.at[kind], device)

    def add(self, q, cols, got):
        total = self.acc[q, :, cols].astype(F32) + got.astype(F32)
        self.acc[q, :, cols] = total.astype(BF)

    def begin(self):
        for q in range(4):
            self.copy(q).start()
            self.load(q).start()

    def first(self):
        for q in range(4):
            self.load(q).wait()
            self.copy(q).wait_recv()
            for cols in self.cols:
                self.add(q, cols, self.sib[q, :, cols])
        for kind in (4, 5, 6, 7):
            self.copy(kind).start()

    def second(self):
        x, y = self.here.x, self.here.y
        low, high = self.cols
        for j in range(2):
            self.copy(4 + j).wait_recv()
            self.add(j * 2 + x, low, self.one[j, :, low])
            self.copy(6 + j).wait_recv()
            self.add(y * 2 + j, high, self.one[j, :, high])
        self.copy(8).start()
        self.copy(9).start()

    def third(self, out):
        own = self.here.y * 2 + self.here.x
        for kind, cols in zip((8, 9), self.cols):
            self.copy(kind).wait_recv()
            out[:, cols] = self.acc[own, :, cols].astype(F32) + self.two[:, cols].astype(F32)
        for kind in range(10):
            self.copy(kind).wait_send()

    @staticmethod
    def scratch(rows, wide):
        return [
            pltpu.VMEM((4, rows, wide), BF), pltpu.VMEM((4, rows, wide), BF),
            pltpu.VMEM((2, rows, wide), BF), pltpu.VMEM((rows, wide), BF),
            pltpu.SemaphoreType.DMA((4,)),
            pltpu.SemaphoreType.DMA((10,)), pltpu.SemaphoreType.DMA((10,)),
        ]


def comm_params(number):
    return pltpu.CompilerParams(
        collective_id=number, has_side_effects=True, vmem_limit_bytes=48 * 2**20
    )


def stats_kernel(n_dp, value, out, land, send, recv):
    here = Place(n_dp)
    group = 2 * n_dp
    ranks = others(here, group)
    greet([peer(here, rank) for rank in ranks])

    def copy(k):
        return remote(
            value, land.at[k], send.at[k], recv.at[k], peer(here, ranks[k])
        )

    for k in range(group - 1):
        copy(k).start()
    total = value[...]
    for k in range(group - 1):
        copy(k).wait_recv()
        total += land[k]
    out[...] = total
    for k in range(group - 1):
        copy(k).wait_send()


def layer_stats(value, n_dp):
    dma = pltpu.SemaphoreType.DMA
    peers = 2 * n_dp - 1
    flat = value.reshape(-1, 128)
    out = pl.pallas_call(
        functools.partial(stats_kernel, n_dp),
        out_shape=jax.ShapeDtypeStruct(flat.shape, F32),
        in_specs=[VMEM],
        out_specs=VMEM,
        scratch_shapes=[pltpu.VMEM((peers,) + flat.shape, F32), dma((peers,)), dma((peers,))],
        compiler_params=comm_params(4),
    )(flat)
    return out.reshape(value.shape)


def front_kernel(
    n_dp, layers, x_own, w_q, w_k, w_v, w_o, small, g_own,
    x_all, qkv, wo, small_all, g_near, wo_col,
    own_sem, x_send, x_recv, a_keep, a_send, a_recv, up_send, up_recv, down_send, down_recv,
    o_keep, o_send, o_recv, s_send, s_recv, t_send, t_recv, g_keep, g_send, g_recv,
):
    here = Place(n_dp)
    group = 2 * n_dp
    layer, rank = here.layer, here.rank
    own = w_q.shape[0]
    cols = qkv.shape[-1]
    ranks = others(here, group)
    away = [flip(layer, i, layers) for i in range(1, layers)]
    greet([peer(here, r) for r in ranks] + [here.at_layer(z) for z in away])
    gather = LayerGather(here, x_own, x_all, own_sem, x_send, x_recv)
    cotangent = LayerGather(here, g_own, g_near, g_keep, g_send, g_recv)
    weights = (w_q, w_k, w_v)

    def rows_at(index):
        return pl.ds(pl.multiple_of(index * own, own), own)

    def block_cols(index):
        return pl.ds(pl.multiple_of(index * cols, cols), cols)

    def swap(w, k):
        return remote(
            weights[w].at[:, block_cols(ranks[k])], qkv.at[w, layer, rows_at(rank)],
            a_send.at[w, k], a_recv.at[w, k], peer(here, ranks[k]),
        )

    def swap_own(w):
        return pltpu.make_async_copy(
            weights[w].at[:, block_cols(rank)], qkv.at[w, layer, rows_at(rank)], a_keep.at[w]
        )

    def small_out(i):
        ref = small_all.at[layer, rank]
        return remote(small, ref, s_send.at[i], s_recv.at[i], here.at_layer(away[i]))

    def small_keep():
        return pltpu.make_async_copy(small, small_all.at[layer, rank], a_keep.at[3])

    def small_share(k):
        ref = small_all.at[:, rank]
        return remote(ref, ref, t_send.at[k], t_recv.at[k], peer(here, ranks[k]))

    def o_own():
        return pltpu.make_async_copy(w_o, wo_col.at[layer], a_keep.at[4])

    for w in range(3):
        swap_own(w).start()
        for k in range(group - 1):
            swap(w, k).start()
    o_own().start()
    small_keep().start()
    for i in range(layers - 1):
        small_out(i).start()
    gather.begin()
    for w in range(3):
        swap_own(w).wait()
        for k in range(group - 1):
            swap(w, k).wait_recv()
    o_own().wait()

    def chain(which, up, s):
        block = layer - s if up else layer + s
        ref = qkv.at[:, block] if which == 0 else wo_col.at[block]
        device = here.at_layer(layer + 1 if up else layer - 1)
        sems = (up_send, up_recv) if up else (down_send, down_recv)
        return remote(ref, ref, sems[0].at[which, s], sems[1].at[which, s], device)

    def step(which, s, wait):
        for up in (True, False):
            leaves = (
                jnp.logical_and(layer + 1 < layers, layer - s >= 0) if up
                else jnp.logical_and(layer >= 1, layer + s < layers)
            )
            comes = layer - 1 - s >= 0 if up else layer + 1 + s < layers
            if wait:
                @pl.when(comes)
                def _():
                    chain(which, up, s).wait_recv()
            else:
                @pl.when(leaves)
                def _():
                    chain(which, up, s).start()

    step(0, 0, False)
    gather.forward()
    step(1, 0, False)
    gather.across()
    small_keep().wait()
    for i in range(layers - 1):
        small_out(i).wait_recv()
    for k in range(group - 1):
        small_share(k).start()
    cotangent.begin()
    for s in range(layers - 1):
        step(0, s, True)
        if s + 1 < layers - 1:
            step(0, s + 1, False)
        if s == 0:
            cotangent.forward()
        step(1, s, True)
        if s + 1 < layers - 1:
            step(1, s + 1, False)
        if s == 0:
            cotangent.across()

    def share(z):
        number = z * group + rank
        target, index = number // layers, number % layers

        def far():
            return remote(
                wo_col.at[z], wo.at[index], o_send.at[z], o_recv.at[index], peer(here, target)
            )

        def near():
            return pltpu.make_async_copy(wo_col.at[z], wo.at[index], o_keep.at[index])

        return target, far, near

    def source(index):
        number = rank * layers + index
        return number % group

    for z in range(layers):
        target, far, near = share(z)

        @pl.when(target != rank)
        def _():
            far().start()

        @pl.when(target == rank)
        def _():
            near().start()

    for index in range(layers):
        @pl.when(source(index) != rank)
        def _():
            remote(
                wo_col.at[0], wo.at[index], o_send.at[0], o_recv.at[index], here.sibling
            ).wait_recv()

        @pl.when(source(index) == rank)
        def _():
            pltpu.make_async_copy(wo_col.at[0], wo.at[index], o_keep.at[index]).wait()

    gather.end()
    cotangent.end()
    for k in range(group - 1):
        small_share(k).wait_recv()
    for w in range(3):
        for k in range(group - 1):
            swap(w, k).wait_send()
    for i in range(layers - 1):
        small_out(i).wait_send()
    for k in range(group - 1):
        small_share(k).wait_send()
    for z in range(layers):
        target, far, near = share(z)

        @pl.when(target != rank)
        def _():
            far().wait_send()

    for which in range(2):
        for s in range(layers - 1):
            @pl.when(jnp.logical_and(layer + 1 < layers, layer - s >= 0))
            def _():
                chain(which, True, s).wait_send()

            @pl.when(jnp.logical_and(layer >= 1, layer + s < layers))
            def _():
                chain(which, False, s).wait_send()


def run_front(x_own, w_q, w_k, w_v, w_o, small, g_own, n_dp, n_dev):
    rows, width = x_own.shape
    own = w_q.shape[0]
    group = 2 * n_dp
    layers = n_dev // group
    cols = width // group
    dma = pltpu.SemaphoreType.DMA
    shape = jax.ShapeDtypeStruct
    chain = dma((2, layers))
    result = pl.pallas_call(
        functools.partial(front_kernel, n_dp, layers),
        out_shape=(
            shape((group, rows, width), BF),
            shape((3, layers, group * own, cols), BF),
            shape((layers, own, width), BF),
            shape((layers, group) + small.shape, BF),
            shape((group, rows, width), BF),
            shape((layers, own, width), BF),
        ),
        in_specs=[ANY] * 7,
        out_specs=(ANY,) * 6,
        scratch_shapes=[
            dma((1,)), dma((10,)), dma((10,)), dma((5,)),
            dma((3, group - 1)), dma((3, group - 1)), chain, chain, chain, chain,
            dma((layers,)), dma((layers,)), dma((layers,)),
            dma((layers,)), dma((layers,)), dma((group,)), dma((group,)),
            dma((1,)), dma((10,)), dma((10,)),
        ],
        compiler_params=pltpu.CompilerParams(
            collective_id=5, has_side_effects=True, vmem_limit_bytes=64 * 2**20
        ),
    )(x_own, w_q, w_k, w_v, w_o, small, g_own)
    x_all, qkv, wo, small_all, g_near, _ = result
    return (
        x_all.reshape(group * rows, width), qkv.reshape(3, width, cols),
        wo.reshape(cols, width), small_all.reshape(width, -1), g_near,
    )


def back_kernel(
    n_dp, layers, part, gw, go, small,
    out, grad_w, grad_o, small_out,
    acc, sib, one, two, load_sem, n_send, n_recv,
    acc_w, acc_o, up_w, up_o, down_w, down_o, swapped, s_own, s_land, s_sum, s_far,
    w_load, o_keep, o_send, o_recv, up_send, up_recv, down_send, down_recv,
    a_keep, a_send, a_recv, s_keep, s_send, s_recv, t_send, t_recv,
):
    here = Place(n_dp)
    group = 2 * n_dp
    layer, rank = here.layer, here.rank
    own = grad_w.shape[1]
    cols = gw.shape[-1]
    ranks = others(here, group)
    away = [flip(layer, i, layers) for i in range(1, layers)]
    greet([peer(here, r) for r in ranks] + [here.at_layer(z) for z in away])
    job = LayerSum(here, part, acc, sib, one, two, load_sem, n_send, n_recv)

    def bring():
        return pltpu.make_async_copy(gw, acc_w, w_load.at[0])

    def share(i):
        number = rank * layers + i
        z, target = number // group, number % group

        def far():
            return remote(
                go.at[i], acc_o.at[z], o_send.at[i], o_recv.at[z], peer(here, target)
            )

        def near():
            return pltpu.make_async_copy(go.at[i], acc_o.at[z], o_keep.at[z])

        return target, far, near

    def small_swap(k):
        return remote(
            small.at[:, ranks[k]], s_land.at[k], s_send.at[k], s_recv.at[k], peer(here, ranks[k])
        )

    def small_keep():
        return pltpu.make_async_copy(small.at[:, rank], s_own, s_keep.at[0])

    bring().start()
    job.begin()
    for i in range(layers):
        target, far, near = share(i)

        @pl.when(target != rank)
        def _():
            far().start()

        @pl.when(target == rank)
        def _():
            near().start()
    small_keep().start()
    for k in range(group - 1):
        small_swap(k).start()

    def chain(which, up, z):
        acc_ref = (acc_w.at[:, z], acc_o.at[z])[which]
        land = ((up_w, up_o) if up else (down_w, down_o))[which].at[z]
        sems = (up_send, up_recv) if up else (down_send, down_recv)
        device = here.at_layer(layer + 1 if up else layer - 1)
        return remote(acc_ref, land, sems[0].at[which, z], sems[1].at[which, z], device)

    def take(which, up, z):
        chain(which, up, z).wait_recv()
        if which == 0:
            land = up_w if up else down_w
            for w in range(3):
                total = acc_w[w, z].astype(F32) + land[z, w].astype(F32)
                acc_w[w, z] = total.astype(BF)
        else:
            land = up_o if up else down_o
            acc_o[z] = (acc_o[z].astype(F32) + land[z].astype(F32)).astype(BF)

    def hop(which, d):
        @pl.when(layer + d < layers)
        def _():
            @pl.when(layer > 0)
            def _():
                take(which, True, layer + d)
            chain(which, True, layer + d).start()

        @pl.when(layer - d >= 0)
        def _():
            @pl.when(layer + 1 < layers)
            def _():
                take(which, False, layer - d)
            chain(which, False, layer - d).start()

    bring().wait()
    hop(0, layers - 1)
    job.first()
    for z in range(layers):
        source = (z * group + rank) // layers

        @pl.when(source != rank)
        def _():
            remote(
                go.at[0], acc_o.at[z], o_send.at[0], o_recv.at[z], here.sibling
            ).wait_recv()

        @pl.when(source == rank)
        def _():
            pltpu.make_async_copy(go.at[0], acc_o.at[z], o_keep.at[z]).wait()
    hop(1, layers - 1)
    small_keep().wait()
    total = s_own[...]
    for k in range(group - 1):
        small_swap(k).wait_recv()
        total += s_land[k]
    s_sum[...] = total

    def small_far(i):
        return remote(
            s_sum.at[away[i]], s_far.at[i], t_send.at[i], t_recv.at[i], here.at_layer(away[i])
        )

    for i in range(layers - 1):
        small_far(i).start()
    job.second()
    for d in range(layers - 2, 0, -1):
        hop(0, d)
        hop(1, d)
    job.third(out)
    total = s_sum[layer]
    for i in range(layers - 1):
        small_far(i).wait_recv()
        total += s_far[i]
    small_out[...] = total

    for which in range(2):
        @pl.when(layer > 0)
        def _():
            take(which, True, layer)

        @pl.when(layer + 1 < layers)
        def _():
            take(which, False, layer)

    def rows_at(index):
        return pl.ds(pl.multiple_of(index * own, own), own)

    def swap(k):
        return remote(
            acc_w.at[:, layer, rows_at(ranks[k])], swapped.at[rank],
            a_send.at[k], a_recv.at[k], peer(here, ranks[k]),
        )

    def swap_own():
        return pltpu.make_async_copy(
            acc_w.at[:, layer, rows_at(rank)], swapped.at[rank], a_keep.at[0]
        )

    swap_own().start()
    for k in range(group - 1):
        swap(k).start()
    grad_o[...] = acc_o[layer].astype(F32)
    swap_own().wait()
    for k in range(group - 1):
        swap(k).wait_recv()
    for r in range(group):
        for w in range(3):
            grad_w[w, :, r * cols : (r + 1) * cols] = swapped[r, w].astype(F32)

    for k in range(group - 1):
        swap(k).wait_send()
        small_swap(k).wait_send()
    for i in range(layers - 1):
        small_far(i).wait_send()
    for i in range(layers):
        target, far, near = share(i)

        @pl.when(target != rank)
        def _():
            far().wait_send()
    for which in range(2):
        for d in range(1, layers):
            @pl.when(layer + d < layers)
            def _():
                chain(which, True, layer + d).wait_send()

            @pl.when(layer - d >= 0)
            def _():
                chain(which, False, layer - d).wait_send()


def run_back(part, gw, go, small, n_dp):
    group, rows, width = part.shape
    cols = gw.shape[-1]
    layers = small.shape[0]
    own = small.shape[2]
    dma = pltpu.SemaphoreType.DMA
    shape = jax.ShapeDtypeStruct
    deep = pltpu.VMEM((layers, 3, group * own, cols), BF)
    flat = pltpu.VMEM((layers, own, width), BF)
    chain = dma((2, layers))
    tiny = small.shape[2:]
    return pl.pallas_call(
        functools.partial(back_kernel, n_dp, layers),
        out_shape=(
            shape((rows, width), F32), shape((3, own, width), F32),
            shape((own, width), F32), shape(tiny, F32),
        ),
        in_specs=[ANY] * 4,
        out_specs=(VMEM,) * 4,
        scratch_shapes=LayerSum.scratch(rows, width) + [
            pltpu.VMEM((3, layers, group * own, cols), BF), flat, deep, flat, deep, flat,
            pltpu.VMEM((group, 3, own, cols), BF),
            pltpu.VMEM((layers,) + tiny, F32), pltpu.VMEM((group - 1, layers) + tiny, F32),
            pltpu.VMEM((layers,) + tiny, F32), pltpu.VMEM((layers,) + tiny, F32),
            dma((1,)), dma((layers,)), dma((layers,)), dma((layers,)),
            chain, chain, chain, chain,
            dma((1,)), dma((group - 1,)), dma((group - 1,)),
            dma((1,)), dma((group - 1,)), dma((group - 1,)), dma((layers,)), dma((layers,)),
        ],
        compiler_params=comm_params(6),
    )(
        part, gw.reshape(3, layers, group * own, cols), go.reshape(layers, own, width), small
    )


class LayerTerms:
    def __init__(self, here, ranks, pick, land, send, recv):
        self.here, self.ranks, self.pick = here, ranks, pick
        self.land, self.send, self.recv = land, send, recv

    def copy(self, k):
        return remote(
            self.pick(self.ranks[k]), self.land.at[k], self.send.at[k], self.recv.at[k],
            peer(self.here, self.ranks[k]),
        )

    def begin(self):
        for k in range(len(self.ranks)):
            self.copy(k).start()

    def total(self, own):
        for k in range(len(self.ranks)):
            self.copy(k).wait_recv()
            own = own + self.land[k].astype(F32)
        return own

    def end(self):
        for k in range(len(self.ranks)):
            self.copy(k).wait_send()


def as_row(column):
    return jnp.broadcast_to(column, (column.shape[0], 128)).T[:1]


def as_column(row):
    return jnp.broadcast_to(row, (128, row.shape[1])).T[:, :1]


def row_sum(value):
    return jnp.sum(value, axis=1, keepdims=True)


def swap_halves(value):
    half = value.shape[1] // 2
    return jnp.concatenate([value[:, half:], value[:, :half]], axis=1)


def probabilities(q_rot, k_rot, scale):
    scores = dot_t(q_rot, k_rot) * scale
    later = (
        lax.broadcasted_iota(jnp.int32, scores.shape, 0)
        >= lax.broadcasted_iota(jnp.int32, scores.shape, 1)
    )
    scores = jnp.where(later, scores, -1e30)
    grown = jnp.exp(scores - jnp.max(scores, axis=1, keepdims=True))
    return grown / row_sum(grown)


def attend_kernel(
    n_dp, layers, seqs,
    x, gain, w, q_gain, k_gain, cosine, sine, wo, ffn_gain, router, hits, g_own,
    normed, q_raw, k_raw, v, q_rot, k_rot, mixed, stats,
    residual, res_unit, res_root, gates, x_out, g_all,
    part, squares, land, n_send, n_recv, out, p_send, p_recv,
    acc, sib, one, two, load_sem, l_send, l_recv, g_keep, gz_send, gz_recv, g_send, g_recv,
):
    here = Place(n_dp)
    group = 2 * n_dp
    ranks = others(here, group)
    greet(
        [peer(here, r) for r in ranks]
        + [here.at_layer(flip(here.layer, i, layers)) for i in range(1, layers)]
    )
    terms = LayerTerms(here, ranks, lambda r: squares, land, n_send, n_recv)
    rest = WideGather(here, layers, g_own, g_all, g_keep, gz_send, gz_recv, g_send, g_recv)
    job = LayerSum(here, part, acc, sib, one, two, load_sem, l_send, l_recv)
    last = layers - 1
    total, width = normed.shape
    rows_own = g_own.shape[0]
    cols = q_raw.shape[1]
    def seats(k):
        ref = g_all.at[here.layer, here.rank, :, pl.ds(width, g_own.shape[1] - width)]
        src = g_own.at[:, pl.ds(width, g_own.shape[1] - width)]
        return remote(src, ref, p_send.at[k], p_recv.at[k], peer(here, ranks[k]))

    rest.begin()
    for k in range(group - 1):
        seats(k).start()

    tile = 256
    squares[...] = jnp.zeros_like(squares)

    def project(t):
        at = slice(t * tile, (t + 1) * tile)
        value = x[at, :].astype(F32)
        root = lax.rsqrt(row_sum(value * value) / width + EPSILON)
        low = (value * root * gain[...]).astype(BF)
        normed[at, :] = low
        q, k = dot(low, w[0]), dot(low, w[1])
        q_raw[at, :] = q
        k_raw[at, :] = k
        v[at, :] = dot(low, w[2]).astype(BF)
        squares[0:1, at] = as_row(row_sum(q * q))
        squares[1:2, at] = as_row(row_sum(k * k))

    for t in range(total // tile):
        project(t)
    terms.begin()
    rest.pass_on(0)
    rest.enter(0)
    stats[...] = terms.total(squares[...])

    length = total // seqs
    for s in range(seqs):
        rows = slice(s * length, (s + 1) * length)
        roots = [
            as_column(lax.rsqrt(stats[i : i + 1, rows] / width + EPSILON)) for i in range(2)
        ]
        for h in range(0, cols, HEAD_DIM):
            head = slice(h, h + HEAD_DIM)
            turned = []
            for raw, root, scale, to in (
                (q_raw, roots[0], q_gain, q_rot), (k_raw, roots[1], k_gain, k_rot),
            ):
                value = raw[rows, head] * root * scale[:, head]
                value = (value * cosine[...] + swap_halves(value) * sine[...]).astype(BF)
                to[rows, head] = value
                turned.append(value)
            probs = probabilities(turned[0], turned[1], HEAD_DIM ** (-0.5)).astype(BF)
            mixed[rows, head] = dot(probs, v[rows, head]).astype(BF)
        if s == 0:
            rest.pass_on(1)
    size = part.shape[1]
    rest.forward(0)
    rest.enter(1)

    def project_out(b, c):
        value = mixed[pl.ds(pl.multiple_of(b * size, size), size), :]
        for n in range(0, width, STEP):
            part[b, :, n : n + STEP] = dot(value, wo[:, n : n + STEP]).astype(BF)
        return c

    lax.fori_loop(0, group, project_out, 0)

    job.begin()
    rest.across(0)
    for i in range(2, last):
        rest.pass_on(i)
    job.first()
    rest.forward(1)
    job.second()
    if last > 2:
        rest.enter(2)
    rest.across(1)
    job.third(out)

    at = pl.ds(pl.multiple_of(here.rank * rows_own, rows_own), rows_own)
    value = x[at, :].astype(F32) + out[...]
    residual[...] = value
    root = lax.rsqrt(row_sum(value * value) / width + EPSILON)
    unit = value * root
    res_unit[...] = unit
    res_root[...] = jnp.broadcast_to(root, res_root.shape)
    low = (unit * ffn_gain[...]).astype(BF)
    x_out[:, :width] = low
    logits = dot(low, router[...])
    chosen = hits[...] > 0.0
    top_logit = jnp.max(jnp.where(chosen, logits, -1e30), axis=1, keepdims=True)
    grown = jnp.where(chosen, jnp.exp(jnp.minimum(logits - top_logit, 0.0)), 0.0)
    shares = grown / row_sum(grown)
    gates[...] = shares
    high = shares.astype(BF).astype(F32)
    x_out[:, width:] = (high + swap_halves(shares - high)).astype(BF)
    for i in range(2, last):
        rest.forward(i)
        if i + 1 < last:
            rest.enter(i + 1)
        rest.across(i)
    rest.end()
    terms.end()
    for k in range(group - 1):
        seats(k).wait()


def run_attend(seqs, n_dp, layers, x, gain, w, *rest):
    g_own = rest[-1]
    total, width = x.shape
    cols = w.shape[-1]
    group = 2 * n_dp
    rows = total // group
    shape = jax.ShapeDtypeStruct
    dma = pltpu.SemaphoreType.DMA
    narrow, narrow_f = shape((total, cols), BF), shape((total, cols), F32)
    result = pl.pallas_call(
        functools.partial(attend_kernel, n_dp, layers, seqs),
        out_shape=(
            shape((total, width), BF), narrow_f, narrow_f, narrow, narrow, narrow, narrow,
            shape((8, total), F32), shape((rows, width), F32), shape((rows, width), F32),
            shape((rows, 128), F32), shape((rows, 128), F32), shape((rows, width + 128), BF),
            shape((layers, group) + g_own.shape, BF),
        ),
        in_specs=[VMEM] * 11 + [ANY],
        out_specs=(VMEM,) * 13 + (ANY,),
        scratch_shapes=[
            pltpu.VMEM((group, rows, width), BF), pltpu.VMEM((8, total), F32),
            pltpu.VMEM((group - 1, 8, total), F32), dma((group - 1,)), dma((group - 1,)),
            pltpu.VMEM((rows, width), F32), dma((group - 1,)), dma((group - 1,)),
        ] + LayerSum.scratch(rows, width) + [
            dma((1,)), dma((layers + 1,)), dma((layers,)), dma((layers, 10)), dma((layers, 10)),
        ],
        compiler_params=pltpu.CompilerParams(
            collective_id=2, has_side_effects=True, vmem_limit_bytes=56 * 2**20
        ),
    )(x, gain, w, *rest)
    return result


def attend_back_kernel(
    seqs, gao, wo, mixed, q_rot, k_rot, v, q_raw, k_raw, stats, q_gain, k_gain, cosine, sine,
    grad_wo, gq, gk, gv, gains, inner, grad_mixed,
):
    total, cols = q_raw.shape
    width = wo.shape[1]
    length = total // seqs
    scale = HEAD_DIM ** (-0.5)
    for n in range(0, width, STEP):
        grad_wo[:, n : n + STEP] = tdot(mixed[...], gao[:, n : n + STEP]).astype(BF)
    grad_mixed[...] = dot_t(gao[...], wo[...]).astype(BF)
    inner[...] = jnp.zeros_like(inner)
    gains[...] = jnp.zeros_like(gains)
    for s in range(seqs):
        rows = slice(s * length, (s + 1) * length)
        roots = [
            as_column(lax.rsqrt(stats[i : i + 1, rows] / width + EPSILON)) for i in range(2)
        ]
        inners = [jnp.zeros((length, 1), F32) for _ in range(2)]
        for h in range(0, cols, HEAD_DIM):
            head = slice(h, h + HEAD_DIM)
            q, k = q_rot[rows, head], k_rot[rows, head]
            probs = probabilities(q, k, scale)
            gm = grad_mixed[rows, head]
            gv[rows, head] = tdot(probs.astype(BF), gm).astype(BF)
            grad_probs = dot_t(gm, v[rows, head])
            delta = row_sum(probs * grad_probs)
            grad_scores = (probs * (grad_probs - delta)).astype(BF)
            for i, (turned, raw, gain, out) in enumerate((
                (dot(grad_scores, k) * scale, q_raw, q_gain, gq),
                (tdot(grad_scores, q) * scale, k_raw, k_gain, gk),
            )):
                back = turned * cosine[...] - swap_halves(turned) * sine[...]
                unit = raw[rows, head] * roots[i]
                gains[i : i + 1, head] += jnp.sum(back * unit, axis=0, keepdims=True)
                back = back * gain[:, head]
                out[rows, head] = back
                inners[i] = inners[i] + row_sum(back * unit)
        for i in range(2):
            inner[i : i + 1, rows] = as_row(inners[i])


def run_attend_back(seqs, gao, wo, mixed, q_rot, k_rot, v, q_raw, k_raw, stats, *rest):
    total, cols = q_raw.shape
    width = wo.shape[1]
    shape = jax.ShapeDtypeStruct
    return pl.pallas_call(
        functools.partial(attend_back_kernel, seqs),
        out_shape=(
            shape((cols, width), BF), shape((total, cols), F32), shape((total, cols), F32),
            shape((total, cols), BF), shape((8, cols), F32), shape((8, total), F32),
        ),
        in_specs=[VMEM] * 13,
        out_specs=(VMEM,) * 6,
        scratch_shapes=[pltpu.VMEM((total, cols), BF)],
        compiler_params=pltpu.CompilerParams(vmem_limit_bytes=48 * 2**20),
    )(gao, wo, mixed, q_rot, k_rot, v, q_raw, k_raw, stats, *rest)


def project_back_kernel(
    gq, gk, gv, q_raw, k_raw, stats, inner, w, normed, x, part, grad_w, gain, low,
):
    total, cols = gq.shape
    group, rows, width = part.shape
    for i, (grad, raw) in enumerate(((gq, q_raw), (gk, k_raw))):
        root = as_column(lax.rsqrt(stats[i : i + 1, :] / width + EPSILON))
        mean = as_column(inner[i : i + 1, :] / width)
        low[i] = (root * (grad[...] - raw[...] * root * mean)).astype(BF)
    low[2] = gv[...]
    gain[...] = jnp.zeros_like(gain)

    def block(b, c):
        at = pl.ds(pl.multiple_of(b * rows, rows), rows)
        value = x[at, :].astype(F32)
        root = lax.rsqrt(row_sum(value * value) / width + EPSILON)
        for n in range(0, width, STEP):
            cut = slice(n, n + STEP)
            total = dot_t(low[0, at, :], w[0, cut, :]) + dot_t(low[1, at, :], w[1, cut, :])
            total = total + dot_t(low[2, at, :], w[2, cut, :])
            part[b, :, cut] = total.astype(BF)
            unit = x[at, cut].astype(F32) * root
            gain[0:1, cut] += jnp.sum(total * unit, axis=0, keepdims=True)
        return c

    lax.fori_loop(0, group, block, 0)
    for n in range(0, width, STEP):
        cut = slice(n, n + STEP)
        rows_t = normed[:, cut]
        for i in range(3):
            grad_w[i, cut, :] = tdot(rows_t, low[i]).astype(BF)


def run_project_back(group, gq, gk, gv, q_raw, k_raw, stats, inner, w, normed, x):
    total, cols = gq.shape
    width = x.shape[1]
    shape = jax.ShapeDtypeStruct
    return pl.pallas_call(
        project_back_kernel,
        out_shape=(
            shape((group, total // group, width), BF), shape((3, width, cols), BF),
            shape((8, width), F32),
        ),
        in_specs=[VMEM] * 10,
        out_specs=(VMEM,) * 3,
        scratch_shapes=[pltpu.VMEM((3, total, cols), BF)],
        compiler_params=pltpu.CompilerParams(vmem_limit_bytes=56 * 2**20),
    )(gq, gk, gv, q_raw, k_raw, stats, inner, w, normed, x)


def ein(spec, left, right):
    return jnp.einsum(spec, left, right, preferred_element_type=F32)


def inv_rms(value):
    return lax.rsqrt(jnp.mean(value * value, axis=-1, keepdims=True) + EPSILON)


def build(n_ep, n_dp):
    n_dev = n_ep * n_dp
    group = 2 * n_dp
    layers = n_dev // group
    rows_of = [[z * group + r for r in range(group)] for z in range(layers)]

    def shards(
        layer_input, grad_out, attn_gain, w_q, w_k, w_v, q_gain, k_gain, w_o, ffn_gain,
        router, w_gate, w_up, w_down, routes,
    ):
        rows, width = layer_input.shape
        cols = width // group
        seqs = 2
        seq_len = rows * n_dp
        own = width // n_dev
        rank = (lax.axis_index("ep") % 2) * n_dp + lax.axis_index("dp")
        experts = router.shape[1]
        top = routes.shape[1]
        cap = 2 * rows * top // experts

        gains = jnp.stack([attn_gain, q_gain, k_gain, ffn_gain]).T
        small = jnp.concatenate(
            [router, gains, jnp.zeros((own, 128 - experts - 4), BF)], axis=1
        )
        group_input, qkv, wo, small, near_g = run_front(
            layer_input, w_q, w_k, w_v, w_o, small, grad_out, n_dp, n_dev
        )
        full_router = small[:, :experts]
        full_attn_gain = small[:, experts].astype(F32)
        full_ffn_gain = small[:, experts + 3].astype(F32)
        head_gains = lax.dynamic_slice_in_dim(small, rank * cols, cols, 0).astype(F32)
        q_gain_own, k_gain_own = head_gains[:, experts + 1], head_gains[:, experts + 2]

        picked = routes[:, :, None] == jnp.arange(experts, dtype=jnp.int32)
        hits = jnp.any(picked, axis=1)
        before = jnp.cumsum(hits.astype(jnp.int32), axis=0) - hits.astype(jnp.int32)
        place = jnp.where(hits, before, -1).astype(BF)
        place = jnp.pad(place.T, ((0, rows - experts), (0, 0)))
        sent = jnp.concatenate([grad_out, place], axis=1)
        hits_wide = jnp.pad(hits.astype(F32), ((0, 0), (0, 128 - experts)))
        router_wide = jnp.pad(full_router, ((0, 0), (0, 128 - experts)))
        half_dim = HEAD_DIM // 2
        frequency = 10000.0 ** (-jnp.arange(half_dim, dtype=F32) * 2.0 / HEAD_DIM)
        angle = jnp.arange(seq_len, dtype=F32)[:, None] * frequency[None, :]
        cosine = jnp.concatenate([jnp.cos(angle)] * 2, axis=-1)
        sine = jnp.concatenate([-jnp.sin(angle), jnp.sin(angle)], axis=-1)
        tables = (q_gain_own[None], k_gain_own[None], cosine, sine)
        (
            normed, q_raw, k_raw, v_low, q_rot, k_rot, mixed, stats,
            residual, res_n, res_root, gates, x_own, all_g,
        ) = run_attend(
            seqs, n_dp, layers, group_input, full_attn_gain[None], qkv, *tables, wo,
            full_ffn_gain[None], router_wide, hits_wide, sent,
        )
        all_g = all_g.reshape((n_dev,) + sent.shape)
        res_root, gates_dense, normed2 = res_root[:, :1], gates[:, :experts], x_own[:, :width]

        expert_sum, grad_sum, x_slots, g_slots, acts = run_experts(
            x_own, all_g, near_g, w_gate, w_up, w_down, n_dp, experts, cap
        )
        grad_w_gate, grad_w_up, grad_w_down = run_weights(x_slots, g_slots, acts)
        output = (residual + expert_sum).astype(BF)
        gate_grads = jnp.where(hits, grad_sum[:, width : width + experts], 0.0)
        weighted = jnp.sum(gates_dense * gate_grads, axis=-1, keepdims=True)
        grad_logits = (gates_dense * (gate_grads - weighted)).astype(BF)

        grad_n2 = grad_sum[:, :width] + ein("te,de->td", grad_logits, full_router)
        grad_y = grad_out.astype(F32)
        grad_ffn_gain = jnp.sum(grad_n2 * res_n, axis=0)
        dn = grad_n2 * full_ffn_gain
        grad_residual = grad_y + res_root * (dn - res_n * jnp.mean(dn * res_n, -1, keepdims=True))

        gao = lax.all_gather(
            grad_residual.astype(BF), AXES, axis=0, tiled=True, axis_index_groups=rows_of
        )
        grad_wo, gq, gk, gv, head_sums, inner = run_attend_back(
            seqs, gao, wo, mixed, q_rot, k_rot, v_low, q_raw, k_raw, stats, *tables
        )
        inner = layer_stats(inner, n_dp)
        part, grad_qkv, in_sums = run_project_back(
            group, gq, gk, gv, q_raw, k_raw, stats, inner, qkv, normed, group_input
        )

        def spread(part):
            return lax.dynamic_update_slice_in_dim(jnp.zeros((width,), F32), part, rank * cols, 0)

        small_grads = jnp.concatenate(
            [
                ein("te,td->ed", grad_logits, normed2),
                in_sums[:1], spread(head_sums[0])[None], spread(head_sums[1])[None],
                grad_ffn_gain[None], jnp.zeros((128 - experts - 4, width), F32),
            ]
        ).T
        grad_normed, grad_qkv, grad_o, small_grads = run_back(
            part, grad_qkv, grad_wo,
            small_grads.reshape(layers, group, own, 128), n_dp,
        )
        own_input = layer_input.astype(F32)
        in_root = inv_rms(own_input)
        in_n = own_input * in_root
        dn = grad_normed * full_attn_gain
        grad_input = grad_residual + in_root * (
            dn - in_n * jnp.mean(dn * in_n, -1, keepdims=True)
        )
        gain_grads = small_grads[:, experts : experts + 4]
        return (
            output, grad_input, gain_grads[:, 0], grad_qkv[0], grad_qkv[1], grad_qkv[2],
            gain_grads[:, 1], gain_grads[:, 2], grad_o, gain_grads[:, 3],
            small_grads[:, :experts], grad_w_gate, grad_w_up, grad_w_down,
        )

    return shards


def solution(mesh):
    row, vec = P(("ep", "dp"), None), P(("ep", "dp"))
    wide, deep = P("ep", None, "dp"), P("ep", "dp", None)
    in_specs = (
        row, row, vec, row, row, row, vec, vec, row, vec, row, wide, wide, deep, row,
    )
    out_specs = (
        row, row, vec, row, row, row, vec, vec, row, vec, row, wide, wide, deep,
    )
    shards = build(mesh.shape["ep"], mesh.shape["dp"])
    return jax.shard_map(shards, mesh=mesh, in_specs=in_specs, out_specs=out_specs, check_vma=False)
```

```python
import functools

import jax
import jax.numpy as jnp
from jax import lax
from jax.experimental import pallas as pl
from jax.experimental.pallas import tpu as pltpu
from jax.sharding import PartitionSpec as P

HEAD_DIM = 128
EPSILON = 1e-05
AXES = ("ep", "dp")
BF = jnp.bfloat16
F32 = jnp.float32
ANY = pl.BlockSpec(memory_space=pl.ANY)
VMEM = pl.BlockSpec(memory_space=pltpu.VMEM)
MESH = pl.DeviceIdType.MESH
STEP = 512
HOOKS = 8


def dot(left, right):
    return jnp.dot(left, right, preferred_element_type=F32)


def dot_t(left, right):
    return lax.dot_general(left, right, (((1,), (1,)), ((), ())), preferred_element_type=F32)


def tdot(left, right):
    return lax.dot_general(left, right, (((0,), (0,)), ((), ())), preferred_element_type=F32)


def flip(value, other, count):
    result, bit = 0, 1
    while bit < count:
        result = result + ((value // bit) % 2 + (other // bit) % 2) % 2 * bit
        bit *= 2
    return result


def nearby(z, i, count):
    both = jnp.minimum(z, count - 1 - z)
    first = 1 - 2 * (z % 2)
    paired = z + first * (1 - 2 * (i % 2)) * (i // 2 + 1)
    side = jnp.where(2 * z < count, 1, -1)
    single = z + side * (i - both + 1)
    return jnp.where(i == count - 1, z, jnp.where(i < 2 * both, paired, single))


class Place:
    def __init__(self, n_dp):
        ep, dp = lax.axis_index("ep"), lax.axis_index("dp")
        half = n_dp // 2
        self.n_dp, self.half = n_dp, half
        self.layer, self.y = ep // 2, ep % 2
        self.x, self.core = dp // 2, dp % 2
        self.rank = self.y * n_dp + dp
        self.ep, self.dp = ep, dp
        self.sibling = (ep, self.x * 2 + 1 - self.core)
        self.over_x = (ep, (1 - self.x) * 2 + self.core)
        self.over_y = (self.layer * 2 + 1 - self.y, dp)

    def at_layer(self, layer):
        return (layer * 2 + self.y, self.dp)


def greet(partners):
    barrier = pltpu.get_barrier_semaphore()
    for partner in partners:
        pl.semaphore_signal(barrier, inc=1, device_id=partner, device_id_type=MESH)
    pl.semaphore_wait(barrier, len(partners))


def experts_kernel(
    n_dp, experts,
    x_own, all_g, near_g, wg_hbm, wu_hbm, wd_hbm,
    out_sum, grad_sum, x_out, g_out, acts_out, all_x,
    sib_o, sib_g, one_o, one_g, two_o, two_g, z_o, z_g,
    wg, wu, wd, xs, gs, gate_rows, acts, xin, gin, stage_o, stage_g, acc_o, acc_g, tmp_o, tmp_g,
    leave_o, leave_g, pin, table,
    w_sem, in_sem, keep_sem, act_sem, own_sem, zx_send, zx_recv, ag_send, ag_recv,
    sib_send, sib_recv, one_send, one_recv, two_send, two_recv, z_send, z_recv, tmp_sem,
):
    n_dev, rows, wide = all_x.shape
    local, width, hid = wg.shape
    cap = xs.shape[2]
    group = 2 * n_dp
    layers = n_dev // group
    m = group * cap
    slots = xin.shape[0]
    half = width // 2
    here = Place(n_dp)
    rank, core, x, y = here.rank, here.core, here.x, here.y
    first = here.ep * local

    def remote(src, dst, send, recv, device):
        return pltpu.make_async_remote_copy(
            src_ref=src, dst_ref=dst, send_sem=send, recv_sem=recv,
            device_id=device, device_id_type=MESH,
        )

    def layer_of(i):
        return nearby(here.layer, i, layers)

    def weights():
        return [
            pltpu.make_async_copy(s, d, w_sem.at[i])
            for i, (s, d) in enumerate(((wg_hbm, wg), (wu_hbm, wu), (wd_hbm, wd)))
        ]

    def z_copy(block, up):
        at = all_x.at[block * group + rank]
        device = here.at_layer(here.layer + 1 if up else here.layer - 1)
        return remote(at, at, zx_send.at[block], zx_recv.at[block], device)

    def z_own(act):
        @pl.when(here.layer + 1 < layers)
        def _():
            act(own_z(True))

        @pl.when(here.layer >= 1)
        def _():
            act(own_z(False))

    def own_z(up):
        device = here.at_layer(here.layer + 1 if up else here.layer - 1)
        return remote(
            x_own, all_x.at[here.layer * group + rank],
            zx_send.at[here.layer if up else layers], zx_recv.at[here.layer], device,
        )

    def passes(i):
        block = layer_of(i)
        up = jnp.logical_and(block < here.layer, here.layer + 1 < layers)
        down = jnp.logical_and(block > here.layer, here.layer >= 1)
        return block, up, down

    def z_pass(i):
        block, up, down = passes(i)

        @pl.when(up)
        def _():
            z_copy(block, True).wait_recv()
            z_copy(block, True).start()

        @pl.when(down)
        def _():
            z_copy(block, False).wait_recv()
            z_copy(block, False).start()

    def z_arrive(i):
        block, up, down = passes(i)

        @pl.when(jnp.logical_not(jnp.logical_or(up, down)))
        def _():
            z_copy(block, True).wait_recv()

    def z_drain(i):
        block, up, down = passes(i)

        @pl.when(up)
        def _():
            z_copy(block, True).wait_send()

        @pl.when(down)
        def _():
            z_copy(block, False).wait_send()

    def own_copy():
        return pltpu.make_async_copy(x_own, all_x.at[here.layer * group + rank], own_sem.at[0])

    over_x_rank = y * n_dp + (1 - x) * 2 + core
    over_y_rank = (1 - y) * n_dp + x * 2 + core
    across_rank = (1 - y) * n_dp + (1 - x) * 2 + core
    first_half, second_half = pl.ds(0, half), pl.ds(half, wide - half)

    def gather_copy(i, kind):
        base = layer_of(i) * group
        which, cols, device = {
            0: (rank, first_half, here.over_x),
            1: (rank, second_half, here.over_x),
            2: (rank, first_half, here.over_y),
            3: (rank, second_half, here.over_y),
            4: (over_x_rank, first_half, here.over_y),
            5: (over_y_rank, second_half, here.over_x),
            6: (rank, pl.ds(0, wide), here.sibling),
            7: (over_x_rank, pl.ds(0, wide), here.sibling),
            8: (over_y_rank, pl.ds(0, wide), here.sibling),
            9: (across_rank, pl.ds(0, wide), here.sibling),
        }[kind]
        ref = all_x.at[base + which, :, cols]
        return remote(ref, ref, ag_send.at[i, kind], ag_recv.at[i, kind], device)

    def gather_a(i):
        @pl.when(i < layers - 1)
        def _():
            z_arrive(i)

        @pl.when(i == layers - 1)
        def _():
            own_copy().wait()

        for kind in (0, 3, 1, 2, 6):
            gather_copy(i, kind).start()

    def gather_b(i):
        for got, then in ((0, 4), (3, 5), (1, 7), (2, 8)):
            gather_copy(i, got).wait_recv()
            gather_copy(i, then).start()

    def gather_c(i):
        gather_copy(i, 4).wait_recv()
        gather_copy(i, 5).wait_recv()
        gather_copy(i, 9).start()

    def gather_d(i):
        for kind in (6, 7, 8, 9):
            gather_copy(i, kind).wait_recv()

    def sib_copy(i, q, slot):
        return (
            remote(stage_o.at[slot], sib_o.at[i, q], sib_send.at[0, slot], sib_recv.at[0, i, q],
                   here.sibling),
            remote(stage_g.at[slot], sib_g.at[i, q], sib_send.at[1, slot], sib_recv.at[1, i, q],
                   here.sibling),
        )

    def one_copy_o(i, j):
        return remote(acc_o.at[j * 2 + 1 - x], one_o.at[i, j], one_send.at[0, j],
                      one_recv.at[0, i, j], here.over_x)

    def one_copy_g(i, j):
        return remote(acc_g.at[(1 - y) * 2 + j], one_g.at[i, j], one_send.at[1, j],
                      one_recv.at[1, i, j], here.over_y)

    def two_copy(i):
        return (
            remote(acc_o.at[(1 - y) * 2 + x], two_o.at[i], two_send.at[0], two_recv.at[0, i],
                   here.over_y),
            remote(acc_g.at[y * 2 + 1 - x], two_g.at[i], two_send.at[1], two_recv.at[1, i],
                   here.over_x),
        )

    def out_copy(i):
        at, device = here.layer, here.at_layer(layer_of(i))
        return (
            remote(leave_o, z_o.at[at], z_send.at[0], z_recv.at[0, at], device),
            remote(leave_g, z_g.at[at], z_send.at[1], z_recv.at[1, at], device),
        )

    def fetch(src_o, src_g, slot):
        return (
            pltpu.make_async_copy(src_o, tmp_o.at[slot], tmp_sem.at[0, slot]),
            pltpu.make_async_copy(src_g, tmp_g.at[slot], tmp_sem.at[1, slot]),
        )

    def start(copies):
        for copy in copies:
            copy.start()

    def finish(copies):
        for copy in copies:
            copy.wait()

    def add(dst, q, tmp, slot):
        total = dst[q].astype(F32) + tmp[slot].astype(F32)
        dst[q] = total.astype(BF)

    def sum_one(i):
        o, g = one_copy_o(i, 1 - y), one_copy_g(i, 1 - x)
        o.wait_recv()
        g.wait_recv()
        copies = fetch(one_o.at[i, 1 - y], one_g.at[i, 1 - x], 0)
        start(copies)
        finish(copies)
        add(acc_o, (1 - y) * 2 + x, tmp_o, 0)
        add(acc_g, y * 2 + 1 - x, tmp_g, 0)
        start(two_copy(i))

    def sum_two(i):
        own = y * 2 + x
        one_copy_o(i, y).wait_recv()
        one_copy_g(i, x).wait_recv()
        ones = fetch(one_o.at[i, y], one_g.at[i, x], 0)
        start(ones)
        for copy in two_copy(i):
            copy.wait_recv()
        twos = fetch(two_o.at[i], two_g.at[i], 1)
        start(twos)
        finish(ones)
        finish(twos)

        @pl.when(i > 0)
        def _():
            for copy in out_copy(i - 1):
                copy.wait_send()

        for acc, tmp, leave in ((acc_o, tmp_o, leave_o), (acc_g, tmp_g, leave_g)):
            total = acc[own].astype(F32) + tmp[0].astype(F32) + tmp[1].astype(F32)
            leave[...] = total.astype(BF)
        for j in range(2):
            one_copy_o(i, j).wait_send()
            one_copy_g(i, j).wait_send()
        for copy in two_copy(i):
            copy.wait_send()

        @pl.when(i < layers - 1)
        def _():
            start(out_copy(i))

    start(weights())
    greet([here.over_x, here.over_y, here.sibling]
          + [here.at_layer(flip(here.layer, i, layers)) for i in range(1, layers)])
    own_copy().start()
    z_own(lambda copy: copy.start())
    z_pass(0)
    gather_a(0)
    z_pass(1)
    gather_b(0)
    for i in range(2, layers - 1):
        z_pass(i)
    gather_c(0)
    gather_a(1)

    def chunk(i, carry):
        base = layer_of(i) * group

        gather_d(i)

        def load(b, slot):
            return (
                pltpu.make_async_copy(all_x.at[base + b], xin.at[slot], in_sem.at[0, slot]),
                pltpu.make_async_copy(
                    all_g.at[base + b, pl.ds(0, experts), pl.ds(width, rows)], pin.at[slot],
                    in_sem.at[2, slot],
                ),
            )

        def load_g(b, slot, act):
            @pl.when(i < layers - 1)
            def _():
                act(pltpu.make_async_copy(
                    all_g.at[base + b, :, pl.ds(0, width)], gin.at[slot], in_sem.at[1, slot]
                ))

            @pl.when(i == layers - 1)
            def _():
                act(pltpu.make_async_copy(near_g.at[b], gin.at[slot], in_sem.at[1, slot]))

        def begin_load(b, slot):
            start(load(b, slot))
            load_g(b, slot, lambda copy: copy.start())

        for b in range(slots - 1):
            begin_load(b, b)

        def bring(b, c):
            slot = lax.rem(b, slots)
            finish(load(b, slot))
            load_g(b, slot, lambda copy: copy.wait())

            @pl.when(b + slots - 1 < group)
            def _():
                begin_load(b + slots - 1, lax.rem(b + slots - 1, slots))

            size = local * cap
            chooses = (
                lax.broadcasted_iota(jnp.int32, (size, experts), 1)
                == lax.broadcasted_iota(jnp.int32, (size, experts), 0) // cap + first
            )
            places = dot(jnp.where(chooses, 1.0, 0.0).astype(BF), pin[slot])
            seat = lax.broadcasted_iota(jnp.int32, (size, rows), 0) % cap
            hot = jnp.where(places == seat.astype(F32), 1.0, 0.0).astype(BF)
            table[b] = hot
            for src, dst in ((xin, xs), (gin, gs)):
                for n in range(0, width, STEP):
                    got = dot(hot, src[slot, :, n : n + STEP]).astype(BF)
                    dst[:, b, :, n : n + STEP] = got.reshape(local, cap, STEP)
            gates = dot(hot, xin[slot, :, width:wide])
            lanes = lax.broadcasted_iota(jnp.int32, gates.shape, 1) % experts
            expert = lax.broadcasted_iota(jnp.int32, gates.shape, 0) // cap + first
            gates = jnp.sum(jnp.where(lanes == expert, gates, 0.0), axis=1, keepdims=True)
            gate_rows[:, b] = jnp.broadcast_to(gates, (local * cap, 128)).reshape(local, cap, 128)
            return c

        lax.fori_loop(0, group, bring, 0)

        def keep(e):
            return (
                pltpu.make_async_copy(xs.at[e], x_out.at[e, pl.ds(base, group)], keep_sem.at[0, e]),
                pltpu.make_async_copy(gs.at[e], g_out.at[e, pl.ds(base, group)], keep_sem.at[1, e]),
            )

        def keep_acts(e, slot):
            return pltpu.make_async_copy(
                acts.at[slot], acts_out.at[:, e, pl.ds(base * cap, m)], act_sem.at[slot]
            )

        lax.fori_loop(0, local, lambda e, c: (start(keep(e)), c)[1], 0)

        @pl.when(i == 0)
        def _():
            finish(weights())

        def expert(e, c):
            def hook(number, when, action):
                @pl.when(jnp.logical_and(e == number * local // HOOKS, when))
                def _():
                    action()

            hook(6, i + 2 < layers, lambda: gather_a(i + 2))
            hook(4, i + 1 < layers, lambda: gather_b(i + 1))
            hook(7, i + 1 < layers, lambda: gather_c(i + 1))
            hook(4, i > 0, lambda: sum_one(i - 1))
            slot = lax.rem(e, 2)

            @pl.when(jnp.logical_or(i > 0, e >= 2))
            def _():
                keep_acts(e, slot).wait()

            xe = xs[e].reshape(m, width)
            ge = gs[e].reshape(m, width)
            gate_part = dot(xe, wg[e])
            up_part = dot(xe, wu[e])
            raw = dot_t(ge, wd[e])
            gate = gate_rows[e].reshape(m, 128)[:, :1]
            sig = 1.0 / (1.0 + jnp.exp(-gate_part))
            silu = gate_part * sig
            hidden = silu * up_part
            own = jnp.sum(hidden * raw, axis=1, keepdims=True)
            lanes = lax.broadcasted_iota(jnp.int32, (m, 128), 1)
            grad_hidden = raw * gate
            hg = (hidden * gate).astype(BF)
            dg = (grad_hidden * up_part * sig * (1.0 + gate_part * (1.0 - sig))).astype(BF)
            du = (grad_hidden * silu).astype(BF)
            gate_rows[e] = jnp.where(lanes == first + e, own, 0.0).reshape(group, cap, 128)
            acts[slot, 0] = hg
            acts[slot, 1] = dg
            acts[slot, 2] = du
            keep_acts(e, slot).start()
            finish(keep(e))
            for n in range(0, width, STEP):
                out = dot(hg, wd[e, :, n : n + STEP]).astype(BF)
                gs[e, :, :, n : n + STEP] = out.reshape(group, cap, STEP)
                back = dot_t(dg, wg[e, n : n + STEP, :]) + dot_t(du, wu[e, n : n + STEP, :])
                xs[e, :, :, n : n + STEP] = back.astype(BF).reshape(group, cap, STEP)
            return c

        lax.fori_loop(0, local, expert, 0)

        def combine(b, put_o, put_g):
            hot = table[b]
            for n in range(0, width, STEP):
                got = gs[:, b, :, n : n + STEP].reshape(local * cap, STEP)
                put_o(n, STEP, tdot(hot, got))
                got = xs[:, b, :, n : n + STEP].reshape(local * cap, STEP)
                put_g(n, STEP, tdot(hot, got))
            got = gate_rows[:, b].reshape(local * cap, 128).astype(BF)
            put_g(width, 128, tdot(hot, got))

        def square(k):
            return (y + 1 - k % 2) % 2, (x + 1 - k // 2) % 2

        def give(k, c):
            slot = lax.rem(k, 2)
            to_y, to_x = square(k)
            q = to_y * 2 + to_x

            @pl.when(jnp.logical_or(i > 0, k >= 2))
            def _():
                for copy in sib_copy(i, q, slot):
                    copy.wait_send()

            def put_o(n, size, value):
                stage_o[slot, :, pl.ds(n, size)] = value.astype(BF)

            def put_g(n, size, value):
                stage_g[slot, :, pl.ds(n, size)] = value.astype(BF)

            combine(q * 2 + 1 - core, put_o, put_g)
            start(sib_copy(i, q, slot))
            return c

        lax.fori_loop(0, 4, give, 0)

        def from_sibling(k):
            to_y, to_x = square(k)
            q = to_y * 2 + to_x
            return fetch(sib_o.at[i, q], sib_g.at[i, q], lax.rem(k, 2))

        def bring_sibling(k):
            to_y, to_x = square(k)
            for copy in sib_copy(i, to_y * 2 + to_x, 0):
                copy.wait_recv()
            start(from_sibling(k))

        @pl.when(i > 0)
        def _():
            sum_two(i - 1)

        bring_sibling(0)

        def hold(k, c):
            slot = lax.rem(k, 2)
            to_y, to_x = square(k)
            q = to_y * 2 + to_x

            @pl.when(k < 3)
            def _():
                bring_sibling(k + 1)

            finish(from_sibling(k))

            def put_o(n, size, value):
                cols = pl.ds(n, size)
                acc_o[q, :, cols] = (value + tmp_o[slot, :, cols].astype(F32)).astype(BF)

            def put_g(n, size, value):
                cols = pl.ds(n, size)
                acc_g[q, :, cols] = (value + tmp_g[slot, :, cols].astype(F32)).astype(BF)

            combine(q * 2 + core, put_o, put_g)

            @pl.when(k < 2)
            def _():
                one_copy_o(i, to_y).start()

            @pl.when(k % 2 == 0)
            def _():
                one_copy_g(i, to_x).start()

            return c

        lax.fori_loop(0, 4, hold, 0)
        return carry

    lax.fori_loop(0, layers, chunk, 0)
    last = layers - 1
    sum_one(last)
    sum_two(last)
    out_sum[...] = leave_o[...].astype(F32)
    grad_sum[...] = leave_g[...].astype(F32)

    def arrive(i):
        at = layer_of(i)
        for copy in (
            remote(leave_o, z_o.at[at], z_send.at[0], z_recv.at[0, at], here.sibling),
            remote(leave_g, z_g.at[at], z_send.at[1], z_recv.at[1, at], here.sibling),
        ):
            copy.wait_recv()
        start(fetch(z_o.at[at], z_g.at[at], i % 2))

    arrive(0)
    for i in range(last):
        if i + 1 < last:
            arrive(i + 1)
        finish(fetch(z_o.at[layer_of(i)], z_g.at[layer_of(i)], i % 2))
        out_sum[...] += tmp_o[i % 2].astype(F32)
        grad_sum[...] += tmp_g[i % 2].astype(F32)
    for slot in range(2):
        for copy in sib_copy(last, slot, slot):
            copy.wait_send()
        pltpu.make_async_copy(
            acts.at[slot], acts_out.at[:, 0, pl.ds(0, m)], act_sem.at[slot]
        ).wait()

    def drain(i, c):
        for kind in range(10):
            gather_copy(i, kind).wait_send()
        return c

    lax.fori_loop(0, layers, drain, 0)
    z_own(lambda copy: copy.wait_send())
    for i in range(last):
        z_drain(i)


def run_experts(x_own, all_g, near_g, wg, wu, wd, n_dp, experts, cap):
    rows, wide = x_own.shape
    n_dev = all_g.shape[0]
    local, width, hid = wg.shape
    group = 2 * n_dp
    layers = n_dev // group
    m = group * cap
    wide_g = width + 128
    slots = 3
    dma = pltpu.SemaphoreType.DMA
    shape = jax.ShapeDtypeStruct
    slot_rows = shape((local, n_dev, cap, width), BF)
    flops = 12 * n_dev * cap * local * width * hid
    result = pl.pallas_call(
        functools.partial(experts_kernel, n_dp, experts),
        out_shape=(
            shape((rows, width), F32), shape((rows, wide_g), F32),
            slot_rows, slot_rows,
            shape((3, local, n_dev * cap, hid), BF),
            shape((n_dev, rows, wide), BF),
            shape((layers, 4, rows, width), BF), shape((layers, 4, rows, wide_g), BF),
            shape((layers, 2, rows, width), BF), shape((layers, 2, rows, wide_g), BF),
            shape((layers, rows, width), BF), shape((layers, rows, wide_g), BF),
            shape((layers, rows, width), BF), shape((layers, rows, wide_g), BF),
        ),
        in_specs=[ANY] * 6,
        out_specs=(VMEM, VMEM) + (ANY,) * 12,
        scratch_shapes=[
            pltpu.VMEM(wg.shape, BF), pltpu.VMEM(wu.shape, BF), pltpu.VMEM(wd.shape, BF),
            pltpu.VMEM((local, group, cap, width), BF),
            pltpu.VMEM((local, group, cap, width), BF),
            pltpu.VMEM((local, group, cap, 128), F32),
            pltpu.VMEM((2, 3, m, hid), BF),
            pltpu.VMEM((slots, rows, wide), BF),
            pltpu.VMEM((slots, rows, width), BF),
            pltpu.VMEM((2, rows, width), BF), pltpu.VMEM((2, rows, wide_g), BF),
            pltpu.VMEM((4, rows, width), BF), pltpu.VMEM((4, rows, wide_g), BF),
            pltpu.VMEM((2, rows, width), BF), pltpu.VMEM((2, rows, wide_g), BF),
            pltpu.VMEM((rows, width), BF), pltpu.VMEM((rows, wide_g), BF),
            pltpu.VMEM((slots, experts, rows), BF), pltpu.VMEM((group, local * cap, rows), BF),
            dma((3,)), dma((3, slots)), dma((2, local)), dma((2,)), dma((1,)),
            dma((layers + 1,)), dma((layers,)), dma((layers, 10)), dma((layers, 10)),
            dma((2, 2)), dma((2, layers, 4)), dma((2, 2)), dma((2, layers, 2)),
            dma((2,)), dma((2, layers)), dma((2,)), dma((2, layers)), dma((2, 2)),
        ],
        compiler_params=pltpu.CompilerParams(
            collective_id=1, has_side_effects=True, vmem_limit_bytes=64 * 2**20
        ),
        cost_estimate=pl.CostEstimate(flops=flops, bytes_accessed=200 * 2**20, transcendentals=0),
    )(x_own, all_g, near_g, wg, wu, wd)
    return result[:5]


def weights_kernel(x, g, acts, grad_g, grad_u, grad_d):
    first = pl.program_id(1) == 0
    xe, ge = x[0], g[0]

    def put(ref, n, size, value, axis):
        at = (0, pl.ds(n, size), slice(None)) if axis == 0 else (0, slice(None), pl.ds(n, size))

        @pl.when(first)
        def _():
            ref[at] = value

        @pl.when(jnp.logical_not(first))
        def _():
            ref[at] += value

    hg, dg, du = acts[0, 0], acts[1, 0], acts[2, 0]
    for n in range(0, xe.shape[1], STEP):
        part = xe[:, n : n + STEP]
        put(grad_g, n, STEP, tdot(part, dg), 0)
        put(grad_u, n, STEP, tdot(part, du), 0)
        put(grad_d, n, STEP, tdot(hg, ge[:, n : n + STEP]), 1)


def run_weights(x_slots, g_slots, acts):
    local, n_dev, cap, width = x_slots.shape
    hid = acts.shape[-1]
    total = n_dev * cap
    tile = min(1024, total)
    x_slots = x_slots.reshape(local, total, width)
    g_slots = g_slots.reshape(local, total, width)
    row = pl.BlockSpec((1, tile, width), lambda e, k: (e, k, 0))
    wide = pl.BlockSpec((1, width, hid), lambda e, k: (e, 0, 0))
    deep = pl.BlockSpec((1, hid, width), lambda e, k: (e, 0, 0))
    return pl.pallas_call(
        weights_kernel,
        grid=(local, total // tile),
        out_shape=(
            jax.ShapeDtypeStruct((local, width, hid), F32),
            jax.ShapeDtypeStruct((local, width, hid), F32),
            jax.ShapeDtypeStruct((local, hid, width), F32),
        ),
        in_specs=[row, row, pl.BlockSpec((3, 1, tile, hid), lambda e, k: (0, e, k, 0))],
        out_specs=(wide, wide, deep),
        compiler_params=pltpu.CompilerParams(vmem_limit_bytes=60 * 2**20),
        cost_estimate=pl.CostEstimate(
            flops=6 * local * total * width * hid, bytes_accessed=130 * 2**20, transcendentals=0
        ),
    )(x_slots, g_slots, acts)


def peer(here, rank):
    return (here.layer * 2 + rank // here.n_dp, rank % here.n_dp)


def others(here, group):
    return [lax.rem(here.rank + k, group) for k in range(1, group)]


def remote(src, dst, send, recv, device):
    return pltpu.make_async_remote_copy(
        src_ref=src, dst_ref=dst, send_sem=send, recv_sem=recv,
        device_id=device, device_id_type=MESH,
    )


class LayerGather:
    def __init__(self, here, own, buf, own_sem, send, recv):
        self.here, self.own, self.buf = here, own, buf
        self.own_sem, self.send, self.recv = own_sem, send, recv

    def copy(self, kind):
        here, buf = self.here, self.buf
        wide = buf.shape[-1]
        half = wide // 256 * 128
        low, high, full = pl.ds(0, half), pl.ds(half, wide - half), pl.ds(0, wide)
        n_dp, x, y, core = here.n_dp, here.x, here.y, here.core
        over_x = y * n_dp + (1 - x) * 2 + core
        over_y = (1 - y) * n_dp + x * 2 + core
        across = (1 - y) * n_dp + (1 - x) * 2 + core
        which, cols, device = {
            0: (here.rank, low, here.over_x),
            1: (here.rank, high, here.over_x),
            2: (here.rank, low, here.over_y),
            3: (here.rank, high, here.over_y),
            4: (over_x, low, here.over_y),
            5: (over_y, high, here.over_x),
            6: (here.rank, full, here.sibling),
            7: (over_x, full, here.sibling),
            8: (over_y, full, here.sibling),
            9: (across, full, here.sibling),
        }[kind]
        dst = buf.at[which, :, cols]
        src = self.own.at[:, cols] if kind in (0, 1, 2, 3, 6) else dst
        return remote(src, dst, self.send.at[kind], self.recv.at[kind], device)

    def keep(self):
        return pltpu.make_async_copy(self.own, self.buf.at[self.here.rank], self.own_sem.at[0])

    def begin(self):
        self.keep().start()
        for kind in (0, 3, 1, 2, 6):
            self.copy(kind).start()

    def forward(self):
        for got, then in ((0, 4), (3, 5), (1, 7), (2, 8)):
            self.copy(got).wait_recv()
            self.copy(then).start()

    def across(self):
        self.copy(4).wait_recv()
        self.copy(5).wait_recv()
        self.copy(9).start()

    def end(self):
        for kind in (6, 7, 8, 9):
            self.copy(kind).wait_recv()
        for kind in range(10):
            self.copy(kind).wait_send()
        self.keep().wait()


class WideGather:
    def __init__(self, here, layers, own, buf, own_sem, z_send, z_recv, send, recv):
        self.here, self.layers, self.own, self.buf = here, layers, own, buf
        self.own_sem, self.z_send, self.z_recv = own_sem, z_send, z_recv
        self.send, self.recv = send, recv
        self.last = layers - 1

    def layer_of(self, i):
        return nearby(self.here.layer, i, self.layers)

    def keep(self):
        return pltpu.make_async_copy(
            self.own, self.buf.at[self.here.layer, self.here.rank], self.own_sem.at[0]
        )

    def over_z(self, block, up, own=False):
        here = self.here
        at = self.buf.at[block, here.rank]
        return remote(
            self.own if own else at, at,
            self.z_send.at[self.layers if own and not up else block], self.z_recv.at[block],
            here.at_layer(here.layer + 1 if up else here.layer - 1),
        )

    def own_z(self, act):
        layer = self.here.layer

        @pl.when(layer + 1 < self.layers)
        def _():
            act(self.over_z(layer, True, True))

        @pl.when(layer >= 1)
        def _():
            act(self.over_z(layer, False, True))

    def passes(self, i):
        layer, block = self.here.layer, self.layer_of(i)
        up = jnp.logical_and(block < layer, layer + 1 < self.layers)
        down = jnp.logical_and(block > layer, layer >= 1)
        return block, up, down

    def pass_on(self, i):
        block, up, down = self.passes(i)

        @pl.when(up)
        def _():
            self.over_z(block, True).wait_recv()
            self.over_z(block, True).start()

        @pl.when(down)
        def _():
            self.over_z(block, False).wait_recv()
            self.over_z(block, False).start()

    def copy(self, i, kind):
        here = self.here
        block = self.buf.at[self.layer_of(i)]
        job = LayerGather(here, block.at[here.rank], block, None, self.send.at[i], self.recv.at[i])
        return job.copy(kind)

    def begin(self):
        self.keep().start()
        self.own_z(lambda copy: copy.start())

    def enter(self, i):
        block, up, down = self.passes(i)

        @pl.when(jnp.logical_not(jnp.logical_or(up, down)))
        def _():
            self.over_z(block, True).wait_recv()

        for kind in (0, 3, 1, 2, 6):
            self.copy(i, kind).start()

    def forward(self, i):
        for got, then in ((0, 4), (3, 5), (1, 7), (2, 8)):
            self.copy(i, got).wait_recv()
            self.copy(i, then).start()

    def across(self, i):
        self.copy(i, 4).wait_recv()
        self.copy(i, 5).wait_recv()
        self.copy(i, 9).start()

    def end(self):
        self.keep().wait()
        for i in range(self.last):
            for kind in (6, 7, 8, 9):
                self.copy(i, kind).wait_recv()
        for i in range(self.last):
            for kind in range(10):
                self.copy(i, kind).wait_send()
        self.own_z(lambda copy: copy.wait_send())
        for i in range(self.last):
            block, up, down = self.passes(i)

            @pl.when(up)
            def _():
                self.over_z(block, True).wait_send()

            @pl.when(down)
            def _():
                self.over_z(block, False).wait_send()


class LayerSum:
    def __init__(self, here, part, acc, sib, one, two, load, send, recv):
        self.here, self.part, self.acc, self.sib = here, part, acc, sib
        self.one, self.two, self.load_sem, self.send, self.recv = one, two, load, send, recv
        wide = acc.shape[-1]
        half = wide // 256 * 128
        self.cols = (pl.ds(0, half), pl.ds(half, wide - half))

    def load(self, q):
        return pltpu.make_async_copy(
            self.part.at[q * 2 + self.here.core], self.acc.at[q], self.load_sem.at[q]
        )

    def copy(self, kind):
        here, acc = self.here, self.acc
        x, y = here.x, here.y
        low, high = self.cols
        if kind < 4:
            src, dst = self.part.at[kind * 2 + 1 - here.core], self.sib.at[kind]
            device = here.sibling
        elif kind < 6:
            j = kind - 4
            src, dst, device = acc.at[j * 2 + 1 - x, :, low], self.one.at[j, :, low], here.over_x
        elif kind < 8:
            j = kind - 6
            src, dst = acc.at[(1 - y) * 2 + j, :, high], self.one.at[j, :, high]
            device = here.over_y
        elif kind == 8:
            src, dst, device = acc.at[(1 - y) * 2 + x, :, low], self.two.at[:, low], here.over_y
        else:
            src, dst, device = acc.at[y * 2 + 1 - x, :, high], self.two.at[:, high], here.over_x
        return remote(src, dst, self.send.at[kind], self.recv.at[kind], device)

    def add(self, q, cols, got):
        total = self.acc[q, :, cols].astype(F32) + got.astype(F32)
        self.acc[q, :, cols] = total.astype(BF)

    def begin(self):
        for q in range(4):
            self.copy(q).start()
            self.load(q).start()

    def first(self):
        for q in range(4):
            self.load(q).wait()
            self.copy(q).wait_recv()
            for cols in self.cols:
                self.add(q, cols, self.sib[q, :, cols])
        for kind in (4, 5, 6, 7):
            self.copy(kind).start()

    def second(self):
        x, y = self.here.x, self.here.y
        low, high = self.cols
        for j in range(2):
            self.copy(4 + j).wait_recv()
            self.add(j * 2 + x, low, self.one[j, :, low])
            self.copy(6 + j).wait_recv()
            self.add(y * 2 + j, high, self.one[j, :, high])
        self.copy(8).start()
        self.copy(9).start()

    def third(self, out):
        own = self.here.y * 2 + self.here.x
        for kind, cols in zip((8, 9), self.cols):
            self.copy(kind).wait_recv()
            out[:, cols] = self.acc[own, :, cols].astype(F32) + self.two[:, cols].astype(F32)
        for kind in range(10):
            self.copy(kind).wait_send()

    @staticmethod
    def scratch(rows, wide):
        return [
            pltpu.VMEM((4, rows, wide), BF), pltpu.VMEM((4, rows, wide), BF),
            pltpu.VMEM((2, rows, wide), BF), pltpu.VMEM((rows, wide), BF),
            pltpu.SemaphoreType.DMA((4,)),
            pltpu.SemaphoreType.DMA((10,)), pltpu.SemaphoreType.DMA((10,)),
        ]


def comm_params(number):
    return pltpu.CompilerParams(
        collective_id=number, has_side_effects=True, vmem_limit_bytes=48 * 2**20
    )


def front_kernel(
    n_dp, layers, x_own, w_q, w_k, w_v, w_o, small, g_own,
    x_all, qkv, wo, small_all, g_near, wo_col,
    own_sem, x_send, x_recv, a_keep, a_send, a_recv, up_send, up_recv, down_send, down_recv,
    o_keep, o_send, o_recv, s_send, s_recv, t_send, t_recv, g_keep, g_send, g_recv,
):
    here = Place(n_dp)
    group = 2 * n_dp
    layer, rank = here.layer, here.rank
    own = w_q.shape[0]
    cols = qkv.shape[-1]
    ranks = others(here, group)
    away = [flip(layer, i, layers) for i in range(1, layers)]
    greet([peer(here, r) for r in ranks] + [here.at_layer(z) for z in away])
    gather = LayerGather(here, x_own, x_all, own_sem, x_send, x_recv)
    cotangent = LayerGather(here, g_own, g_near, g_keep, g_send, g_recv)
    weights = (w_q, w_k, w_v)

    def rows_at(index):
        return pl.ds(pl.multiple_of(index * own, own), own)

    def block_cols(index):
        return pl.ds(pl.multiple_of(index * cols, cols), cols)

    def swap(w, k):
        return remote(
            weights[w].at[:, block_cols(ranks[k])], qkv.at[w, layer, rows_at(rank)],
            a_send.at[w, k], a_recv.at[w, k], peer(here, ranks[k]),
        )

    def swap_own(w):
        return pltpu.make_async_copy(
            weights[w].at[:, block_cols(rank)], qkv.at[w, layer, rows_at(rank)], a_keep.at[w]
        )

    def small_out(i):
        ref = small_all.at[layer, rank]
        return remote(small, ref, s_send.at[i], s_recv.at[i], here.at_layer(away[i]))

    def small_keep():
        return pltpu.make_async_copy(small, small_all.at[layer, rank], a_keep.at[3])

    def small_share(k):
        ref = small_all.at[:, rank]
        return remote(ref, ref, t_send.at[k], t_recv.at[k], peer(here, ranks[k]))

    def o_own():
        return pltpu.make_async_copy(w_o, wo_col.at[layer], a_keep.at[4])

    for w in range(3):
        swap_own(w).start()
        for k in range(group - 1):
            swap(w, k).start()
    o_own().start()
    small_keep().start()
    for i in range(layers - 1):
        small_out(i).start()
    gather.begin()
    for w in range(3):
        swap_own(w).wait()
        for k in range(group - 1):
            swap(w, k).wait_recv()
    o_own().wait()

    def chain(which, up, s):
        block = layer - s if up else layer + s
        ref = qkv.at[:, block] if which == 0 else wo_col.at[block]
        device = here.at_layer(layer + 1 if up else layer - 1)
        sems = (up_send, up_recv) if up else (down_send, down_recv)
        return remote(ref, ref, sems[0].at[which, s], sems[1].at[which, s], device)

    def step(which, s, wait):
        for up in (True, False):
            leaves = (
                jnp.logical_and(layer + 1 < layers, layer - s >= 0) if up
                else jnp.logical_and(layer >= 1, layer + s < layers)
            )
            comes = layer - 1 - s >= 0 if up else layer + 1 + s < layers
            if wait:
                @pl.when(comes)
                def _():
                    chain(which, up, s).wait_recv()
            else:
                @pl.when(leaves)
                def _():
                    chain(which, up, s).start()

    step(0, 0, False)
    gather.forward()
    step(1, 0, False)
    gather.across()
    small_keep().wait()
    for i in range(layers - 1):
        small_out(i).wait_recv()
    for k in range(group - 1):
        small_share(k).start()
    cotangent.begin()
    for s in range(layers - 1):
        step(0, s, True)
        if s + 1 < layers - 1:
            step(0, s + 1, False)
        if s == 0:
            cotangent.forward()
        step(1, s, True)
        if s + 1 < layers - 1:
            step(1, s + 1, False)
        if s == 0:
            cotangent.across()

    def share(z):
        number = z * group + rank
        target, index = number // layers, number % layers

        def far():
            return remote(
                wo_col.at[z], wo.at[index], o_send.at[z], o_recv.at[index], peer(here, target)
            )

        def near():
            return pltpu.make_async_copy(wo_col.at[z], wo.at[index], o_keep.at[index])

        return target, far, near

    def source(index):
        number = rank * layers + index
        return number % group

    for z in range(layers):
        target, far, near = share(z)

        @pl.when(target != rank)
        def _():
            far().start()

        @pl.when(target == rank)
        def _():
            near().start()

    for index in range(layers):
        @pl.when(source(index) != rank)
        def _():
            remote(
                wo_col.at[0], wo.at[index], o_send.at[0], o_recv.at[index], here.sibling
            ).wait_recv()

        @pl.when(source(index) == rank)
        def _():
            pltpu.make_async_copy(wo_col.at[0], wo.at[index], o_keep.at[index]).wait()

    gather.end()
    cotangent.end()
    for k in range(group - 1):
        small_share(k).wait_recv()
    for w in range(3):
        for k in range(group - 1):
            swap(w, k).wait_send()
    for i in range(layers - 1):
        small_out(i).wait_send()
    for k in range(group - 1):
        small_share(k).wait_send()
    for z in range(layers):
        target, far, near = share(z)

        @pl.when(target != rank)
        def _():
            far().wait_send()

    for which in range(2):
        for s in range(layers - 1):
            @pl.when(jnp.logical_and(layer + 1 < layers, layer - s >= 0))
            def _():
                chain(which, True, s).wait_send()

            @pl.when(jnp.logical_and(layer >= 1, layer + s < layers))
            def _():
                chain(which, False, s).wait_send()


def run_front(x_own, w_q, w_k, w_v, w_o, small, g_own, n_dp, n_dev):
    rows, width = x_own.shape
    own = w_q.shape[0]
    group = 2 * n_dp
    layers = n_dev // group
    cols = width // group
    dma = pltpu.SemaphoreType.DMA
    shape = jax.ShapeDtypeStruct
    chain = dma((2, layers))
    result = pl.pallas_call(
        functools.partial(front_kernel, n_dp, layers),
        out_shape=(
            shape((group, rows, width), BF),
            shape((3, layers, group * own, cols), BF),
            shape((layers, own, width), BF),
            shape((layers, group) + small.shape, BF),
            shape((group, rows, width), BF),
            shape((layers, own, width), BF),
        ),
        in_specs=[ANY] * 7,
        out_specs=(ANY,) * 6,
        scratch_shapes=[
            dma((1,)), dma((10,)), dma((10,)), dma((5,)),
            dma((3, group - 1)), dma((3, group - 1)), chain, chain, chain, chain,
            dma((layers,)), dma((layers,)), dma((layers,)),
            dma((layers,)), dma((layers,)), dma((group,)), dma((group,)),
            dma((1,)), dma((10,)), dma((10,)),
        ],
        compiler_params=pltpu.CompilerParams(
            collective_id=5, has_side_effects=True, vmem_limit_bytes=64 * 2**20
        ),
    )(x_own, w_q, w_k, w_v, w_o, small, g_own)
    x_all, qkv, wo, small_all, g_near, _ = result
    return (
        x_all.reshape(group * rows, width), qkv.reshape(3, width, cols),
        wo.reshape(cols, width), small_all.reshape(width, -1), g_near,
    )


class LayerTerms:
    def __init__(self, here, ranks, pick, land, send, recv):
        self.here, self.ranks, self.pick = here, ranks, pick
        self.land, self.send, self.recv = land, send, recv

    def copy(self, k):
        return remote(
            self.pick(self.ranks[k]), self.land.at[k], self.send.at[k], self.recv.at[k],
            peer(self.here, self.ranks[k]),
        )

    def begin(self):
        for k in range(len(self.ranks)):
            self.copy(k).start()

    def total(self, own):
        for k in range(len(self.ranks)):
            self.copy(k).wait_recv()
            own = own + self.land[k].astype(F32)
        return own

    def end(self):
        for k in range(len(self.ranks)):
            self.copy(k).wait_send()


class ColumnTerms:
    def __init__(self, here, layers, pick, land, send, recv):
        self.here, self.pick = here, pick
        self.away = [flip(here.layer, i, layers) for i in range(1, layers)]
        self.land, self.send, self.recv = land, send, recv

    def copy(self, i):
        return remote(
            self.pick(self.away[i]), self.land.at[i], self.send.at[i], self.recv.at[i],
            self.here.at_layer(self.away[i]),
        )

    def begin(self):
        for i in range(len(self.away)):
            self.copy(i).start()

    def total(self, own):
        for i in range(len(self.away)):
            self.copy(i).wait_recv()
            own = own + self.land[i].astype(F32)
        return own

    def end(self):
        for i in range(len(self.away)):
            self.copy(i).wait_send()


def as_row(column):
    return jnp.broadcast_to(column, (column.shape[0], 128)).T[:1]


def as_column(row):
    return jnp.broadcast_to(row, (128, row.shape[1])).T[:, :1]


def row_sum(value):
    return jnp.sum(value, axis=1, keepdims=True)


def swap_halves(value):
    half = value.shape[1] // 2
    return jnp.concatenate([value[:, half:], value[:, :half]], axis=1)


def probabilities(q_rot, k_rot, scale):
    scores = dot_t(q_rot, k_rot) * scale
    later = (
        lax.broadcasted_iota(jnp.int32, scores.shape, 0)
        >= lax.broadcasted_iota(jnp.int32, scores.shape, 1)
    )
    scores = jnp.where(later, scores, -1e30)
    grown = jnp.exp(scores - jnp.max(scores, axis=1, keepdims=True))
    return grown / row_sum(grown)


def attend_kernel(
    n_dp, layers, seqs,
    x, gain, w, q_gain, k_gain, cosine, sine, wo, ffn_gain, router, hits, g_own,
    normed, q_raw, k_raw, v, q_rot, k_rot, mixed, stats,
    residual, res_unit, res_root, gates, x_out, g_all,
    part, squares, land, n_send, n_recv, out, p_send, p_recv,
    acc, sib, one, two, load_sem, l_send, l_recv, g_keep, gz_send, gz_recv, g_send, g_recv,
):
    here = Place(n_dp)
    group = 2 * n_dp
    ranks = others(here, group)
    greet(
        [peer(here, r) for r in ranks]
        + [here.at_layer(flip(here.layer, i, layers)) for i in range(1, layers)]
    )
    terms = LayerTerms(here, ranks, lambda r: squares, land, n_send, n_recv)
    rest = WideGather(here, layers, g_own, g_all, g_keep, gz_send, gz_recv, g_send, g_recv)
    job = LayerSum(here, part, acc, sib, one, two, load_sem, l_send, l_recv)
    last = layers - 1
    total, width = normed.shape
    rows_own = g_own.shape[0]
    cols = q_raw.shape[1]
    def seats(k):
        ref = g_all.at[here.layer, here.rank, :, pl.ds(width, g_own.shape[1] - width)]
        src = g_own.at[:, pl.ds(width, g_own.shape[1] - width)]
        return remote(src, ref, p_send.at[k], p_recv.at[k], peer(here, ranks[k]))

    rest.begin()
    for k in range(group - 1):
        seats(k).start()

    tile = 256
    squares[...] = jnp.zeros_like(squares)

    def project(t):
        at = slice(t * tile, (t + 1) * tile)
        value = x[at, :].astype(F32)
        root = lax.rsqrt(row_sum(value * value) / width + EPSILON)
        low = (value * root * gain[...]).astype(BF)
        normed[at, :] = low
        q, k = dot(low, w[0]), dot(low, w[1])
        q_raw[at, :] = q
        k_raw[at, :] = k
        v[at, :] = dot(low, w[2]).astype(BF)
        squares[0:1, at] = as_row(row_sum(q * q))
        squares[1:2, at] = as_row(row_sum(k * k))

    for t in range(total // tile):
        project(t)
    terms.begin()
    rest.pass_on(0)
    rest.enter(0)
    stats[...] = terms.total(squares[...])

    length = total // seqs
    for s in range(seqs):
        rows = slice(s * length, (s + 1) * length)
        roots = [
            as_column(lax.rsqrt(stats[i : i + 1, rows] / width + EPSILON)) for i in range(2)
        ]
        for h in range(0, cols, HEAD_DIM):
            head = slice(h, h + HEAD_DIM)
            turned = []
            for raw, root, scale, to in (
                (q_raw, roots[0], q_gain, q_rot), (k_raw, roots[1], k_gain, k_rot),
            ):
                value = raw[rows, head] * root * scale[:, head]
                value = (value * cosine[...] + swap_halves(value) * sine[...]).astype(BF)
                to[rows, head] = value
                turned.append(value)
            probs = probabilities(turned[0], turned[1], HEAD_DIM ** (-0.5)).astype(BF)
            mixed[rows, head] = dot(probs, v[rows, head]).astype(BF)
        if s == 0:
            rest.pass_on(1)
    size = part.shape[1]
    rest.forward(0)
    rest.enter(1)

    def project_out(b, c):
        value = mixed[pl.ds(pl.multiple_of(b * size, size), size), :]
        for n in range(0, width, STEP):
            part[b, :, n : n + STEP] = dot(value, wo[:, n : n + STEP]).astype(BF)
        return c

    lax.fori_loop(0, group, project_out, 0)

    job.begin()
    rest.across(0)
    for i in range(2, last):
        rest.pass_on(i)
    job.first()
    rest.forward(1)
    job.second()
    if last > 2:
        rest.enter(2)
    rest.across(1)
    job.third(out)

    at = pl.ds(pl.multiple_of(here.rank * rows_own, rows_own), rows_own)
    value = x[at, :].astype(F32) + out[...]
    residual[...] = value
    root = lax.rsqrt(row_sum(value * value) / width + EPSILON)
    unit = value * root
    res_unit[...] = unit
    res_root[...] = jnp.broadcast_to(root, res_root.shape)
    low = (unit * ffn_gain[...]).astype(BF)
    x_out[:, :width] = low
    logits = dot(low, router[...])
    chosen = hits[...] > 0.0
    top_logit = jnp.max(jnp.where(chosen, logits, -1e30), axis=1, keepdims=True)
    grown = jnp.where(chosen, jnp.exp(jnp.minimum(logits - top_logit, 0.0)), 0.0)
    shares = grown / row_sum(grown)
    gates[...] = shares
    high = shares.astype(BF).astype(F32)
    x_out[:, width:] = (high + swap_halves(shares - high)).astype(BF)
    for i in range(2, last):
        rest.forward(i)
        if i + 1 < last:
            rest.enter(i + 1)
        rest.across(i)
    rest.end()
    terms.end()
    for k in range(group - 1):
        seats(k).wait()


def run_attend(seqs, n_dp, layers, x, gain, w, *rest):
    g_own = rest[-1]
    total, width = x.shape
    cols = w.shape[-1]
    group = 2 * n_dp
    rows = total // group
    shape = jax.ShapeDtypeStruct
    dma = pltpu.SemaphoreType.DMA
    narrow, narrow_f = shape((total, cols), BF), shape((total, cols), F32)
    result = pl.pallas_call(
        functools.partial(attend_kernel, n_dp, layers, seqs),
        out_shape=(
            shape((total, width), BF), narrow_f, narrow_f, narrow, narrow, narrow, narrow,
            shape((8, total), F32), shape((rows, width), F32), shape((rows, width), F32),
            shape((rows, 128), F32), shape((rows, 128), F32), shape((rows, width + 128), BF),
            shape((layers, group) + g_own.shape, BF),
        ),
        in_specs=[VMEM] * 11 + [ANY],
        out_specs=(VMEM,) * 13 + (ANY,),
        scratch_shapes=[
            pltpu.VMEM((group, rows, width), BF), pltpu.VMEM((8, total), F32),
            pltpu.VMEM((group - 1, 8, total), F32), dma((group - 1,)), dma((group - 1,)),
            pltpu.VMEM((rows, width), F32), dma((group - 1,)), dma((group - 1,)),
        ] + LayerSum.scratch(rows, width) + [
            dma((1,)), dma((layers + 1,)), dma((layers,)), dma((layers, 10)), dma((layers, 10)),
        ],
        compiler_params=pltpu.CompilerParams(
            collective_id=2, has_side_effects=True, vmem_limit_bytes=56 * 2**20
        ),
    )(x, gain, w, *rest)
    return result


def back_kernel(
    n_dp, layers, seqs,
    gao, wo, mixed, q_rot, k_rot, v, normed, q_raw, k_raw, stats, q_gain, k_gain, cosine, sine,
    w, x, early,
    out, grad_w, grad_o, small_out,
    grad_mixed, gq, gk, low, inner, gains, rowmat, small, part,
    acc, sib, one, two, load_sem, n_send, n_recv,
    go, acc_w, acc_o, up_w, up_o, up_v, down_w, down_o, down_v, swapped, land, s_land, s_sum, s_far,
    i_send, i_recv, o_keep, o_send, o_recv, up_send, up_recv, down_send, down_recv,
    a_keep, a_send, a_recv, s_send, s_recv, t_send, t_recv,
):
    here = Place(n_dp)
    group = 2 * n_dp
    layer, rank = here.layer, here.rank
    total, cols = q_raw.shape
    width = wo.shape[1]
    own = grad_w.shape[1]
    size = group * own
    length = total // seqs
    scale = HEAD_DIM ** (-0.5)
    last = layers - 1
    ranks = others(here, group)
    greet(
        [peer(here, r) for r in ranks]
        + [here.at_layer(flip(layer, i, layers)) for i in range(1, layers)]
    )
    job = LayerSum(here, part, acc, sib, one, two, load_sem, n_send, n_recv)
    terms = LayerTerms(here, ranks, lambda r: inner, land, i_send, i_recv)
    small_terms = LayerTerms(here, ranks, lambda r: small.at[:, r], s_land, s_send, s_recv)
    far_terms = ColumnTerms(here, layers, lambda z: s_sum.at[z], s_far, t_send, t_recv)

    def share(i):
        number = rank * layers + i
        z, target = number // group, number % group

        def far():
            return remote(
                go.at[i], acc_o.at[z], o_send.at[i], o_recv.at[z], peer(here, target)
            )

        def near():
            return pltpu.make_async_copy(go.at[i], acc_o.at[z], o_keep.at[z])

        return target, far, near

    def shared(z):
        source = (z * group + rank) // layers

        @pl.when(source != rank)
        def _():
            remote(
                go.at[0], acc_o.at[z], o_send.at[0], o_recv.at[z], here.sibling
            ).wait_recv()

        @pl.when(source == rank)
        def _():
            pltpu.make_async_copy(go.at[0], acc_o.at[z], o_keep.at[z]).wait()

    def rows_of(z):
        return pl.ds(pl.multiple_of(z * size, size), size)

    def chain(which, up, z):
        src = (acc_w.at[0:2, rows_of(z)], acc_o.at[z], acc_w.at[2, rows_of(z)])[which]
        to = ((up_w, up_o, up_v) if up else (down_w, down_o, down_v))[which].at[z]
        sems = (up_send, up_recv) if up else (down_send, down_recv)
        device = here.at_layer(layer + 1 if up else layer - 1)
        return remote(src, to, sems[0].at[which, z], sems[1].at[which, z], device)

    def take(which, up, z):
        chain(which, up, z).wait_recv()
        if which == 0:
            got = up_w if up else down_w
            for i in range(2):
                value = acc_w[i, rows_of(z)].astype(F32) + got[z, i].astype(F32)
                acc_w[i, rows_of(z)] = value.astype(BF)
        elif which == 1:
            got = up_o if up else down_o
            acc_o[z] = (acc_o[z].astype(F32) + got[z].astype(F32)).astype(BF)
        else:
            got = up_v if up else down_v
            value = acc_w[2, rows_of(z)].astype(F32) + got[z].astype(F32)
            acc_w[2, rows_of(z)] = value.astype(BF)

    def launch(which):
        for d in range(last, 0, -1):
            @pl.when(layer == 0)
            def _():
                chain(which, True, layer + d).start()

            @pl.when(layer == last)
            def _():
                chain(which, False, layer - d).start()

    def relay(which, d):
        @pl.when(jnp.logical_and(layer > 0, layer + d < layers))
        def _():
            take(which, True, layer + d)
            chain(which, True, layer + d).start()

        @pl.when(jnp.logical_and(layer < last, layer - d >= 0))
        def _():
            take(which, False, layer - d)
            chain(which, False, layer - d).start()

    def relay_all(which):
        for d in range(last - 1, 0, -1):
            relay(which, d)

    def settle(which):
        @pl.when(layer > 0)
        def _():
            take(which, True, layer)

        @pl.when(layer < last)
        def _():
            take(which, False, layer)

    for n in range(0, width, STEP):
        got = tdot(mixed[...], gao[:, n : n + STEP]).astype(BF)
        go[:, :, n : n + STEP] = got.reshape(layers, own, STEP)
    for i in range(layers):
        target, far, near = share(i)

        @pl.when(target != rank)
        def _():
            far().start()

        @pl.when(target == rank)
        def _():
            near().start()
    grad_mixed[...] = dot_t(gao[...], wo[...]).astype(BF)
    inner[...] = jnp.zeros_like(inner)
    gains[...] = jnp.zeros_like(gains)

    for s in range(seqs):
        rows = slice(s * length, (s + 1) * length)
        roots = [
            as_column(lax.rsqrt(stats[i : i + 1, rows] / width + EPSILON)) for i in range(2)
        ]
        inners = [jnp.zeros((length, 1), F32) for _ in range(2)]
        for h in range(0, cols, HEAD_DIM):
            head = slice(h, h + HEAD_DIM)
            q, k = q_rot[rows, head], k_rot[rows, head]
            probs = probabilities(q, k, scale)
            gm = grad_mixed[rows, head]
            low[2, rows, head] = tdot(probs.astype(BF), gm).astype(BF)
            grad_probs = dot_t(gm, v[rows, head])
            delta = row_sum(probs * grad_probs)
            grad_scores = (probs * (grad_probs - delta)).astype(BF)
            for i, (turned, raw, gain, to) in enumerate((
                (dot(grad_scores, k) * scale, q_raw, q_gain, gq),
                (tdot(grad_scores, q) * scale, k_raw, k_gain, gk),
            )):
                back = turned * cosine[...] - swap_halves(turned) * sine[...]
                unit = raw[rows, head] * roots[i]
                gains[i : i + 1, head] += jnp.sum(back * unit, axis=0, keepdims=True)
                back = back * gain[:, head]
                to[rows, head] = back
                inners[i] = inners[i] + row_sum(back * unit)
        for i in range(2):
            inner[i : i + 1, rows] = as_row(inners[i])
        if s == 0:
            for z in range(layers):
                shared(z)
            launch(1)
    terms.begin()

    def weight_grads(i):
        for n in range(0, width, STEP):
            acc_w[i, n : n + STEP, :] = tdot(normed[:, n : n + STEP], low[i]).astype(BF)

    weight_grads(2)
    launch(2)
    relay_all(1)
    means = terms.total(inner[...]) / width
    for i, (grad, raw) in enumerate(((gq, q_raw), (gk, k_raw))):
        root = as_column(lax.rsqrt(stats[i : i + 1, :] / width + EPSILON))
        mean = as_column(means[i : i + 1, :])
        low[i] = (root * (grad[...] - raw[...] * root * mean)).astype(BF)
        weight_grads(i)
    launch(0)
    rowmat[...] = early[...]

    def project(b, c):
        at = pl.ds(pl.multiple_of(b * part.shape[1], part.shape[1]), part.shape[1])
        value = x[at, :].astype(F32)
        root = lax.rsqrt(row_sum(value * value) / width + EPSILON)
        for n in range(0, width, STEP):
            cut = slice(n, n + STEP)
            got = dot_t(low[0, at, :], w[0, cut, :]) + dot_t(low[1, at, :], w[1, cut, :])
            got = got + dot_t(low[2, at, :], w[2, cut, :])
            part[b, :, cut] = got.astype(BF)
            unit = x[at, cut].astype(F32) * root
            rowmat[64:65, cut] += jnp.sum(got * unit, axis=0, keepdims=True)
        return c

    lax.fori_loop(0, group, project, 0)
    job.begin()
    head_cols = pl.ds(pl.multiple_of(rank * cols, cols), cols)
    rowmat[65:66, head_cols] = gains[0:1, :]
    rowmat[66:67, head_cols] = gains[1:2, :]
    for n in range(0, width, 128):
        turned = rowmat[:, n : n + 128].T
        for i in range(128 // own):
            number = n // own + i
            small[number // group, number % group] = turned[i * own : (i + 1) * own]
    relay_all(2)
    job.first()
    small_terms.begin()
    for d in range(last - 1, 0, -1):
        relay(0, d)
        if d == last - 1:
            job.second()
    if last < 2:
        job.second()
    s_sum[...] = small_terms.total(small[:, rank])
    far_terms.begin()
    job.third(out)
    settle(1)
    settle(2)
    grad_o[...] = acc_o[layer].astype(F32)
    small_out[...] = far_terms.total(s_sum[layer])
    settle(0)

    def block(index):
        return acc_w.at[:, pl.ds(pl.multiple_of(layer * size + index * own, own), own)]

    def swap(k):
        return remote(
            block(ranks[k]), swapped.at[rank], a_send.at[k], a_recv.at[k], peer(here, ranks[k])
        )

    def swap_own():
        return pltpu.make_async_copy(block(rank), swapped.at[rank], a_keep.at[0])

    swap_own().start()
    for k in range(group - 1):
        swap(k).start()
    swap_own().wait()
    for k in range(group - 1):
        swap(k).wait_recv()
    for r in range(group):
        for i in range(3):
            grad_w[i, :, r * cols : (r + 1) * cols] = swapped[r, i].astype(F32)

    terms.end()
    small_terms.end()
    far_terms.end()
    for k in range(group - 1):
        swap(k).wait_send()
    for i in range(layers):
        target, far, near = share(i)

        @pl.when(target != rank)
        def _():
            far().wait_send()
    for which in range(3):
        for d in range(1, layers):
            @pl.when(layer + d < layers)
            def _():
                chain(which, True, layer + d).wait_send()

            @pl.when(layer - d >= 0)
            def _():
                chain(which, False, layer - d).wait_send()


def run_back(seqs, n_dp, layers, gao, wo, mixed, q_rot, k_rot, v, normed, q_raw, k_raw, *rest):
    total, cols = q_raw.shape
    width = wo.shape[1]
    group = 2 * n_dp
    rows = total // group
    own = width // (layers * group)
    size = group * own
    dma = pltpu.SemaphoreType.DMA
    shape = jax.ShapeDtypeStruct
    many, few = dma((3, layers)), dma((layers,))
    near = dma((group - 1,))
    tiny = (layers, own, 128)
    return pl.pallas_call(
        functools.partial(back_kernel, n_dp, layers, seqs),
        out_shape=(
            shape((rows, width), F32), shape((3, own, width), F32),
            shape((own, width), F32), shape((own, 128), F32),
        ),
        in_specs=[VMEM] * 17,
        out_specs=(VMEM,) * 4,
        scratch_shapes=[
            pltpu.VMEM((total, cols), BF), pltpu.VMEM((total, cols), F32),
            pltpu.VMEM((total, cols), F32), pltpu.VMEM((3, total, cols), BF),
            pltpu.VMEM((8, total), F32), pltpu.VMEM((8, cols), F32),
            pltpu.VMEM((128, width), F32), pltpu.VMEM((layers, group, own, 128), F32),
            pltpu.VMEM((group, rows, width), BF),
        ] + LayerSum.scratch(rows, width) + [
            pltpu.VMEM((layers, own, width), BF), pltpu.VMEM((3, width, cols), BF),
            pltpu.VMEM((layers, own, width), BF),
        ] + [
            pltpu.VMEM((layers, 2, size, cols), BF), pltpu.VMEM((layers, own, width), BF),
            pltpu.VMEM((layers, size, cols), BF),
        ] * 2 + [
            pltpu.VMEM((group, 3, own, cols), BF), pltpu.VMEM((group - 1, 8, total), F32),
            pltpu.VMEM((group - 1,) + tiny, F32), pltpu.VMEM(tiny, F32), pltpu.VMEM(tiny, F32),
            near, near, few, few, few, many, many, many, many,
            dma((1,)), near, near, near, near, few, few,
        ],
        compiler_params=pltpu.CompilerParams(
            collective_id=6, has_side_effects=True, vmem_limit_bytes=63 * 2**20
        ),
    )(gao, wo, mixed, q_rot, k_rot, v, normed, q_raw, k_raw, *rest)


def ein(spec, left, right):
    return jnp.einsum(spec, left, right, preferred_element_type=F32)


def inv_rms(value):
    return lax.rsqrt(jnp.mean(value * value, axis=-1, keepdims=True) + EPSILON)


def build(n_ep, n_dp):
    n_dev = n_ep * n_dp
    group = 2 * n_dp
    layers = n_dev // group
    rows_of = [[z * group + r for r in range(group)] for z in range(layers)]

    def shards(
        layer_input, grad_out, attn_gain, w_q, w_k, w_v, q_gain, k_gain, w_o, ffn_gain,
        router, w_gate, w_up, w_down, routes,
    ):
        rows, width = layer_input.shape
        cols = width // group
        seqs = 2
        seq_len = rows * n_dp
        own = width // n_dev
        rank = (lax.axis_index("ep") % 2) * n_dp + lax.axis_index("dp")
        experts = router.shape[1]
        top = routes.shape[1]
        cap = 2 * rows * top // experts

        gains = jnp.stack([attn_gain, q_gain, k_gain, ffn_gain]).T
        small = jnp.concatenate(
            [router, gains, jnp.zeros((own, 128 - experts - 4), BF)], axis=1
        )
        group_input, qkv, wo, small, near_g = run_front(
            layer_input, w_q, w_k, w_v, w_o, small, grad_out, n_dp, n_dev
        )
        full_router = small[:, :experts]
        full_attn_gain = small[:, experts].astype(F32)
        full_ffn_gain = small[:, experts + 3].astype(F32)
        head_gains = lax.dynamic_slice_in_dim(small, rank * cols, cols, 0).astype(F32)
        q_gain_own, k_gain_own = head_gains[:, experts + 1], head_gains[:, experts + 2]

        picked = routes[:, :, None] == jnp.arange(experts, dtype=jnp.int32)
        hits = jnp.any(picked, axis=1)
        before = jnp.cumsum(hits.astype(jnp.int32), axis=0) - hits.astype(jnp.int32)
        place = jnp.where(hits, before, -1).astype(BF)
        place = jnp.pad(place.T, ((0, rows - experts), (0, 0)))
        sent = jnp.concatenate([grad_out, place], axis=1)
        hits_wide = jnp.pad(hits.astype(F32), ((0, 0), (0, 128 - experts)))
        router_wide = jnp.pad(full_router, ((0, 0), (0, 128 - experts)))
        half_dim = HEAD_DIM // 2
        frequency = 10000.0 ** (-jnp.arange(half_dim, dtype=F32) * 2.0 / HEAD_DIM)
        angle = jnp.arange(seq_len, dtype=F32)[:, None] * frequency[None, :]
        cosine = jnp.concatenate([jnp.cos(angle)] * 2, axis=-1)
        sine = jnp.concatenate([-jnp.sin(angle), jnp.sin(angle)], axis=-1)
        tables = (q_gain_own[None], k_gain_own[None], cosine, sine)
        (
            normed, q_raw, k_raw, v_low, q_rot, k_rot, mixed, stats,
            residual, res_n, res_root, gates, x_own, all_g,
        ) = run_attend(
            seqs, n_dp, layers, group_input, full_attn_gain[None], qkv, *tables, wo,
            full_ffn_gain[None], router_wide, hits_wide, sent,
        )
        all_g = all_g.reshape((n_dev,) + sent.shape)
        res_root, gates_dense, normed2 = res_root[:, :1], gates[:, :experts], x_own[:, :width]

        expert_sum, grad_sum, x_slots, g_slots, acts = run_experts(
            x_own, all_g, near_g, w_gate, w_up, w_down, n_dp, experts, cap
        )
        grad_w_gate, grad_w_up, grad_w_down = run_weights(x_slots, g_slots, acts)
        output = (residual + expert_sum).astype(BF)
        gate_grads = jnp.where(hits, grad_sum[:, width : width + experts], 0.0)
        weighted = jnp.sum(gates_dense * gate_grads, axis=-1, keepdims=True)
        grad_logits = (gates_dense * (gate_grads - weighted)).astype(BF)

        grad_n2 = grad_sum[:, :width] + ein("te,de->td", grad_logits, full_router)
        grad_y = grad_out.astype(F32)
        grad_ffn_gain = jnp.sum(grad_n2 * res_n, axis=0)
        dn = grad_n2 * full_ffn_gain
        grad_residual = grad_y + res_root * (dn - res_n * jnp.mean(dn * res_n, -1, keepdims=True))

        gao = lax.all_gather(
            grad_residual.astype(BF), AXES, axis=0, tiled=True, axis_index_groups=rows_of
        )
        early = jnp.concatenate(
            [
                ein("te,td->ed", grad_logits, normed2), jnp.zeros((3, width), F32),
                grad_ffn_gain[None], jnp.zeros((128 - experts - 4, width), F32),
            ]
        )
        grad_normed, grad_qkv, grad_o, small_grads = run_back(
            seqs, n_dp, layers, gao, wo, mixed, q_rot, k_rot, v_low, normed, q_raw, k_raw, stats,
            *tables, qkv, group_input, early,
        )
        own_input = layer_input.astype(F32)
        in_root = inv_rms(own_input)
        in_n = own_input * in_root
        dn = grad_normed * full_attn_gain
        grad_input = grad_residual + in_root * (
            dn - in_n * jnp.mean(dn * in_n, -1, keepdims=True)
        )
        gain_grads = small_grads[:, experts : experts + 4]
        return (
            output, grad_input, gain_grads[:, 0], grad_qkv[0], grad_qkv[1], grad_qkv[2],
            gain_grads[:, 1], gain_grads[:, 2], grad_o, gain_grads[:, 3],
            small_grads[:, :experts], grad_w_gate, grad_w_up, grad_w_down,
        )

    return shards


def solution(mesh):
    row, vec = P(("ep", "dp"), None), P(("ep", "dp"))
    wide, deep = P("ep", None, "dp"), P("ep", "dp", None)
    in_specs = (
        row, row, vec, row, row, row, vec, vec, row, vec, row, wide, wide, deep, row,
    )
    out_specs = (
        row, row, vec, row, row, row, vec, vec, row, vec, row, wide, wide, deep,
    )
    shards = build(mesh.shape["ep"], mesh.shape["dp"])
    return jax.shard_map(shards, mesh=mesh, in_specs=in_specs, out_specs=out_specs, check_vma=False)
```

```python
import functools

import jax
import jax.numpy as jnp
import numpy as np
from jax import lax
from jax.experimental import pallas as pl
from jax.experimental.pallas import tpu as pltpu
from jax.sharding import PartitionSpec as P

HEAD_DIM = 128
EPSILON = 1e-05
AXES = ("ep", "dp")
BF = jnp.bfloat16
F32 = jnp.float32
ANY = pl.BlockSpec(memory_space=pl.ANY)
VMEM = pl.BlockSpec(memory_space=pltpu.VMEM)
MESH = pl.DeviceIdType.MESH
STEP = 512
HOOKS = 8


def dot(left, right):
    return jnp.dot(left, right, preferred_element_type=F32)


def dot_t(left, right):
    return lax.dot_general(left, right, (((1,), (1,)), ((), ())), preferred_element_type=F32)


def tdot(left, right):
    return lax.dot_general(left, right, (((0,), (0,)), ((), ())), preferred_element_type=F32)


def flip(value, other, count):
    result, bit = 0, 1
    while bit < count:
        result = result + ((value // bit) % 2 + (other // bit) % 2) % 2 * bit
        bit *= 2
    return result


def nearby(z, i, count):
    both = jnp.minimum(z, count - 1 - z)
    first = 1 - 2 * (z % 2)
    paired = z + first * (1 - 2 * (i % 2)) * (i // 2 + 1)
    side = jnp.where(2 * z < count, 1, -1)
    single = z + side * (i - both + 1)
    return jnp.where(i == count - 1, z, jnp.where(i < 2 * both, paired, single))


class Place:
    def __init__(self, n_dp):
        ep, dp = lax.axis_index("ep"), lax.axis_index("dp")
        half = n_dp // 2
        self.n_dp, self.half = n_dp, half
        self.layer, self.y = ep // 2, ep % 2
        self.x, self.core = dp // 2, dp % 2
        self.rank = self.y * n_dp + dp
        self.ep, self.dp = ep, dp
        self.sibling = (ep, self.x * 2 + 1 - self.core)
        self.over_x = (ep, (1 - self.x) * 2 + self.core)
        self.over_y = (self.layer * 2 + 1 - self.y, dp)

    def at_layer(self, layer):
        return (layer * 2 + self.y, self.dp)


def greet(partners):
    barrier = pltpu.get_barrier_semaphore()
    for partner in partners:
        pl.semaphore_signal(barrier, inc=1, device_id=partner, device_id_type=MESH)
    pl.semaphore_wait(barrier, len(partners))


def experts_kernel(
    n_dp, experts,
    x_own, all_g, near_g, wg_hbm, wu_hbm, wd_hbm,
    out_sum, grad_sum, x_out, g_out, acts_out, all_x,
    sib_o, sib_g, one_o, one_g, two_o, two_g, z_o, z_g,
    wg, wu, wd, xs, gs, gate_rows, acts, xin, gin, stage_o, stage_g, acc_o, acc_g, tmp_o, tmp_g,
    leave_o, leave_g, pin, table,
    w_sem, in_sem, keep_sem, act_sem, own_sem, zx_send, zx_recv, ag_send, ag_recv,
    sib_send, sib_recv, one_send, one_recv, two_send, two_recv, z_send, z_recv, tmp_sem,
):
    n_dev, rows, wide = all_x.shape
    local, width, hid = wg.shape
    cap = xs.shape[2]
    group = 2 * n_dp
    layers = n_dev // group
    m = group * cap
    slots = xin.shape[0]
    half = width // 2
    here = Place(n_dp)
    rank, core, x, y = here.rank, here.core, here.x, here.y
    first = here.ep * local

    def remote(src, dst, send, recv, device):
        return pltpu.make_async_remote_copy(
            src_ref=src, dst_ref=dst, send_sem=send, recv_sem=recv,
            device_id=device, device_id_type=MESH,
        )

    def layer_of(i):
        return nearby(here.layer, i, layers)

    def weights():
        return [
            pltpu.make_async_copy(s, d, w_sem.at[i])
            for i, (s, d) in enumerate(((wg_hbm, wg), (wu_hbm, wu), (wd_hbm, wd)))
        ]

    def z_copy(block, up):
        at = all_x.at[block * group + rank]
        device = here.at_layer(here.layer + 1 if up else here.layer - 1)
        return remote(at, at, zx_send.at[block], zx_recv.at[block], device)

    def z_own(act):
        @pl.when(here.layer + 1 < layers)
        def _():
            act(own_z(True))

        @pl.when(here.layer >= 1)
        def _():
            act(own_z(False))

    def own_z(up):
        device = here.at_layer(here.layer + 1 if up else here.layer - 1)
        return remote(
            x_own, all_x.at[here.layer * group + rank],
            zx_send.at[here.layer if up else layers], zx_recv.at[here.layer], device,
        )

    def passes(i):
        block = layer_of(i)
        up = jnp.logical_and(block < here.layer, here.layer + 1 < layers)
        down = jnp.logical_and(block > here.layer, here.layer >= 1)
        return block, up, down

    def z_pass(i):
        block, up, down = passes(i)

        @pl.when(up)
        def _():
            z_copy(block, True).wait_recv()
            z_copy(block, True).start()

        @pl.when(down)
        def _():
            z_copy(block, False).wait_recv()
            z_copy(block, False).start()

    def z_arrive(i):
        block, up, down = passes(i)

        @pl.when(jnp.logical_not(jnp.logical_or(up, down)))
        def _():
            z_copy(block, True).wait_recv()

    def z_drain(i):
        block, up, down = passes(i)

        @pl.when(up)
        def _():
            z_copy(block, True).wait_send()

        @pl.when(down)
        def _():
            z_copy(block, False).wait_send()

    def own_copy():
        return pltpu.make_async_copy(x_own, all_x.at[here.layer * group + rank], own_sem.at[0])

    over_x_rank = y * n_dp + (1 - x) * 2 + core
    over_y_rank = (1 - y) * n_dp + x * 2 + core
    across_rank = (1 - y) * n_dp + (1 - x) * 2 + core
    first_half, second_half = pl.ds(0, half), pl.ds(half, wide - half)

    def gather_copy(i, kind):
        base = layer_of(i) * group
        which, cols, device = {
            0: (rank, first_half, here.over_x),
            1: (rank, second_half, here.over_x),
            2: (rank, first_half, here.over_y),
            3: (rank, second_half, here.over_y),
            4: (over_x_rank, first_half, here.over_y),
            5: (over_y_rank, second_half, here.over_x),
            6: (rank, pl.ds(0, wide), here.sibling),
            7: (over_x_rank, pl.ds(0, wide), here.sibling),
            8: (over_y_rank, pl.ds(0, wide), here.sibling),
            9: (across_rank, pl.ds(0, wide), here.sibling),
        }[kind]
        ref = all_x.at[base + which, :, cols]
        return remote(ref, ref, ag_send.at[i, kind], ag_recv.at[i, kind], device)

    def gather_a(i):
        @pl.when(i < layers - 1)
        def _():
            z_arrive(i)

        @pl.when(i == layers - 1)
        def _():
            own_copy().wait()

        for kind in (0, 3, 1, 2, 6):
            gather_copy(i, kind).start()

    def gather_b(i):
        for got, then in ((0, 4), (3, 5), (1, 7), (2, 8)):
            gather_copy(i, got).wait_recv()
            gather_copy(i, then).start()

    def gather_c(i):
        gather_copy(i, 4).wait_recv()
        gather_copy(i, 5).wait_recv()
        gather_copy(i, 9).start()

    def gather_d(i):
        for kind in (6, 7, 8, 9):
            gather_copy(i, kind).wait_recv()

    def sib_copy(i, q, slot):
        return (
            remote(stage_o.at[slot], sib_o.at[i, q], sib_send.at[0, slot], sib_recv.at[0, i, q],
                   here.sibling),
            remote(stage_g.at[slot], sib_g.at[i, q], sib_send.at[1, slot], sib_recv.at[1, i, q],
                   here.sibling),
        )

    def one_copy_o(i, j):
        return remote(acc_o.at[j * 2 + 1 - x], one_o.at[i, j], one_send.at[0, j],
                      one_recv.at[0, i, j], here.over_x)

    def one_copy_g(i, j):
        return remote(acc_g.at[(1 - y) * 2 + j], one_g.at[i, j], one_send.at[1, j],
                      one_recv.at[1, i, j], here.over_y)

    def two_copy(i):
        return (
            remote(acc_o.at[(1 - y) * 2 + x], two_o.at[i], two_send.at[0], two_recv.at[0, i],
                   here.over_y),
            remote(acc_g.at[y * 2 + 1 - x], two_g.at[i], two_send.at[1], two_recv.at[1, i],
                   here.over_x),
        )

    def out_copy(i):
        at, device = here.layer, here.at_layer(layer_of(i))
        return (
            remote(leave_o, z_o.at[at], z_send.at[0], z_recv.at[0, at], device),
            remote(leave_g, z_g.at[at], z_send.at[1], z_recv.at[1, at], device),
        )

    def fetch(src_o, src_g, slot):
        return (
            pltpu.make_async_copy(src_o, tmp_o.at[slot], tmp_sem.at[0, slot]),
            pltpu.make_async_copy(src_g, tmp_g.at[slot], tmp_sem.at[1, slot]),
        )

    def start(copies):
        for copy in copies:
            copy.start()

    def finish(copies):
        for copy in copies:
            copy.wait()

    def add(dst, q, tmp, slot):
        total = dst[q].astype(F32) + tmp[slot].astype(F32)
        dst[q] = total.astype(BF)

    def sum_one(i):
        o, g = one_copy_o(i, 1 - y), one_copy_g(i, 1 - x)
        o.wait_recv()
        g.wait_recv()
        copies = fetch(one_o.at[i, 1 - y], one_g.at[i, 1 - x], 0)
        start(copies)
        finish(copies)
        add(acc_o, (1 - y) * 2 + x, tmp_o, 0)
        add(acc_g, y * 2 + 1 - x, tmp_g, 0)
        start(two_copy(i))

    def sum_two(i):
        own = y * 2 + x
        one_copy_o(i, y).wait_recv()
        one_copy_g(i, x).wait_recv()
        ones = fetch(one_o.at[i, y], one_g.at[i, x], 0)
        start(ones)
        for copy in two_copy(i):
            copy.wait_recv()
        twos = fetch(two_o.at[i], two_g.at[i], 1)
        start(twos)
        finish(ones)
        finish(twos)

        @pl.when(i > 0)
        def _():
            for copy in out_copy(i - 1):
                copy.wait_send()

        for acc, tmp, leave in ((acc_o, tmp_o, leave_o), (acc_g, tmp_g, leave_g)):
            total = acc[own].astype(F32) + tmp[0].astype(F32) + tmp[1].astype(F32)
            leave[...] = total.astype(BF)
        for j in range(2):
            one_copy_o(i, j).wait_send()
            one_copy_g(i, j).wait_send()
        for copy in two_copy(i):
            copy.wait_send()

        @pl.when(i < layers - 1)
        def _():
            start(out_copy(i))

    start(weights())
    greet([here.over_x, here.over_y, here.sibling]
          + [here.at_layer(flip(here.layer, i, layers)) for i in range(1, layers)])
    own_copy().start()
    z_own(lambda copy: copy.start())
    z_pass(0)
    gather_a(0)
    z_pass(1)
    gather_b(0)
    for i in range(2, layers - 1):
        z_pass(i)
    gather_c(0)
    gather_a(1)

    def chunk(i, carry):
        base = layer_of(i) * group

        gather_d(i)

        def load(b, slot):
            return (
                pltpu.make_async_copy(all_x.at[base + b], xin.at[slot], in_sem.at[0, slot]),
                pltpu.make_async_copy(
                    all_g.at[base + b, pl.ds(0, experts), pl.ds(width, rows)], pin.at[slot],
                    in_sem.at[2, slot],
                ),
            )

        def load_g(b, slot, act):
            @pl.when(i < layers - 1)
            def _():
                act(pltpu.make_async_copy(
                    all_g.at[base + b, :, pl.ds(0, width)], gin.at[slot], in_sem.at[1, slot]
                ))

            @pl.when(i == layers - 1)
            def _():
                act(pltpu.make_async_copy(near_g.at[b], gin.at[slot], in_sem.at[1, slot]))

        def begin_load(b, slot):
            start(load(b, slot))
            load_g(b, slot, lambda copy: copy.start())

        for b in range(slots - 1):
            begin_load(b, b)

        def bring(b, c):
            slot = lax.rem(b, slots)
            finish(load(b, slot))
            load_g(b, slot, lambda copy: copy.wait())

            @pl.when(b + slots - 1 < group)
            def _():
                begin_load(b + slots - 1, lax.rem(b + slots - 1, slots))

            size = local * cap
            chooses = (
                lax.broadcasted_iota(jnp.int32, (size, experts), 1)
                == lax.broadcasted_iota(jnp.int32, (size, experts), 0) // cap + first
            )
            places = dot(jnp.where(chooses, 1.0, 0.0).astype(BF), pin[slot])
            seat = lax.broadcasted_iota(jnp.int32, (size, rows), 0) % cap
            hot = jnp.where(places == seat.astype(F32), 1.0, 0.0).astype(BF)
            table[b] = hot
            for src, dst in ((xin, xs), (gin, gs)):
                for n in range(0, width, STEP):
                    got = dot(hot, src[slot, :, n : n + STEP]).astype(BF)
                    dst[:, b, :, n : n + STEP] = got.reshape(local, cap, STEP)
            gates = dot(hot, xin[slot, :, width:wide])
            lanes = lax.broadcasted_iota(jnp.int32, gates.shape, 1) % experts
            expert = lax.broadcasted_iota(jnp.int32, gates.shape, 0) // cap + first
            gates = jnp.sum(jnp.where(lanes == expert, gates, 0.0), axis=1, keepdims=True)
            gate_rows[:, b] = jnp.broadcast_to(gates, (local * cap, 128)).reshape(local, cap, 128)
            return c

        lax.fori_loop(0, group, bring, 0)

        def keep(e):
            return (
                pltpu.make_async_copy(xs.at[e], x_out.at[e, pl.ds(base, group)], keep_sem.at[0, e]),
                pltpu.make_async_copy(gs.at[e], g_out.at[e, pl.ds(base, group)], keep_sem.at[1, e]),
            )

        def keep_acts(e, slot):
            return pltpu.make_async_copy(
                acts.at[slot], acts_out.at[:, e, pl.ds(base * cap, m)], act_sem.at[slot]
            )

        lax.fori_loop(0, local, lambda e, c: (start(keep(e)), c)[1], 0)

        @pl.when(i == 0)
        def _():
            finish(weights())

        def expert(e, c):
            def hook(number, when, action):
                @pl.when(jnp.logical_and(e == number * local // HOOKS, when))
                def _():
                    action()

            hook(6, i + 2 < layers, lambda: gather_a(i + 2))
            hook(4, i + 1 < layers, lambda: gather_b(i + 1))
            hook(7, i + 1 < layers, lambda: gather_c(i + 1))
            hook(4, i > 0, lambda: sum_one(i - 1))
            slot = lax.rem(e, 2)

            @pl.when(jnp.logical_or(i > 0, e >= 2))
            def _():
                keep_acts(e, slot).wait()

            xe = xs[e].reshape(m, width)
            ge = gs[e].reshape(m, width)
            gate_part = dot(xe, wg[e])
            up_part = dot(xe, wu[e])
            raw = dot_t(ge, wd[e])
            gate = gate_rows[e].reshape(m, 128)[:, :1]
            sig = 1.0 / (1.0 + jnp.exp(-gate_part))
            silu = gate_part * sig
            hidden = silu * up_part
            own = jnp.sum(hidden * raw, axis=1, keepdims=True)
            lanes = lax.broadcasted_iota(jnp.int32, (m, 128), 1)
            grad_hidden = raw * gate
            hg = (hidden * gate).astype(BF)
            dg = (grad_hidden * up_part * sig * (1.0 + gate_part * (1.0 - sig))).astype(BF)
            du = (grad_hidden * silu).astype(BF)
            gate_rows[e] = jnp.where(lanes == first + e, own, 0.0).reshape(group, cap, 128)
            acts[slot, 0] = hg
            acts[slot, 1] = dg
            acts[slot, 2] = du
            keep_acts(e, slot).start()
            finish(keep(e))
            for n in range(0, width, STEP):
                out = dot(hg, wd[e, :, n : n + STEP]).astype(BF)
                gs[e, :, :, n : n + STEP] = out.reshape(group, cap, STEP)
                back = dot_t(dg, wg[e, n : n + STEP, :]) + dot_t(du, wu[e, n : n + STEP, :])
                xs[e, :, :, n : n + STEP] = back.astype(BF).reshape(group, cap, STEP)
            return c

        lax.fori_loop(0, local, expert, 0)

        def combine(b, put_o, put_g):
            hot = table[b]
            for n in range(0, width, STEP):
                got = gs[:, b, :, n : n + STEP].reshape(local * cap, STEP)
                put_o(n, STEP, tdot(hot, got))
                got = xs[:, b, :, n : n + STEP].reshape(local * cap, STEP)
                put_g(n, STEP, tdot(hot, got))
            got = gate_rows[:, b].reshape(local * cap, 128).astype(BF)
            put_g(width, 128, tdot(hot, got))

        def square(k):
            return (y + 1 - k % 2) % 2, (x + 1 - k // 2) % 2

        def give(k, c):
            slot = lax.rem(k, 2)
            to_y, to_x = square(k)
            q = to_y * 2 + to_x

            @pl.when(jnp.logical_or(i > 0, k >= 2))
            def _():
                for copy in sib_copy(i, q, slot):
                    copy.wait_send()

            def put_o(n, size, value):
                stage_o[slot, :, pl.ds(n, size)] = value.astype(BF)

            def put_g(n, size, value):
                stage_g[slot, :, pl.ds(n, size)] = value.astype(BF)

            combine(q * 2 + 1 - core, put_o, put_g)
            start(sib_copy(i, q, slot))
            return c

        lax.fori_loop(0, 4, give, 0)

        def from_sibling(k):
            to_y, to_x = square(k)
            q = to_y * 2 + to_x
            return fetch(sib_o.at[i, q], sib_g.at[i, q], lax.rem(k, 2))

        def bring_sibling(k):
            to_y, to_x = square(k)
            for copy in sib_copy(i, to_y * 2 + to_x, 0):
                copy.wait_recv()
            start(from_sibling(k))

        @pl.when(i > 0)
        def _():
            sum_two(i - 1)

        bring_sibling(0)

        def hold(k, c):
            slot = lax.rem(k, 2)
            to_y, to_x = square(k)
            q = to_y * 2 + to_x

            @pl.when(k < 3)
            def _():
                bring_sibling(k + 1)

            finish(from_sibling(k))

            def put_o(n, size, value):
                cols = pl.ds(n, size)
                acc_o[q, :, cols] = (value + tmp_o[slot, :, cols].astype(F32)).astype(BF)

            def put_g(n, size, value):
                cols = pl.ds(n, size)
                acc_g[q, :, cols] = (value + tmp_g[slot, :, cols].astype(F32)).astype(BF)

            combine(q * 2 + core, put_o, put_g)

            @pl.when(k < 2)
            def _():
                one_copy_o(i, to_y).start()

            @pl.when(k % 2 == 0)
            def _():
                one_copy_g(i, to_x).start()

            return c

        lax.fori_loop(0, 4, hold, 0)
        return carry

    lax.fori_loop(0, layers, chunk, 0)
    last = layers - 1
    sum_one(last)
    sum_two(last)
    out_sum[...] = leave_o[...].astype(F32)
    grad_sum[...] = leave_g[...].astype(F32)

    def arrive(i):
        at = layer_of(i)
        for copy in (
            remote(leave_o, z_o.at[at], z_send.at[0], z_recv.at[0, at], here.sibling),
            remote(leave_g, z_g.at[at], z_send.at[1], z_recv.at[1, at], here.sibling),
        ):
            copy.wait_recv()
        start(fetch(z_o.at[at], z_g.at[at], i % 2))

    arrive(0)
    for i in range(last):
        if i + 1 < last:
            arrive(i + 1)
        finish(fetch(z_o.at[layer_of(i)], z_g.at[layer_of(i)], i % 2))
        out_sum[...] += tmp_o[i % 2].astype(F32)
        grad_sum[...] += tmp_g[i % 2].astype(F32)
    for slot in range(2):
        for copy in sib_copy(last, slot, slot):
            copy.wait_send()
        pltpu.make_async_copy(
            acts.at[slot], acts_out.at[:, 0, pl.ds(0, m)], act_sem.at[slot]
        ).wait()

    def drain(i, c):
        for kind in range(10):
            gather_copy(i, kind).wait_send()
        return c

    lax.fori_loop(0, layers, drain, 0)
    z_own(lambda copy: copy.wait_send())
    for i in range(last):
        z_drain(i)


def run_experts(x_own, all_g, near_g, wg, wu, wd, n_dp, experts, cap):
    rows, wide = x_own.shape
    n_dev = all_g.shape[0]
    local, width, hid = wg.shape
    group = 2 * n_dp
    layers = n_dev // group
    m = group * cap
    wide_g = width + 128
    slots = 3
    dma = pltpu.SemaphoreType.DMA
    shape = jax.ShapeDtypeStruct
    slot_rows = shape((local, n_dev, cap, width), BF)
    flops = 12 * n_dev * cap * local * width * hid
    result = pl.pallas_call(
        functools.partial(experts_kernel, n_dp, experts),
        out_shape=(
            shape((rows, width), F32), shape((rows, wide_g), F32),
            slot_rows, slot_rows,
            shape((3, local, n_dev * cap, hid), BF),
            shape((n_dev, rows, wide), BF),
            shape((layers, 4, rows, width), BF), shape((layers, 4, rows, wide_g), BF),
            shape((layers, 2, rows, width), BF), shape((layers, 2, rows, wide_g), BF),
            shape((layers, rows, width), BF), shape((layers, rows, wide_g), BF),
            shape((layers, rows, width), BF), shape((layers, rows, wide_g), BF),
        ),
        in_specs=[ANY] * 6,
        out_specs=(VMEM, VMEM) + (ANY,) * 12,
        scratch_shapes=[
            pltpu.VMEM(wg.shape, BF), pltpu.VMEM(wu.shape, BF), pltpu.VMEM(wd.shape, BF),
            pltpu.VMEM((local, group, cap, width), BF),
            pltpu.VMEM((local, group, cap, width), BF),
            pltpu.VMEM((local, group, cap, 128), F32),
            pltpu.VMEM((2, 3, m, hid), BF),
            pltpu.VMEM((slots, rows, wide), BF),
            pltpu.VMEM((slots, rows, width), BF),
            pltpu.VMEM((2, rows, width), BF), pltpu.VMEM((2, rows, wide_g), BF),
            pltpu.VMEM((4, rows, width), BF), pltpu.VMEM((4, rows, wide_g), BF),
            pltpu.VMEM((2, rows, width), BF), pltpu.VMEM((2, rows, wide_g), BF),
            pltpu.VMEM((rows, width), BF), pltpu.VMEM((rows, wide_g), BF),
            pltpu.VMEM((slots, experts, rows), BF), pltpu.VMEM((group, local * cap, rows), BF),
            dma((3,)), dma((3, slots)), dma((2, local)), dma((2,)), dma((1,)),
            dma((layers + 1,)), dma((layers,)), dma((layers, 10)), dma((layers, 10)),
            dma((2, 2)), dma((2, layers, 4)), dma((2, 2)), dma((2, layers, 2)),
            dma((2,)), dma((2, layers)), dma((2,)), dma((2, layers)), dma((2, 2)),
        ],
        compiler_params=pltpu.CompilerParams(
            collective_id=1, has_side_effects=True, vmem_limit_bytes=64 * 2**20
        ),
        cost_estimate=pl.CostEstimate(flops=flops, bytes_accessed=200 * 2**20, transcendentals=0),
    )(x_own, all_g, near_g, wg, wu, wd)
    return result[:5]


def weights_kernel(x, g, acts, grad_g, grad_u, grad_d):
    first = pl.program_id(1) == 0
    xe, ge = x[0], g[0]

    def put(ref, n, size, value, axis):
        at = (0, pl.ds(n, size), slice(None)) if axis == 0 else (0, slice(None), pl.ds(n, size))

        @pl.when(first)
        def _():
            ref[at] = value

        @pl.when(jnp.logical_not(first))
        def _():
            ref[at] += value

    hg, dg, du = acts[0, 0], acts[1, 0], acts[2, 0]
    for n in range(0, xe.shape[1], STEP):
        part = xe[:, n : n + STEP]
        put(grad_g, n, STEP, tdot(part, dg), 0)
        put(grad_u, n, STEP, tdot(part, du), 0)
        put(grad_d, n, STEP, tdot(hg, ge[:, n : n + STEP]), 1)


def run_weights(x_slots, g_slots, acts):
    local, n_dev, cap, width = x_slots.shape
    hid = acts.shape[-1]
    total = n_dev * cap
    tile = min(1024, total)
    x_slots = x_slots.reshape(local, total, width)
    g_slots = g_slots.reshape(local, total, width)
    row = pl.BlockSpec((1, tile, width), lambda e, k: (e, k, 0))
    wide = pl.BlockSpec((1, width, hid), lambda e, k: (e, 0, 0))
    deep = pl.BlockSpec((1, hid, width), lambda e, k: (e, 0, 0))
    return pl.pallas_call(
        weights_kernel,
        grid=(local, total // tile),
        out_shape=(
            jax.ShapeDtypeStruct((local, width, hid), F32),
            jax.ShapeDtypeStruct((local, width, hid), F32),
            jax.ShapeDtypeStruct((local, hid, width), F32),
        ),
        in_specs=[row, row, pl.BlockSpec((3, 1, tile, hid), lambda e, k: (0, e, k, 0))],
        out_specs=(wide, wide, deep),
        compiler_params=pltpu.CompilerParams(vmem_limit_bytes=60 * 2**20),
        cost_estimate=pl.CostEstimate(
            flops=6 * local * total * width * hid, bytes_accessed=130 * 2**20, transcendentals=0
        ),
    )(x_slots, g_slots, acts)


def peer(here, rank):
    return (here.layer * 2 + rank // here.n_dp, rank % here.n_dp)


def others(here, group):
    return [lax.rem(here.rank + k, group) for k in range(1, group)]


def remote(src, dst, send, recv, device):
    return pltpu.make_async_remote_copy(
        src_ref=src, dst_ref=dst, send_sem=send, recv_sem=recv,
        device_id=device, device_id_type=MESH,
    )


class LayerGather:
    def __init__(self, here, own, buf, own_sem, send, recv):
        self.here, self.own, self.buf = here, own, buf
        self.own_sem, self.send, self.recv = own_sem, send, recv

    def copy(self, kind):
        here, buf = self.here, self.buf
        wide = buf.shape[-1]
        half = wide // 256 * 128
        low, high, full = pl.ds(0, half), pl.ds(half, wide - half), pl.ds(0, wide)
        n_dp, x, y, core = here.n_dp, here.x, here.y, here.core
        over_x = y * n_dp + (1 - x) * 2 + core
        over_y = (1 - y) * n_dp + x * 2 + core
        across = (1 - y) * n_dp + (1 - x) * 2 + core
        which, cols, device = {
            0: (here.rank, low, here.over_x),
            1: (here.rank, high, here.over_x),
            2: (here.rank, low, here.over_y),
            3: (here.rank, high, here.over_y),
            4: (over_x, low, here.over_y),
            5: (over_y, high, here.over_x),
            6: (here.rank, full, here.sibling),
            7: (over_x, full, here.sibling),
            8: (over_y, full, here.sibling),
            9: (across, full, here.sibling),
        }[kind]
        dst = buf.at[which, :, cols]
        src = self.own.at[:, cols] if kind in (0, 1, 2, 3, 6) else dst
        return remote(src, dst, self.send.at[kind], self.recv.at[kind], device)

    def keep(self):
        return pltpu.make_async_copy(self.own, self.buf.at[self.here.rank], self.own_sem.at[0])

    def begin(self):
        self.keep().start()
        for kind in (0, 3, 1, 2, 6):
            self.copy(kind).start()

    def forward(self):
        for got, then in ((0, 4), (3, 5), (1, 7), (2, 8)):
            self.copy(got).wait_recv()
            self.copy(then).start()

    def across(self):
        self.copy(4).wait_recv()
        self.copy(5).wait_recv()
        self.copy(9).start()

    def end(self):
        for kind in (6, 7, 8, 9):
            self.copy(kind).wait_recv()
        for kind in range(10):
            self.copy(kind).wait_send()
        self.keep().wait()


class WideGather:
    def __init__(self, here, layers, own, buf, own_sem, z_send, z_recv, send, recv):
        self.here, self.layers, self.own, self.buf = here, layers, own, buf
        self.own_sem, self.z_send, self.z_recv = own_sem, z_send, z_recv
        self.send, self.recv = send, recv
        self.last = layers - 1

    def layer_of(self, i):
        return nearby(self.here.layer, i, self.layers)

    def keep(self):
        return pltpu.make_async_copy(
            self.own, self.buf.at[self.here.layer, self.here.rank], self.own_sem.at[0]
        )

    def over_z(self, block, up, own=False):
        here = self.here
        at = self.buf.at[block, here.rank]
        return remote(
            self.own if own else at, at,
            self.z_send.at[self.layers if own and not up else block], self.z_recv.at[block],
            here.at_layer(here.layer + 1 if up else here.layer - 1),
        )

    def own_z(self, act):
        layer = self.here.layer

        @pl.when(layer + 1 < self.layers)
        def _():
            act(self.over_z(layer, True, True))

        @pl.when(layer >= 1)
        def _():
            act(self.over_z(layer, False, True))

    def passes(self, i):
        layer, block = self.here.layer, self.layer_of(i)
        up = jnp.logical_and(block < layer, layer + 1 < self.layers)
        down = jnp.logical_and(block > layer, layer >= 1)
        return block, up, down

    def pass_on(self, i):
        block, up, down = self.passes(i)

        @pl.when(up)
        def _():
            self.over_z(block, True).wait_recv()
            self.over_z(block, True).start()

        @pl.when(down)
        def _():
            self.over_z(block, False).wait_recv()
            self.over_z(block, False).start()

    def copy(self, i, kind):
        here = self.here
        block = self.buf.at[self.layer_of(i)]
        job = LayerGather(here, block.at[here.rank], block, None, self.send.at[i], self.recv.at[i])
        return job.copy(kind)

    def begin(self):
        self.keep().start()
        self.own_z(lambda copy: copy.start())

    def enter(self, i):
        block, up, down = self.passes(i)

        @pl.when(jnp.logical_not(jnp.logical_or(up, down)))
        def _():
            self.over_z(block, True).wait_recv()

        for kind in (0, 3, 1, 2, 6):
            self.copy(i, kind).start()

    def forward(self, i):
        for got, then in ((0, 4), (3, 5), (1, 7), (2, 8)):
            self.copy(i, got).wait_recv()
            self.copy(i, then).start()

    def across(self, i):
        self.copy(i, 4).wait_recv()
        self.copy(i, 5).wait_recv()
        self.copy(i, 9).start()

    def end(self):
        self.keep().wait()
        for i in range(self.last):
            for kind in (6, 7, 8, 9):
                self.copy(i, kind).wait_recv()
        for i in range(self.last):
            for kind in range(10):
                self.copy(i, kind).wait_send()
        self.own_z(lambda copy: copy.wait_send())
        for i in range(self.last):
            block, up, down = self.passes(i)

            @pl.when(up)
            def _():
                self.over_z(block, True).wait_send()

            @pl.when(down)
            def _():
                self.over_z(block, False).wait_send()


class LayerSum:
    def __init__(self, here, part, acc, sib, one, two, load, send, recv):
        self.here, self.part, self.acc, self.sib = here, part, acc, sib
        self.one, self.two, self.load_sem, self.send, self.recv = one, two, load, send, recv
        wide = acc.shape[-1]
        half = wide // 256 * 128
        self.cols = (pl.ds(0, half), pl.ds(half, wide - half))

    def load(self, q):
        return pltpu.make_async_copy(
            self.part.at[q * 2 + self.here.core], self.acc.at[q], self.load_sem.at[q]
        )

    def copy(self, kind):
        here, acc = self.here, self.acc
        x, y = here.x, here.y
        low, high = self.cols
        if kind < 4:
            src, dst = self.part.at[kind * 2 + 1 - here.core], self.sib.at[kind]
            device = here.sibling
        elif kind < 6:
            j = kind - 4
            src, dst, device = acc.at[j * 2 + 1 - x, :, low], self.one.at[j, :, low], here.over_x
        elif kind < 8:
            j = kind - 6
            src, dst = acc.at[(1 - y) * 2 + j, :, high], self.one.at[j, :, high]
            device = here.over_y
        elif kind == 8:
            src, dst, device = acc.at[(1 - y) * 2 + x, :, low], self.two.at[:, low], here.over_y
        else:
            src, dst, device = acc.at[y * 2 + 1 - x, :, high], self.two.at[:, high], here.over_x
        return remote(src, dst, self.send.at[kind], self.recv.at[kind], device)

    def add(self, q, cols, got):
        total = self.acc[q, :, cols].astype(F32) + got.astype(F32)
        self.acc[q, :, cols] = total.astype(BF)

    def begin(self):
        for q in range(4):
            self.copy(q).start()
            self.load(q).start()

    def first(self):
        for q in range(4):
            self.load(q).wait()
            self.copy(q).wait_recv()
            for cols in self.cols:
                self.add(q, cols, self.sib[q, :, cols])
        for kind in (4, 5, 6, 7):
            self.copy(kind).start()

    def second(self):
        x, y = self.here.x, self.here.y
        low, high = self.cols
        for j in range(2):
            self.copy(4 + j).wait_recv()
            self.add(j * 2 + x, low, self.one[j, :, low])
            self.copy(6 + j).wait_recv()
            self.add(y * 2 + j, high, self.one[j, :, high])
        self.copy(8).start()
        self.copy(9).start()

    def third(self, out):
        own = self.here.y * 2 + self.here.x
        for kind, cols in zip((8, 9), self.cols):
            self.copy(kind).wait_recv()
            out[:, cols] = self.acc[own, :, cols].astype(F32) + self.two[:, cols].astype(F32)
        for kind in range(10):
            self.copy(kind).wait_send()

    @staticmethod
    def scratch(rows, wide):
        return [
            pltpu.VMEM((4, rows, wide), BF), pltpu.VMEM((4, rows, wide), BF),
            pltpu.VMEM((2, rows, wide), BF), pltpu.VMEM((rows, wide), BF),
            pltpu.SemaphoreType.DMA((4,)),
            pltpu.SemaphoreType.DMA((10,)), pltpu.SemaphoreType.DMA((10,)),
        ]


def comm_params(number):
    return pltpu.CompilerParams(
        collective_id=number, has_side_effects=True, vmem_limit_bytes=48 * 2**20
    )


def front_kernel(
    n_dp, layers, x_own, w_q, w_k, w_v, w_o, small, g_own,
    x_all, qkv, wo, small_all, g_near, wo_col,
    own_sem, x_send, x_recv, a_keep, a_send, a_recv, up_send, up_recv, down_send, down_recv,
    o_keep, o_send, o_recv, s_send, s_recv, t_send, t_recv, g_keep, g_send, g_recv,
):
    here = Place(n_dp)
    group = 2 * n_dp
    layer, rank = here.layer, here.rank
    own = w_q.shape[0]
    cols = qkv.shape[-1]
    ranks = others(here, group)
    away = [flip(layer, i, layers) for i in range(1, layers)]
    greet([peer(here, r) for r in ranks] + [here.at_layer(z) for z in away])
    gather = LayerGather(here, x_own, x_all, own_sem, x_send, x_recv)
    cotangent = LayerGather(here, g_own, g_near, g_keep, g_send, g_recv)
    weights = (w_q, w_k, w_v)

    def rows_at(index):
        return pl.ds(pl.multiple_of(index * own, own), own)

    def block_cols(index):
        return pl.ds(pl.multiple_of(index * cols, cols), cols)

    def swap(w, k):
        return remote(
            weights[w].at[:, block_cols(ranks[k])], qkv.at[w, layer, rows_at(rank)],
            a_send.at[w, k], a_recv.at[w, k], peer(here, ranks[k]),
        )

    def swap_own(w):
        return pltpu.make_async_copy(
            weights[w].at[:, block_cols(rank)], qkv.at[w, layer, rows_at(rank)], a_keep.at[w]
        )

    def small_out(i):
        ref = small_all.at[layer, rank]
        return remote(small, ref, s_send.at[i], s_recv.at[i], here.at_layer(away[i]))

    def small_keep():
        return pltpu.make_async_copy(small, small_all.at[layer, rank], a_keep.at[3])

    def small_share(k):
        ref = small_all.at[:, rank]
        return remote(ref, ref, t_send.at[k], t_recv.at[k], peer(here, ranks[k]))

    def o_own():
        return pltpu.make_async_copy(w_o, wo_col.at[layer], a_keep.at[4])

    for w in range(3):
        swap_own(w).start()
        for k in range(group - 1):
            swap(w, k).start()
    o_own().start()
    small_keep().start()
    for i in range(layers - 1):
        small_out(i).start()
    gather.begin()
    for w in range(3):
        swap_own(w).wait()
        for k in range(group - 1):
            swap(w, k).wait_recv()
    o_own().wait()

    def chain(which, up, s):
        block = layer - s if up else layer + s
        ref = qkv.at[:, block] if which == 0 else wo_col.at[block]
        device = here.at_layer(layer + 1 if up else layer - 1)
        sems = (up_send, up_recv) if up else (down_send, down_recv)
        return remote(ref, ref, sems[0].at[which, s], sems[1].at[which, s], device)

    def step(which, s, wait):
        for up in (True, False):
            leaves = (
                jnp.logical_and(layer + 1 < layers, layer - s >= 0) if up
                else jnp.logical_and(layer >= 1, layer + s < layers)
            )
            comes = layer - 1 - s >= 0 if up else layer + 1 + s < layers
            if wait:
                @pl.when(comes)
                def _():
                    chain(which, up, s).wait_recv()
            else:
                @pl.when(leaves)
                def _():
                    chain(which, up, s).start()

    step(0, 0, False)
    gather.forward()
    step(1, 0, False)
    gather.across()
    small_keep().wait()
    for i in range(layers - 1):
        small_out(i).wait_recv()
    for k in range(group - 1):
        small_share(k).start()
    cotangent.begin()
    for s in range(layers - 1):
        step(0, s, True)
        if s + 1 < layers - 1:
            step(0, s + 1, False)
        if s == 0:
            cotangent.forward()
        step(1, s, True)
        if s + 1 < layers - 1:
            step(1, s + 1, False)
        if s == 0:
            cotangent.across()

    def share(z):
        number = z * group + rank
        target, index = number // layers, number % layers

        def far():
            return remote(
                wo_col.at[z], wo.at[index], o_send.at[z], o_recv.at[index], peer(here, target)
            )

        def near():
            return pltpu.make_async_copy(wo_col.at[z], wo.at[index], o_keep.at[index])

        return target, far, near

    def source(index):
        number = rank * layers + index
        return number % group

    for z in range(layers):
        target, far, near = share(z)

        @pl.when(target != rank)
        def _():
            far().start()

        @pl.when(target == rank)
        def _():
            near().start()

    for index in range(layers):
        @pl.when(source(index) != rank)
        def _():
            remote(
                wo_col.at[0], wo.at[index], o_send.at[0], o_recv.at[index], here.sibling
            ).wait_recv()

        @pl.when(source(index) == rank)
        def _():
            pltpu.make_async_copy(wo_col.at[0], wo.at[index], o_keep.at[index]).wait()

    gather.end()
    cotangent.end()
    for k in range(group - 1):
        small_share(k).wait_recv()
    for w in range(3):
        for k in range(group - 1):
            swap(w, k).wait_send()
    for i in range(layers - 1):
        small_out(i).wait_send()
    for k in range(group - 1):
        small_share(k).wait_send()
    for z in range(layers):
        target, far, near = share(z)

        @pl.when(target != rank)
        def _():
            far().wait_send()

    for which in range(2):
        for s in range(layers - 1):
            @pl.when(jnp.logical_and(layer + 1 < layers, layer - s >= 0))
            def _():
                chain(which, True, s).wait_send()

            @pl.when(jnp.logical_and(layer >= 1, layer + s < layers))
            def _():
                chain(which, False, s).wait_send()


def run_front(x_own, w_q, w_k, w_v, w_o, small, g_own, n_dp, n_dev):
    rows, width = x_own.shape
    own = w_q.shape[0]
    group = 2 * n_dp
    layers = n_dev // group
    cols = width // group
    dma = pltpu.SemaphoreType.DMA
    shape = jax.ShapeDtypeStruct
    chain = dma((2, layers))
    result = pl.pallas_call(
        functools.partial(front_kernel, n_dp, layers),
        out_shape=(
            shape((group, rows, width), BF),
            shape((3, layers, group * own, cols), BF),
            shape((layers, own, width), BF),
            shape((layers, group) + small.shape, BF),
            shape((group, rows, width), BF),
            shape((layers, own, width), BF),
        ),
        in_specs=[ANY] * 7,
        out_specs=(ANY,) * 6,
        scratch_shapes=[
            dma((1,)), dma((10,)), dma((10,)), dma((5,)),
            dma((3, group - 1)), dma((3, group - 1)), chain, chain, chain, chain,
            dma((layers,)), dma((layers,)), dma((layers,)),
            dma((layers,)), dma((layers,)), dma((group,)), dma((group,)),
            dma((1,)), dma((10,)), dma((10,)),
        ],
        compiler_params=pltpu.CompilerParams(
            collective_id=5, has_side_effects=True, vmem_limit_bytes=64 * 2**20
        ),
    )(x_own, w_q, w_k, w_v, w_o, small, g_own)
    x_all, qkv, wo, small_all, g_near, _ = result
    return (
        x_all.reshape(group * rows, width), qkv.reshape(3, width, cols),
        wo.reshape(cols, width), small_all.reshape(width, -1), g_near,
    )


class LayerTerms:
    def __init__(self, here, ranks, pick, land, send, recv):
        self.here, self.ranks, self.pick = here, ranks, pick
        self.land, self.send, self.recv = land, send, recv

    def copy(self, k):
        return remote(
            self.pick(self.ranks[k]), self.land.at[k], self.send.at[k], self.recv.at[k],
            peer(self.here, self.ranks[k]),
        )

    def begin(self):
        for k in range(len(self.ranks)):
            self.copy(k).start()

    def total(self, own):
        for k in range(len(self.ranks)):
            self.copy(k).wait_recv()
            own = own + self.land[k].astype(F32)
        return own

    def end(self):
        for k in range(len(self.ranks)):
            self.copy(k).wait_send()


class ColumnTerms:
    def __init__(self, here, layers, pick, land, send, recv):
        self.here, self.pick = here, pick
        self.away = [flip(here.layer, i, layers) for i in range(1, layers)]
        self.land, self.send, self.recv = land, send, recv

    def copy(self, i):
        return remote(
            self.pick(self.away[i]), self.land.at[i], self.send.at[i], self.recv.at[i],
            self.here.at_layer(self.away[i]),
        )

    def begin(self):
        for i in range(len(self.away)):
            self.copy(i).start()

    def total(self, own):
        for i in range(len(self.away)):
            self.copy(i).wait_recv()
            own = own + self.land[i].astype(F32)
        return own

    def end(self):
        for i in range(len(self.away)):
            self.copy(i).wait_send()


def as_row(column):
    return jnp.broadcast_to(column, (column.shape[0], 128)).T[:1]


def as_column(row):
    return jnp.broadcast_to(row, (128, row.shape[1])).T[:, :1]


def row_sum(value):
    return jnp.sum(value, axis=1, keepdims=True)


def swap_halves(value):
    half = value.shape[1] // 2
    return jnp.concatenate([value[:, half:], value[:, :half]], axis=1)


def probabilities(q_rot, k_rot, scale):
    scores = dot_t(q_rot, k_rot) * scale
    later = (
        lax.broadcasted_iota(jnp.int32, scores.shape, 0)
        >= lax.broadcasted_iota(jnp.int32, scores.shape, 1)
    )
    scores = jnp.where(later, scores, -1e30)
    grown = jnp.exp(scores - jnp.max(scores, axis=1, keepdims=True))
    return grown / row_sum(grown)


def attend_kernel(
    n_dp, layers, seqs,
    x, small, w, cosine, sine, wo, hits, g_own,
    normed, q_raw, k_raw, v, q_rot, k_rot, mixed, stats,
    residual, res_unit, res_root, gates, x_out, gain_rows, head_gains, g_all,
    part, squares, land, n_send, n_recv, out, p_send, p_recv,
    acc, sib, one, two, load_sem, l_send, l_recv, g_keep, gz_send, gz_recv, g_send, g_recv,
):
    here = Place(n_dp)
    group = 2 * n_dp
    ranks = others(here, group)
    greet(
        [peer(here, r) for r in ranks]
        + [here.at_layer(flip(here.layer, i, layers)) for i in range(1, layers)]
    )
    terms = LayerTerms(here, ranks, lambda r: squares, land, n_send, n_recv)
    rest = WideGather(here, layers, g_own, g_all, g_keep, gz_send, gz_recv, g_send, g_recv)
    job = LayerSum(here, part, acc, sib, one, two, load_sem, l_send, l_recv)
    last = layers - 1
    total, width = normed.shape
    rows_own = g_own.shape[0]
    cols = q_raw.shape[1]
    def seats(k):
        ref = g_all.at[here.layer, here.rank, :, pl.ds(width, g_own.shape[1] - width)]
        src = g_own.at[:, pl.ds(width, g_own.shape[1] - width)]
        return remote(src, ref, p_send.at[k], p_recv.at[k], peer(here, ranks[k]))

    rest.begin()
    for k in range(group - 1):
        seats(k).start()

    experts = small.shape[1] // 2
    for n in range(0, width, 128):
        turned = small[n : n + 128, :].astype(F32).T
        gain_rows[:, n : n + 128] = turned[experts : experts + 8]
    head_cols = pl.ds(pl.multiple_of(here.rank * cols, cols), cols)
    head_gains[...] = gain_rows[:, head_cols]
    gain, ffn_gain = gain_rows[0:1, :], gain_rows[3:4, :]

    tile = 256
    squares[...] = jnp.zeros_like(squares)

    def project(t):
        at = slice(t * tile, (t + 1) * tile)
        value = x[at, :].astype(F32)
        root = lax.rsqrt(row_sum(value * value) / width + EPSILON)
        low = (value * root * gain).astype(BF)
        normed[at, :] = low
        q, k = dot(low, w[0]), dot(low, w[1])
        q_raw[at, :] = q
        k_raw[at, :] = k
        v[at, :] = dot(low, w[2]).astype(BF)
        squares[0:1, at] = as_row(row_sum(q * q))
        squares[1:2, at] = as_row(row_sum(k * k))

    for t in range(total // tile):
        project(t)
    terms.begin()
    rest.pass_on(0)
    rest.enter(0)
    stats[...] = terms.total(squares[...])

    length = total // seqs
    for s in range(seqs):
        rows = slice(s * length, (s + 1) * length)
        roots = [
            as_column(lax.rsqrt(stats[i : i + 1, rows] / width + EPSILON)) for i in range(2)
        ]
        for h in range(0, cols, HEAD_DIM):
            head = slice(h, h + HEAD_DIM)
            turned = []
            for raw, root, scale, to in (
                (q_raw, roots[0], head_gains[1:2, head], q_rot),
                (k_raw, roots[1], head_gains[2:3, head], k_rot),
            ):
                value = raw[rows, head] * root * scale
                value = (value * cosine[...] + swap_halves(value) * sine[...]).astype(BF)
                to[rows, head] = value
                turned.append(value)
            probs = probabilities(turned[0], turned[1], HEAD_DIM ** (-0.5)).astype(BF)
            mixed[rows, head] = dot(probs, v[rows, head]).astype(BF)
        if s == 0:
            rest.pass_on(1)
    size = part.shape[1]
    rest.forward(0)
    rest.enter(1)

    def project_out(b, c):
        value = mixed[pl.ds(pl.multiple_of(b * size, size), size), :]
        for n in range(0, width, STEP):
            part[b, :, n : n + STEP] = dot(value, wo[:, n : n + STEP]).astype(BF)
        return c

    lax.fori_loop(0, group, project_out, 0)

    job.begin()
    rest.across(0)
    for i in range(2, last):
        rest.pass_on(i)
    job.first()
    rest.forward(1)
    job.second()
    if last > 2:
        rest.enter(2)
    rest.across(1)
    job.third(out)

    at = pl.ds(pl.multiple_of(here.rank * rows_own, rows_own), rows_own)
    value = x[at, :].astype(F32) + out[...]
    residual[...] = value
    root = lax.rsqrt(row_sum(value * value) / width + EPSILON)
    unit = value * root
    res_unit[...] = unit
    res_root[...] = jnp.broadcast_to(root, res_root.shape)
    low = (unit * ffn_gain).astype(BF)
    x_out[:, :width] = low
    logits = dot(low, small[...])
    chosen = hits[...] > 0.0
    top_logit = jnp.max(jnp.where(chosen, logits, -1e30), axis=1, keepdims=True)
    grown = jnp.where(chosen, jnp.exp(jnp.minimum(logits - top_logit, 0.0)), 0.0)
    shares = grown / row_sum(grown)
    gates[...] = shares
    high = shares.astype(BF).astype(F32)
    x_out[:, width:] = (high + swap_halves(shares - high)).astype(BF)
    for i in range(2, last):
        rest.forward(i)
        if i + 1 < last:
            rest.enter(i + 1)
        rest.across(i)
    rest.end()
    terms.end()
    for k in range(group - 1):
        seats(k).wait()


def run_attend(seqs, n_dp, layers, x, small, w, *rest):
    g_own = rest[-1]
    total, width = x.shape
    cols = w.shape[-1]
    group = 2 * n_dp
    rows = total // group
    shape = jax.ShapeDtypeStruct
    dma = pltpu.SemaphoreType.DMA
    narrow, narrow_f = shape((total, cols), BF), shape((total, cols), F32)
    result = pl.pallas_call(
        functools.partial(attend_kernel, n_dp, layers, seqs),
        out_shape=(
            shape((total, width), BF), narrow_f, narrow_f, narrow, narrow, narrow, narrow,
            shape((8, total), F32), shape((rows, width), F32), shape((rows, width), F32),
            shape((rows, 128), F32), shape((rows, 128), F32), shape((rows, width + 128), BF),
            shape((8, width), F32), shape((8, cols), F32),
            shape((layers, group) + g_own.shape, BF),
        ),
        in_specs=[VMEM] * 7 + [ANY],
        out_specs=(VMEM,) * 15 + (ANY,),
        scratch_shapes=[
            pltpu.VMEM((group, rows, width), BF), pltpu.VMEM((8, total), F32),
            pltpu.VMEM((group - 1, 8, total), F32), dma((group - 1,)), dma((group - 1,)),
            pltpu.VMEM((rows, width), F32), dma((group - 1,)), dma((group - 1,)),
        ] + LayerSum.scratch(rows, width) + [
            dma((1,)), dma((layers + 1,)), dma((layers,)), dma((layers, 10)), dma((layers, 10)),
        ],
        compiler_params=pltpu.CompilerParams(
            collective_id=2, has_side_effects=True, vmem_limit_bytes=56 * 2**20
        ),
    )(x, small, w, *rest)
    return result


def back_kernel(
    n_dp, layers, seqs,
    gao, wo, mixed, q_rot, k_rot, v, normed, q_raw, k_raw, stats, head_gains, cosine, sine,
    w, x, early,
    out, grad_w, grad_o, small_out,
    grad_mixed, gq, gk, low, inner, gains, rowmat, small, part,
    acc, sib, one, two, load_sem, n_send, n_recv,
    go, acc_w, acc_o, up_w, up_o, up_v, down_w, down_o, down_v, swapped, land, s_land, s_sum, s_far,
    i_send, i_recv, o_keep, o_send, o_recv, up_send, up_recv, down_send, down_recv,
    a_keep, a_send, a_recv, s_send, s_recv, t_send, t_recv,
):
    here = Place(n_dp)
    group = 2 * n_dp
    layer, rank = here.layer, here.rank
    total, cols = q_raw.shape
    width = wo.shape[1]
    own = grad_w.shape[1]
    size = group * own
    length = total // seqs
    scale = HEAD_DIM ** (-0.5)
    last = layers - 1
    ranks = others(here, group)
    greet(
        [peer(here, r) for r in ranks]
        + [here.at_layer(flip(layer, i, layers)) for i in range(1, layers)]
    )
    job = LayerSum(here, part, acc, sib, one, two, load_sem, n_send, n_recv)
    terms = LayerTerms(here, ranks, lambda r: inner, land, i_send, i_recv)
    small_terms = LayerTerms(here, ranks, lambda r: small.at[:, r], s_land, s_send, s_recv)
    far_terms = ColumnTerms(here, layers, lambda z: s_sum.at[z], s_far, t_send, t_recv)

    def share(i):
        number = rank * layers + i
        z, target = number // group, number % group

        def far():
            return remote(
                go.at[i], acc_o.at[z], o_send.at[i], o_recv.at[z], peer(here, target)
            )

        def near():
            return pltpu.make_async_copy(go.at[i], acc_o.at[z], o_keep.at[z])

        return target, far, near

    def shared(z):
        source = (z * group + rank) // layers

        @pl.when(source != rank)
        def _():
            remote(
                go.at[0], acc_o.at[z], o_send.at[0], o_recv.at[z], here.sibling
            ).wait_recv()

        @pl.when(source == rank)
        def _():
            pltpu.make_async_copy(go.at[0], acc_o.at[z], o_keep.at[z]).wait()

    def rows_of(z):
        return pl.ds(pl.multiple_of(z * size, size), size)

    def chain(which, up, z):
        src = (acc_w.at[0:2, rows_of(z)], acc_o.at[z], acc_w.at[2, rows_of(z)])[which]
        to = ((up_w, up_o, up_v) if up else (down_w, down_o, down_v))[which].at[z]
        sems = (up_send, up_recv) if up else (down_send, down_recv)
        device = here.at_layer(layer + 1 if up else layer - 1)
        return remote(src, to, sems[0].at[which, z], sems[1].at[which, z], device)

    def take(which, up, z):
        chain(which, up, z).wait_recv()
        if which == 0:
            got = up_w if up else down_w
            for i in range(2):
                value = acc_w[i, rows_of(z)].astype(F32) + got[z, i].astype(F32)
                acc_w[i, rows_of(z)] = value.astype(BF)
        elif which == 1:
            got = up_o if up else down_o
            acc_o[z] = (acc_o[z].astype(F32) + got[z].astype(F32)).astype(BF)
        else:
            got = up_v if up else down_v
            value = acc_w[2, rows_of(z)].astype(F32) + got[z].astype(F32)
            acc_w[2, rows_of(z)] = value.astype(BF)

    def launch(which):
        for d in range(last, 0, -1):
            @pl.when(layer == 0)
            def _():
                chain(which, True, layer + d).start()

            @pl.when(layer == last)
            def _():
                chain(which, False, layer - d).start()

    def relay(which, d):
        @pl.when(jnp.logical_and(layer > 0, layer + d < layers))
        def _():
            take(which, True, layer + d)
            chain(which, True, layer + d).start()

        @pl.when(jnp.logical_and(layer < last, layer - d >= 0))
        def _():
            take(which, False, layer - d)
            chain(which, False, layer - d).start()

    def relay_all(which):
        for d in range(last - 1, 0, -1):
            relay(which, d)

    def settle(which):
        @pl.when(layer > 0)
        def _():
            take(which, True, layer)

        @pl.when(layer < last)
        def _():
            take(which, False, layer)

    for n in range(0, width, STEP):
        got = tdot(mixed[...], gao[:, n : n + STEP]).astype(BF)
        go[:, :, n : n + STEP] = got.reshape(layers, own, STEP)
    for i in range(layers):
        target, far, near = share(i)

        @pl.when(target != rank)
        def _():
            far().start()

        @pl.when(target == rank)
        def _():
            near().start()
    grad_mixed[...] = dot_t(gao[...], wo[...]).astype(BF)
    inner[...] = jnp.zeros_like(inner)
    gains[...] = jnp.zeros_like(gains)

    for s in range(seqs):
        rows = slice(s * length, (s + 1) * length)
        roots = [
            as_column(lax.rsqrt(stats[i : i + 1, rows] / width + EPSILON)) for i in range(2)
        ]
        inners = [jnp.zeros((length, 1), F32) for _ in range(2)]
        for h in range(0, cols, HEAD_DIM):
            head = slice(h, h + HEAD_DIM)
            q, k = q_rot[rows, head], k_rot[rows, head]
            probs = probabilities(q, k, scale)
            gm = grad_mixed[rows, head]
            low[2, rows, head] = tdot(probs.astype(BF), gm).astype(BF)
            grad_probs = dot_t(gm, v[rows, head])
            delta = row_sum(probs * grad_probs)
            grad_scores = (probs * (grad_probs - delta)).astype(BF)
            for i, (turned, raw, gain, to) in enumerate((
                (dot(grad_scores, k) * scale, q_raw, head_gains[1:2, head], gq),
                (tdot(grad_scores, q) * scale, k_raw, head_gains[2:3, head], gk),
            )):
                back = turned * cosine[...] - swap_halves(turned) * sine[...]
                unit = raw[rows, head] * roots[i]
                gains[i : i + 1, head] += jnp.sum(back * unit, axis=0, keepdims=True)
                back = back * gain
                to[rows, head] = back
                inners[i] = inners[i] + row_sum(back * unit)
        for i in range(2):
            inner[i : i + 1, rows] = as_row(inners[i])
        if s == 0:
            for z in range(layers):
                shared(z)
            launch(1)
    terms.begin()

    def weight_grads(i):
        for n in range(0, width, STEP):
            acc_w[i, n : n + STEP, :] = tdot(normed[:, n : n + STEP], low[i]).astype(BF)

    weight_grads(2)
    launch(2)
    relay_all(1)
    means = terms.total(inner[...]) / width
    for i, (grad, raw) in enumerate(((gq, q_raw), (gk, k_raw))):
        root = as_column(lax.rsqrt(stats[i : i + 1, :] / width + EPSILON))
        mean = as_column(means[i : i + 1, :])
        low[i] = (root * (grad[...] - raw[...] * root * mean)).astype(BF)
        weight_grads(i)
    launch(0)
    rowmat[...] = early[...]

    def project(b, c):
        at = pl.ds(pl.multiple_of(b * part.shape[1], part.shape[1]), part.shape[1])
        value = x[at, :].astype(F32)
        root = lax.rsqrt(row_sum(value * value) / width + EPSILON)
        for n in range(0, width, STEP):
            cut = slice(n, n + STEP)
            got = dot_t(low[0, at, :], w[0, cut, :]) + dot_t(low[1, at, :], w[1, cut, :])
            got = got + dot_t(low[2, at, :], w[2, cut, :])
            part[b, :, cut] = got.astype(BF)
            unit = x[at, cut].astype(F32) * root
            rowmat[64:65, cut] += jnp.sum(got * unit, axis=0, keepdims=True)
        return c

    lax.fori_loop(0, group, project, 0)
    job.begin()
    head_cols = pl.ds(pl.multiple_of(rank * cols, cols), cols)
    rowmat[65:66, head_cols] = gains[0:1, :]
    rowmat[66:67, head_cols] = gains[1:2, :]
    for n in range(0, width, 128):
        turned = rowmat[:, n : n + 128].T
        for i in range(128 // own):
            number = n // own + i
            small[number // group, number % group] = turned[i * own : (i + 1) * own]
    relay_all(2)
    job.first()
    small_terms.begin()
    for d in range(last - 1, 0, -1):
        relay(0, d)
        if d == last - 1:
            job.second()
    if last < 2:
        job.second()
    s_sum[...] = small_terms.total(small[:, rank])
    far_terms.begin()
    job.third(out)
    settle(1)
    settle(2)
    grad_o[...] = acc_o[layer].astype(F32)
    small_out[...] = far_terms.total(s_sum[layer])
    settle(0)

    def block(index):
        return acc_w.at[:, pl.ds(pl.multiple_of(layer * size + index * own, own), own)]

    def swap(k):
        return remote(
            block(ranks[k]), swapped.at[rank], a_send.at[k], a_recv.at[k], peer(here, ranks[k])
        )

    def swap_own():
        return pltpu.make_async_copy(block(rank), swapped.at[rank], a_keep.at[0])

    swap_own().start()
    for k in range(group - 1):
        swap(k).start()
    swap_own().wait()
    for k in range(group - 1):
        swap(k).wait_recv()
    for r in range(group):
        for i in range(3):
            grad_w[i, :, r * cols : (r + 1) * cols] = swapped[r, i].astype(F32)

    terms.end()
    small_terms.end()
    far_terms.end()
    for k in range(group - 1):
        swap(k).wait_send()
    for i in range(layers):
        target, far, near = share(i)

        @pl.when(target != rank)
        def _():
            far().wait_send()
    for which in range(3):
        for d in range(1, layers):
            @pl.when(layer + d < layers)
            def _():
                chain(which, True, layer + d).wait_send()

            @pl.when(layer - d >= 0)
            def _():
                chain(which, False, layer - d).wait_send()


def run_back(seqs, n_dp, layers, gao, wo, mixed, q_rot, k_rot, v, normed, q_raw, k_raw, *rest):
    total, cols = q_raw.shape
    width = wo.shape[1]
    group = 2 * n_dp
    rows = total // group
    own = width // (layers * group)
    size = group * own
    dma = pltpu.SemaphoreType.DMA
    shape = jax.ShapeDtypeStruct
    many, few = dma((3, layers)), dma((layers,))
    near = dma((group - 1,))
    tiny = (layers, own, 128)
    return pl.pallas_call(
        functools.partial(back_kernel, n_dp, layers, seqs),
        out_shape=(
            shape((rows, width), F32), shape((3, own, width), F32),
            shape((own, width), F32), shape((own, 128), F32),
        ),
        in_specs=[VMEM] * 16,
        out_specs=(VMEM,) * 4,
        scratch_shapes=[
            pltpu.VMEM((total, cols), BF), pltpu.VMEM((total, cols), F32),
            pltpu.VMEM((total, cols), F32), pltpu.VMEM((3, total, cols), BF),
            pltpu.VMEM((8, total), F32), pltpu.VMEM((8, cols), F32),
            pltpu.VMEM((128, width), F32), pltpu.VMEM((layers, group, own, 128), F32),
            pltpu.VMEM((group, rows, width), BF),
        ] + LayerSum.scratch(rows, width) + [
            pltpu.VMEM((layers, own, width), BF), pltpu.VMEM((3, width, cols), BF),
            pltpu.VMEM((layers, own, width), BF),
        ] + [
            pltpu.VMEM((layers, 2, size, cols), BF), pltpu.VMEM((layers, own, width), BF),
            pltpu.VMEM((layers, size, cols), BF),
        ] * 2 + [
            pltpu.VMEM((group, 3, own, cols), BF), pltpu.VMEM((group - 1, 8, total), F32),
            pltpu.VMEM((group - 1,) + tiny, F32), pltpu.VMEM(tiny, F32), pltpu.VMEM(tiny, F32),
            near, near, few, few, few, many, many, many, many,
            dma((1,)), near, near, near, near, few, few,
        ],
        compiler_params=pltpu.CompilerParams(
            collective_id=6, has_side_effects=True, vmem_limit_bytes=63 * 2**20
        ),
    )(gao, wo, mixed, q_rot, k_rot, v, normed, q_raw, k_raw, *rest)


def ein(spec, left, right):
    return jnp.einsum(spec, left, right, preferred_element_type=F32)


def inv_rms(value):
    return lax.rsqrt(jnp.mean(value * value, axis=-1, keepdims=True) + EPSILON)


def build(n_ep, n_dp):
    n_dev = n_ep * n_dp
    group = 2 * n_dp
    layers = n_dev // group
    rows_of = [[z * group + r for r in range(group)] for z in range(layers)]

    def shards(
        layer_input, grad_out, attn_gain, w_q, w_k, w_v, q_gain, k_gain, w_o, ffn_gain,
        router, w_gate, w_up, w_down, routes,
    ):
        rows, width = layer_input.shape
        cols = width // group
        seqs = 2
        seq_len = rows * n_dp
        own = width // n_dev
        rank = (lax.axis_index("ep") % 2) * n_dp + lax.axis_index("dp")
        experts = router.shape[1]
        top = routes.shape[1]
        cap = 2 * rows * top // experts

        gains = jnp.stack([attn_gain, q_gain, k_gain, ffn_gain]).T
        small = jnp.concatenate(
            [router, gains, jnp.zeros((own, 128 - experts - 4), BF)], axis=1
        )
        group_input, qkv, wo, small, near_g = run_front(
            layer_input, w_q, w_k, w_v, w_o, small, grad_out, n_dp, n_dev
        )
        full_router = small[:, :experts]

        picked = routes[:, :, None] == jnp.arange(experts, dtype=jnp.int32)
        hits = jnp.any(picked, axis=1)
        before = jnp.cumsum(hits.astype(jnp.int32), axis=0) - hits.astype(jnp.int32)
        place = jnp.where(hits, before, -1).astype(BF)
        place = jnp.pad(place.T, ((0, rows - experts), (0, 0)))
        sent = jnp.concatenate([grad_out, place], axis=1)
        hits_wide = jnp.pad(hits.astype(F32), ((0, 0), (0, 128 - experts)))
        half_dim = HEAD_DIM // 2
        frequency = 10000.0 ** (-np.arange(half_dim, dtype=np.float32) * 2.0 / HEAD_DIM)
        angle = np.arange(seq_len, dtype=np.float32)[:, None] * frequency[None, :]
        angle = angle.astype(np.float32)
        cosine = jnp.asarray(np.concatenate([np.cos(angle)] * 2, axis=-1), F32)
        sine = jnp.asarray(np.concatenate([-np.sin(angle), np.sin(angle)], axis=-1), F32)
        (
            normed, q_raw, k_raw, v_low, q_rot, k_rot, mixed, stats,
            residual, res_n, res_root, gates, x_own, gain_rows, head_gains, all_g,
        ) = run_attend(
            seqs, n_dp, layers, group_input, small, qkv, cosine, sine, wo, hits_wide, sent
        )
        full_attn_gain, full_ffn_gain = gain_rows[0], gain_rows[3]
        all_g = all_g.reshape((n_dev,) + sent.shape)
        res_root, gates_dense, normed2 = res_root[:, :1], gates[:, :experts], x_own[:, :width]

        expert_sum, grad_sum, x_slots, g_slots, acts = run_experts(
            x_own, all_g, near_g, w_gate, w_up, w_down, n_dp, experts, cap
        )
        grad_w_gate, grad_w_up, grad_w_down = run_weights(x_slots, g_slots, acts)
        output = (residual + expert_sum).astype(BF)
        gate_grads = jnp.where(hits, grad_sum[:, width : width + experts], 0.0)
        weighted = jnp.sum(gates_dense * gate_grads, axis=-1, keepdims=True)
        grad_logits = (gates_dense * (gate_grads - weighted)).astype(BF)

        grad_n2 = grad_sum[:, :width] + ein("te,de->td", grad_logits, full_router)
        grad_y = grad_out.astype(F32)
        grad_ffn_gain = jnp.sum(grad_n2 * res_n, axis=0)
        dn = grad_n2 * full_ffn_gain
        grad_residual = grad_y + res_root * (dn - res_n * jnp.mean(dn * res_n, -1, keepdims=True))

        gao = lax.all_gather(
            grad_residual.astype(BF), AXES, axis=0, tiled=True, axis_index_groups=rows_of
        )
        early = jnp.concatenate(
            [
                ein("te,td->ed", grad_logits, normed2), jnp.zeros((3, width), F32),
                grad_ffn_gain[None], jnp.zeros((128 - experts - 4, width), F32),
            ]
        )
        grad_normed, grad_qkv, grad_o, small_grads = run_back(
            seqs, n_dp, layers, gao, wo, mixed, q_rot, k_rot, v_low, normed, q_raw, k_raw, stats,
            head_gains, cosine, sine, qkv, group_input, early,
        )
        own_input = layer_input.astype(F32)
        in_root = inv_rms(own_input)
        in_n = own_input * in_root
        dn = grad_normed * full_attn_gain
        grad_input = grad_residual + in_root * (
            dn - in_n * jnp.mean(dn * in_n, -1, keepdims=True)
        )
        gain_grads = small_grads[:, experts : experts + 4]
        return (
            output, grad_input, gain_grads[:, 0], grad_qkv[0], grad_qkv[1], grad_qkv[2],
            gain_grads[:, 1], gain_grads[:, 2], grad_o, gain_grads[:, 3],
            small_grads[:, :experts], grad_w_gate, grad_w_up, grad_w_down,
        )

    return shards


def solution(mesh):
    row, vec = P(("ep", "dp"), None), P(("ep", "dp"))
    wide, deep = P("ep", None, "dp"), P("ep", "dp", None)
    in_specs = (
        row, row, vec, row, row, row, vec, vec, row, vec, row, wide, wide, deep, row,
    )
    out_specs = (
        row, row, vec, row, row, row, vec, vec, row, vec, row, wide, wide, deep,
    )
    shards = build(mesh.shape["ep"], mesh.shape["dp"])
    return jax.shard_map(shards, mesh=mesh, in_specs=in_specs, out_specs=out_specs, check_vma=False)
```
